32 devices in a mesh: section: 4 (over y, core), dp: 8 (over z, x).
Axes of the slice: x: 2, y: 2, z: 4, core: 2. Of those that a mesh axis runs over, the one named last changes fastest.
Arguments:
- embeds: bfloat16 [64, 197, 768], P('dp'), may hold values from -6 to 6
- mask: int32 [64, 197], P('dp'), may hold values from 0 to 1, as said below
- cotangent: bfloat16 [64, 197, 768], P('dp'), may hold values from -6 to 6
- section_weight: bfloat16 [4, 768, 3072], P('section')
- down_weight: bfloat16 [4, 3072, 768], P('section'), may hold values from -0.109375 to 0.109375
- section_vectors: float32 [4, 8, 768], P('section')
- rel_table: float32 [4, 12, 732], P('section'), may hold values from -4 to 4
Outputs:
- activations: bfloat16 [4, 64, 197, 768], P('section', 'dp')
- input_grads: float32 [4, 64, 197, 768], P('section', 'dp')
- grad_weight: float32 [4, 768, 3072], P('section')
- grad_down: float32 [4, 3072, 768], P('section')
- grad_vectors: float32 [4, 8, 768], P('section')
- grad_table: float32 [4, 12, 732], P('section')
The draws below stay inside these ranges and needn't reach their ends.
Inputs may be any that keep to these rules, and one draw needn't show every extreme that they name: `mask`: column 0 (class row) is 0. Each image masks between 40 and 110 of its patches as one compact block around a centre; some image masks exactly 110 and another exactly 40.
All inputs are finite; a program needn't handle non-finite values.
Results may differ from the reference program's by a relative error of at most 0.015.
Values may be sent and summed in bfloat16 or wider, within the bound.
No kernel may reach another device: no remote copies, remote signals or barrier semaphores. Data moves between devices by JAX's collectives and lax.ppermute only.
A program may use at most 192 MiB of HBM per device.

```python
import math
import jax
import jax.numpy as jnp
from jax import lax

D = 768
H = 12
HD = 64
FF = 3072
GRID = 14
MASK_LO = 40
MASK_HI = 110
L = 197
RELS = 732
SECTIONS = 4
IMAGES = 64


def draw_mask(key, part):
    key = jax.random.fold_in(key, 13)
    streams = jax.random.split(key, 6)
    patches = GRID * GRID
    extent = MASK_HI - MASK_LO
    levels = jax.random.randint(streams[0], (IMAGES,), 0, extent + 1)
    counts = MASK_LO + levels * levels * levels // (extent * extent)
    numbers = jnp.arange(IMAGES, dtype=jnp.int32)
    top_pick = jax.random.randint(streams[1], (), 0, IMAGES)
    bottom_pick = (top_pick + jax.random.randint(streams[2], (), 1, IMAGES)) % IMAGES
    counts = jnp.where(numbers == top_pick, MASK_HI, jnp.where(numbers == bottom_pick, MASK_LO, counts))
    centre_row = jax.random.randint(streams[3], (IMAGES, 1), 0, GRID)
    centre_col = jax.random.randint(streams[4], (IMAGES, 1), 0, GRID)
    places = jnp.arange(patches, dtype=jnp.int32)
    row_of = places // GRID
    col_of = places % GRID
    distance = (row_of[None, :] - centre_row) * (row_of[None, :] - centre_row) + (col_of[None, :] - centre_col) * (col_of[None, :] - centre_col)
    shuffle = jax.vmap(lambda sub: jax.random.permutation(sub, patches))(jax.random.split(streams[5], IMAGES))
    ranking = distance * patches + shuffle.astype(jnp.int32)
    ranks = jnp.argsort(jnp.argsort(ranking, axis=1, stable=True), axis=1, stable=True)
    chosen = (ranks < counts[:, None]).astype(jnp.int32)
    return jnp.concatenate([jnp.zeros((IMAGES, 1), jnp.int32), chosen], 1)


def draw_section_weight(key, part):
    key = jax.random.fold_in(key, 11)
    base = jax.random.normal(key, (SECTIONS, D, FF), jnp.float32) * D ** (-0.5)
    section_ids = lax.broadcasted_iota(jnp.int32, (SECTIONS, 1, FF), 0)
    columns = lax.broadcasted_iota(jnp.int32, (SECTIONS, 1, FF), 2)
    boost = jnp.where((section_ids % 2 == 0) & (columns >= 3 * D), 4.0, 1.0)
    return (base * boost).astype(jnp.bfloat16)


def draw_section_vectors(key, part):
    key = jax.random.fold_in(key, 12)
    streams = jax.random.split(key, 3)
    layout = (SECTIONS, 8, D)
    normal = jax.random.normal(streams[0], layout, jnp.float32)
    gains = jax.random.uniform(streams[1], layout, jnp.float32, 0.6, 1.4)
    scales = jnp.exp(jax.random.uniform(streams[2], layout, jnp.float32, math.log(0.5), math.log(1.5)))
    row_ids = lax.broadcasted_iota(jnp.int32, layout, 1)
    return jnp.where(row_ids == 0, gains, jnp.where(row_ids == 2, scales, jnp.where(row_ids == 6, normal, 0.3 * normal)))


def block_scale(stream_key, shape, shards, least, largest):
    def one(axis_at, parts):
        heights = jax.random.uniform(jax.random.fold_in(jax.random.fold_in(stream_key, 6), axis_at), (parts,), jnp.float32, least / len(shards), largest / len(shards))
        return jnp.repeat(jnp.exp(heights), shape[axis_at] // parts).reshape((-1,) + (1,) * (len(shape) - axis_at - 1))

    factor_of = one(*shards[0])
    for cut in shards[1:]:
        factor_of = factor_of * one(*cut)
    return factor_of


def gaussian(own_key, shape, deviation, bound, pieces=(), held_as=jnp.bfloat16):
    drawn = jax.random.normal(own_key, shape, jnp.float32) * deviation
    if len(pieces) > 0:
        drawn = block_scale(own_key, shape, pieces, -0.22, 0.18) * drawn
    return jnp.clip(drawn, min=-bound, max=bound).astype(held_as)


def setup_inputs(seed: int = 0) -> dict:
    key_of = jax.random.split(jax.random.key(seed), 8)
    embeds = gaussian(key_of[0], (IMAGES, L, D), 1.0, 6.0, ((0, 8),))
    mask = draw_mask(jax.random.fold_in(key_of[7], 71), 0)
    cotangent = gaussian(key_of[2], (IMAGES, L, D), 1.0, 6.0, ((0, 8),))
    section_weight = draw_section_weight(jax.random.fold_in(key_of[7], 71), 0)
    down_weight = gaussian(key_of[4], (SECTIONS, FF, D), FF ** -0.5, 0.109375, ((0, 4),))
    section_vectors = draw_section_vectors(jax.random.fold_in(key_of[7], 71), 0)
    rel_table = gaussian(key_of[6], (SECTIONS, H, RELS), 1.0, 4.0, ((0, 4),), jnp.float32)
    return dict(embeds=embeds, mask=mask, cotangent=cotangent, section_weight=section_weight, down_weight=down_weight, section_vectors=section_vectors, rel_table=rel_table)


@jax.custom_vjp
def low(v):
    return lax.optimization_barrier(v.astype(jnp.bfloat16)).astype(jnp.float32)

@jax.custom_vjp
def low_back(v):
    return v

def low_keep(v):
    return (low(v), None)

def low_pass(kept, grad):
    return (grad,)

def back_keep(v):
    return (v, None)

def back_low(kept, grad):
    return (low(grad),)
low.defvjp(low_keep, low_pass)
low_back.defvjp(back_keep, back_low)
EPS = 1e-06
HIGH = lax.Precision.HIGHEST

def norm_rows(values, gain, shift):
    center = values - lax.optimization_barrier(jnp.mean(values, -1, keepdims=True))
    spread = lax.optimization_barrier(jnp.mean(center * center, -1, keepdims=True))
    return center * lax.rsqrt(spread + EPS) * gain + shift

def relative_index(grid):
    side_len = 2 * grid - 1
    total = side_len * side_len + 3
    places = jnp.arange(grid * grid, dtype=jnp.int32)
    row_of = places // grid
    col_of = places % grid
    patch_part = (row_of[:, None] - row_of[None, :] + grid - 1) * side_len + (col_of[:, None] - col_of[None, :] + grid - 1)
    top_row = jnp.full((1, grid * grid), total - 3, jnp.int32)
    left_col = jnp.full((grid * grid, 1), total - 2, jnp.int32)
    corner = jnp.full((1, 1), total - 1, jnp.int32)
    upper = jnp.concatenate([corner, top_row], 1)
    lower_part = jnp.concatenate([left_col, patch_part.astype(jnp.int32)], 1)
    return jnp.concatenate([upper, lower_part], 0).astype(jnp.int32)

def matmul(left, right):
    return jnp.dot(left, right, precision=HIGH, preferred_element_type=jnp.float32)

def attend(stream, matrix, vectors, rel_bias, lookup):
    normed = low(norm_rows(stream, vectors[0], vectors[1]))
    joined = low_back(matmul(normed, matrix[:, :3 * D]))
    queries = low(joined[:, :D] + vectors[4]).reshape(L, H, HD)
    key_rows = low(joined[:, D:2 * D]).reshape(L, H, HD)
    value_rows = low(joined[:, 2 * D:] + vectors[5]).reshape(L, H, HD)
    raw = low_back(jnp.einsum('qhd,khd->hqk', queries, key_rows, precision=HIGH))
    scores = raw * HD ** (-0.5) + jnp.take(rel_bias, lookup, axis=1)
    weights_low = low(jax.nn.softmax(scores, axis=-1))
    context = low(low_back(jnp.einsum('hqk,khd->qhd', weights_low, value_rows, precision=HIGH).reshape(L, D)))
    branch = low_back(matmul(context, matrix[:, 3 * D:])) + vectors[3]
    return stream + vectors[2] * branch

def feed(stream, matrix, down_matrix, vectors):
    normed = low(norm_rows(stream, vectors[0], vectors[1]))
    hidden = low_back(matmul(normed, matrix)) + vectors[4:].reshape(-1)
    active = low(jax.nn.gelu(hidden, approximate=False))
    branch = low_back(matmul(active, down_matrix)) + vectors[3]
    return stream + vectors[2] * branch

def reference(embeds, mask, cotangent, section_weight, down_weight, section_vectors, rel_table):
    lookup = relative_index(GRID)
    params = (section_weight.astype(jnp.float32), down_weight.astype(jnp.float32), section_vectors, rel_table)
    count = embeds.shape[0]
    probes = jnp.zeros((count, SECTIONS, L, D), jnp.float32)

    def per_image(weights, embed_row, cover_row, probe):
        matrix, down_matrix, vectors, rel_bias = weights
        cover = cover_row.astype(jnp.float32)[:, None]
        stream = embed_row * (1.0 - cover) + vectors[0, 6] * cover
        sectioned = []
        for section_id in range(SECTIONS):
            if section_id > 0:
                stream = low_back(sectioned[-1]) + probe[section_id]
            if section_id % 2 == 0:
                result = attend(stream, matrix[section_id], vectors[section_id], rel_bias[section_id], lookup)
            else:
                result = feed(stream, matrix[section_id], down_matrix[section_id], vectors[section_id])
            sectioned.append(low(result))
        return jnp.stack(sectioned)

    def forward(weights, embed_all, probe_all):

        def one_image(item):
            return jax.checkpoint(per_image)(weights, item[0], item[1], item[2])
        return lax.map(one_image, (embed_all, mask, probe_all))
    sectioned_all, pull = jax.vjp(forward, params, embeds.astype(jnp.float32), probes)
    upstream = jnp.zeros_like(sectioned_all).at[:, SECTIONS - 1].set(cotangent.astype(jnp.float32))
    grad_params, grad_embeds, grad_probes = pull(upstream)
    activations = jnp.swapaxes(sectioned_all, 0, 1).astype(jnp.bfloat16)
    input_grads = jnp.swapaxes(grad_probes, 0, 1).at[0].set(grad_embeds)
    return (activations, input_grads, grad_params[0], grad_params[1], grad_params[2], grad_params[3])
```

```python
import math
from functools import partial

import jax
import jax.numpy as jnp
from jax import lax
from jax.experimental import pallas as pl
from jax.experimental.pallas import tpu as pltpu
from jax.sharding import PartitionSpec as P

EPS = 1e-06
F32 = jnp.float32
BF = jnp.bfloat16
HD = 64
ANY = pl.BlockSpec(memory_space=pl.ANY)
VMEM = pl.BlockSpec(memory_space=pltpu.VMEM)
SMEM = pl.BlockSpec(memory_space=pltpu.SMEM)


def dot(left, right):
    return jnp.dot(left, right, preferred_element_type=F32)


def dot_nt(left, right):
    return lax.dot_general(left, right, (((1,), (1,)), ((), ())), preferred_element_type=F32)


def dot_tn(left, right):
    return lax.dot_general(left, right, (((0,), (0,)), ((), ())), preferred_element_type=F32)


def norm_stats(x):
    center = x - jnp.mean(x, -1, keepdims=True)
    rstd = lax.rsqrt(jnp.mean(center * center, -1, keepdims=True) + EPS)
    return center * rstd, rstd


def norm_back(g, da, xhat, rstd, gain):
    w = da * gain
    return g + rstd * (w - jnp.mean(w, -1, keepdims=True) - xhat * jnp.mean(w * xhat, -1, keepdims=True))


def rows_sum(v):
    return jnp.sum(v, 0, keepdims=True)


def gelu_parts(h):
    z = jnp.abs(h) * 0.7071067811865476
    t = 1.0 / (1.0 + 0.3275911 * z)
    gauss = jnp.exp(-0.5 * h * h)
    poly = t * (0.127414796 + t * (-0.142248368 + t * (0.7107068705 + t * (-0.7265760135 + t * 0.5307027145))))
    tail = poly * gauss
    phi = jnp.where(h >= 0.0, 1.0 - tail, tail)
    return h * phi, phi + h * (gauss * 0.3989422804014327)


class Copies:
    def __init__(self, sems):
        self.sems, self.used, self.out = sems, 0, []

    def start(self, src, dst):
        copy = pltpu.make_async_copy(src, dst, self.sems.at[self.used])
        self.used += 1
        copy.start()
        return copy

    def choose(self, first, a, b, dst):
        sem = self.sems.at[self.used]
        self.used += 1

        @pl.when(first)
        def _():
            pltpu.make_async_copy(a, dst, sem).start()

        @pl.when(jnp.logical_not(first))
        def _():
            pltpu.make_async_copy(b, dst, sem).start()

        return pltpu.make_async_copy(a, dst, sem)

    def store(self, src, dst):
        self.out.append(self.start(src, dst))

    def store_choose(self, first, src, a, b):
        sem = self.sems.at[self.used]
        self.used += 1

        @pl.when(first)
        def _():
            pltpu.make_async_copy(src, a, sem).start()

        @pl.when(jnp.logical_not(first))
        def _():
            pltpu.make_async_copy(src, b, sem).start()

        self.out.append(pltpu.make_async_copy(src, a, sem))

    def finish(self):
        for copy in self.out:
            copy.wait()


def image_of(ref, i):
    return ref.at[i] if len(ref.shape) == 3 else ref


def head_masks(scale):
    lane = lax.broadcasted_iota(jnp.int32, (1, 2 * HD), 1)
    low = jnp.where(lane < HD, scale, 0.0).astype(BF)
    high = jnp.where(lane < HD, 0.0, scale).astype(BF)
    return low, high


def attend_forward(i, refs_in, refs_state, refs_extra, scratch):
    flags, x_ref, vec_ref, own_ref, other_ref, bias_ref = refs_in
    x_ref = image_of(x_ref, i)
    sa, a1, ctx, y1, pb = refs_state
    x_v, w_v, bias_v, a_v, qkv_v, pb_v, c_v, b_v, y_v, sems = scratch
    rows, width = x_v.shape
    heads, keys = pb_v.shape[0], pb_v.shape[2]

    @pl.when(flags[0] == 1)
    def _():
        cp = Copies(sems)
        first = flags[1] == 0
        in_x = cp.start(x_ref, x_v)
        three = pl.ds(0, 3 * width)
        last = pl.ds(3 * width, width)
        in_w = cp.choose(first, own_ref.at[:, three], other_ref.at[:, three], w_v.at[:, three])
        in_b = cp.start(bias_ref, bias_v)
        in_p = cp.choose(first, own_ref.at[:, last], other_ref.at[:, last], w_v.at[:, last])
        in_x.wait()
        cp.store(x_v, sa.at[i, 0])
        x = x_v[...].astype(F32)
        xhat, rstd = norm_stats(x)
        a_v[...] = (xhat * vec_ref[0:1, :] + vec_ref[1:2, :]).astype(BF)
        cp.store(a_v, a1.at[i])
        qkv_v[rows:, :] = jnp.zeros((keys - rows, 3 * width), BF)
        in_w.wait()
        a = a_v[...]
        block = 256
        for j in range(3 * width // block):
            cols = slice(j * block, (j + 1) * block)
            part = dot(a, w_v[:, cols])
            kind, at = divmod(j * block, width)
            if kind == 0:
                part = part + vec_ref[4:5, at : at + block]
            if kind == 2:
                part = part + vec_ref[5:6, at : at + block]
            qkv_v[0:rows, cols] = part.astype(BF)
        for kind in range(3):
            cp.store(qkv_v.at[0:rows, pl.ds(kind * width, width)], sa.at[i, 1 + kind])
        in_b.wait()
        scaled = head_masks(HD ** (-0.5))
        plain = head_masks(1.0)
        for j in range(heads // 2):
            q = qkv_v[0:rows, j * 128 : (j + 1) * 128]
            k = qkv_v[:, width + j * 128 : width + (j + 1) * 128]
            u = qkv_v[:, 2 * width + j * 128 : 2 * width + (j + 1) * 128]
            total = None
            for t in range(2):
                s = dot_nt(q * scaled[t], k) + bias_v[2 * j + t]
                e = jnp.exp(s - jnp.max(s, -1, keepdims=True))
                p = (e * (1.0 / jnp.sum(e, -1, keepdims=True))).astype(BF)
                pb_v[2 * j + t] = p
                part = dot(p, u * plain[t])
                total = part if total is None else total + part
            c_v[:, j * 128 : (j + 1) * 128] = total.astype(BF)
        cp.store(pb_v, pb.at[i])
        cp.store(c_v, ctx.at[i])
        in_p.wait()
        b = dot(c_v[...], w_v[:, 3 * width :]) + vec_ref[3:4, :]
        b_v[...] = b.astype(BF)
        cp.store(b_v, sa.at[i, 4])
        y_v[...] = (x_v[...].astype(F32) + vec_ref[2:3, :] * b).astype(BF)
        cp.store(y_v, y1.at[i])
        cp.finish()


def feed_forward(i, refs_in, refs_state, refs_extra, scratch):
    flags, y1, vec_ref, own_ref, other_ref, own_d, other_d = refs_in
    lh0, lh1, rh0, rh1, gp, b2, y2, dx1, vgf = refs_state
    (send,) = refs_extra
    x_v, w1_v, w2_v, a_v, g_v, gp_v, b_v, y_v, sems = scratch
    rows, width = x_v.shape
    hidden = g_v.shape[1]
    cuts = 4
    step = hidden // cuts

    @pl.when(flags[0] == 1)
    def _():
        cp = Copies(sems)
        first = flags[1] == 0
        in_x = cp.start(y1.at[i], x_v)
        in_1 = []
        for c in range(cuts):
            at = pl.ds(c * step, step)
            in_1.append(cp.choose(first, other_ref.at[:, at], own_ref.at[:, at], w1_v.at[:, at]))
        in_2 = cp.choose(first, other_d, own_d, w2_v)
        in_x.wait()
        xhat, rstd = norm_stats(x_v[...].astype(F32))
        a_v[...] = (xhat * vec_ref[0:1, :] + vec_ref[1:2, :]).astype(BF)
        cp.store_choose(first, a_v, rh1.at[i], rh0.at[i])
        a = a_v[...]
        block = 256
        for j in range(hidden // block):
            if j * block % step == 0:
                in_1[j * block // step].wait()
            row, at = divmod(j * block, width)
            cols = slice(j * block, (j + 1) * block)
            h = dot(a, w1_v[:, cols]) + vec_ref[4 + row : 5 + row, at : at + block]
            value, slope = gelu_parts(h)
            g_v[:, cols] = value.astype(BF)
            gp_v[:, cols] = slope.astype(BF)
        cp.store_choose(first, g_v, lh0.at[i], lh1.at[i])
        cp.store(gp_v, gp.at[i])
        in_2.wait()
        b = dot(g_v[...], w2_v[...]) + vec_ref[3:4, :]
        b_v[...] = b.astype(BF)
        y_v[...] = (x_v[...].astype(F32) + vec_ref[2:3, :] * b).astype(BF)
        cp.store(y_v, send)
        cp.store(b_v, b2.at[i])
        cp.store(y_v, y2.at[i])
        cp.finish()


def feed_backward(i, refs_in, refs_state, refs_extra, scratch):
    flags, g_ref, vec_ref, own_ref, other_ref, own_d, other_d, y1 = refs_in
    lh0, lh1, rh0, rh1, gp, b2, y2, dx1, vgf = refs_state
    g_ref = image_of(g_ref, i)
    x_v, gin_v, w1_v, w2_v, gp_v, b_v, e_v, dh_v, dx_v, vg_v, sems = scratch
    rows, width = x_v.shape
    hidden = dh_v.shape[1]
    cuts = 4
    step = hidden // cuts

    @pl.when(flags[0] == 1)
    def _():
        cp = Copies(sems)
        first = flags[1] == 0
        in_g = cp.start(g_ref, gin_v)
        in_2 = []
        for c in range(cuts):
            at = pl.ds(c * step, step)
            in_2.append(cp.choose(first, other_d.at[at], own_d.at[at], w2_v.at[at]))
        in_p = cp.start(gp.at[i], gp_v)
        in_b = cp.start(b2.at[i], b_v)
        in_x = cp.start(y1.at[i], x_v)
        in_1 = cp.choose(first, other_ref, own_ref, w1_v)
        in_g.wait()
        g = gin_v[...].astype(F32)
        scaled = g * vec_ref[2:3, :]
        e_v[...] = scaled.astype(BF)
        cp.store_choose(first, e_v, rh0.at[i], rh1.at[i])
        vg_v[3:4, :] = rows_sum(scaled)
        in_p.wait()
        e = e_v[...]
        block = 256
        for j in range(hidden // block):
            if j * block % step == 0:
                in_2[j * block // step].wait()
            row, at = divmod(j * block, width)
            cols = slice(j * block, (j + 1) * block)
            dh = dot_nt(e, w2_v[cols, :]) * gp_v[:, cols].astype(F32)
            dh_v[:, cols] = dh.astype(BF)
            vg_v[4 + row : 5 + row, at : at + block] = rows_sum(dh)
        cp.store_choose(first, dh_v, lh1.at[i], lh0.at[i])
        in_b.wait()
        vg_v[2:3, :] = rows_sum(gin_v[...].astype(F32) * b_v[...].astype(F32))
        in_x.wait()
        in_1.wait()
        da = dot_nt(dh_v[...], w1_v[...])
        xhat, rstd = norm_stats(x_v[...].astype(F32))
        vg_v[0:1, :] = rows_sum(da * xhat)
        vg_v[1:2, :] = rows_sum(da)
        dx = norm_back(gin_v[...].astype(F32), da, xhat, rstd, vec_ref[0:1, :])
        dx_v[...] = dx.astype(BF)
        cp.store(dx_v, dx1.at[i])
        cp.store(vg_v, vgf.at[i])
        cp.finish()


def attend_backward(i, refs_in, refs_state, refs_extra, scratch):
    flags, dx1, vec_ref, own_ref, other_ref, sa, pb = refs_in
    ea, dq, dl, dx0, vga = refs_state
    (send,) = refs_extra
    x_v, gin_v, w_v, pb_v, b_v, e_v, qkv_v, dc_v, dq_v, dl_v, dx_v, vg_v, sems = scratch
    rows, width = x_v.shape
    heads, keys = pb_v.shape[0], pb_v.shape[2]

    @pl.when(flags[0] == 1)
    def _():
        cp = Copies(sems)
        first = flags[1] == 0
        three = pl.ds(0, 3 * width)
        last = pl.ds(3 * width, width)
        in_g = cp.start(dx1.at[i], gin_v)
        in_p = cp.choose(first, own_ref.at[:, last], other_ref.at[:, last], w_v.at[:, last])
        ins = [cp.start(sa.at[i, 1 + kind], qkv_v.at[0:rows, pl.ds(kind * width, width)]) for kind in range(3)]
        in_pb = cp.start(pb.at[i], pb_v)
        in_b = cp.start(sa.at[i, 4], b_v)
        in_x = cp.start(sa.at[i, 0], x_v)
        in_w = cp.choose(first, own_ref.at[:, three], other_ref.at[:, three], w_v.at[:, three])
        qkv_v[rows:, :] = jnp.zeros((keys - rows, 3 * width), BF)
        in_g.wait()
        scaled = gin_v[...].astype(F32) * vec_ref[2:3, :]
        e_v[...] = scaled.astype(BF)
        cp.store(e_v, ea.at[i])
        vg_v[3:4, :] = rows_sum(scaled)
        vg_v[6:8, :] = jnp.zeros((2, width), F32)
        in_p.wait()
        dc_v[...] = dot_nt(e_v[...], w_v[:, 3 * width :]).astype(BF)
        for copy in ins:
            copy.wait()
        in_pb.wait()
        factor = HD ** (-0.5)
        plain = head_masks(1.0)
        for j in range(heads // 2):
            cols = slice(j * 128, (j + 1) * 128)
            q = qkv_v[0:rows, j * 128 : (j + 1) * 128]
            k = qkv_v[:, width + j * 128 : width + (j + 1) * 128]
            u = qkv_v[:, 2 * width + j * 128 : 2 * width + (j + 1) * 128]
            dc = dc_v[:, cols]
            dq_t, dk_t, du_t = None, None, None
            for t in range(2):
                dc_t = dc * plain[t]
                p = pb_v[2 * j + t]
                dp = dot_nt(dc_t, u)
                pf = p.astype(F32)
                wp = pf * dp
                ds = wp - pf * jnp.sum(wp, -1, keepdims=True)
                dlog = (ds * factor).astype(BF)
                dl_v[2 * j + t] = dlog
                du = dot_tn(p, dc_t)
                dqp = dot(dlog, k * plain[t])
                dkp = dot_tn(dlog, q * plain[t])
                dq_t = dqp if dq_t is None else dq_t + dqp
                dk_t = dkp if dk_t is None else dk_t + dkp
                du_t = du if du_t is None else du_t + du
            dq_v[:, j * 128 : (j + 1) * 128] = dq_t.astype(BF)
            dq_v[:, width + j * 128 : width + (j + 1) * 128] = dk_t[0:rows].astype(BF)
            dq_v[:, 2 * width + j * 128 : 2 * width + (j + 1) * 128] = du_t[0:rows].astype(BF)
            vg_v[4:5, cols] = rows_sum(dq_t)
            vg_v[5:6, cols] = rows_sum(du_t)
        cp.store(dl_v, dl.at[i])
        cp.store(dq_v, dq.at[i])
        in_b.wait()
        vg_v[2:3, :] = rows_sum(gin_v[...].astype(F32) * b_v[...].astype(F32))
        in_x.wait()
        in_w.wait()
        da = dot_nt(dq_v[...], w_v[:, 0 : 3 * width])
        xhat, rstd = norm_stats(x_v[...].astype(F32))
        vg_v[0:1, :] = rows_sum(da * xhat)
        vg_v[1:2, :] = rows_sum(da)
        dx = norm_back(gin_v[...].astype(F32), da, xhat, rstd, vec_ref[0:1, :])
        dx_v[...] = dx.astype(BF)
        cp.store(dx_v, send)
        cp.store(dx_v, dx0.at[i])
        cp.store(vg_v, vga.at[i])
        cp.finish()


def run(body, i, name, ins, specs, state, shapes, extra, scratch, sems, flops, moved):
    fresh = state is None
    n_in, n_state, n_extra = len(ins), len(shapes), len(extra)
    given = 0 if fresh else n_state

    def kernel(*refs):
        refs_in = refs[:n_in]
        outs = refs[n_in + given : n_in + given + n_state]
        more = refs[n_in + given + n_state : n_in + given + n_state + n_extra]
        body(i, refs_in, outs, more, refs[n_in + given + n_state + n_extra :])

    made = pl.pallas_call(
        kernel,
        out_shape=tuple(shapes) + tuple(extra),
        in_specs=list(specs) + [ANY] * given,
        out_specs=tuple([ANY] * (n_state + n_extra)),
        scratch_shapes=[pltpu.VMEM(s.shape, s.dtype) for s in scratch] + [pltpu.SemaphoreType.DMA((sems,))],
        input_output_aliases={} if fresh else {n_in + k: k for k in range(n_state)},
        compiler_params=pltpu.CompilerParams(vmem_limit_bytes=56 * 2**20),
        cost_estimate=pl.CostEstimate(flops=flops, bytes_accessed=moved, transcendentals=0),
        name=name,
    )(*ins, *([] if fresh else state))
    return list(made[:n_state]), list(made[n_state:])


def sd(shape, dtype=BF):
    return jax.ShapeDtypeStruct(shape, dtype)


class Kernels:
    def __init__(self, images, rows, keys, width, hidden, heads):
        self.n, self.r, self.k, self.d, self.f, self.h = images, rows, keys, width, hidden, heads

    def att_f(self, i, flags, x, vec, own, other, bias, state):
        n, r, k, d, h = self.n, self.r, self.k, self.d, self.h
        shapes = [sd((n, 5, r, d)), sd((n, r, d)), sd((n, r, d)), sd((n, r, d)), sd((n, h, r, k))]
        scratch = [sd((r, d)), sd((d, 4 * d)), sd((h, r, k), F32), sd((r, d)), sd((k, 3 * d)), sd((h, r, k)), sd((r, d)), sd((r, d)), sd((r, d))]
        return run(attend_forward, i, "attend_forward", [flags, x, vec, own, other, bias], [SMEM, ANY, VMEM, ANY, ANY, ANY], state, shapes, [], scratch, 16, 2 * r * d * 4 * d + 4 * h * r * k * HD, 12000000)

    def feed_state(self):
        n, r, d, f = self.n, self.r, self.d, self.f
        wide, narrow = sd((n, r, f)), sd((n, r, d))
        return [wide, wide, narrow, narrow, wide, narrow, narrow, narrow, sd((n, 8, d), F32)]

    def ff_f(self, i, flags, y1, vec, own, other, own_d, other_d, state):
        r, d, f = self.r, self.d, self.f
        scratch = [sd((r, d)), sd((d, f)), sd((f, d)), sd((r, d)), sd((r, f)), sd((r, f)), sd((r, d)), sd((r, d))]
        return run(feed_forward, i, "feed_forward", [flags, y1, vec, own, other, own_d, other_d], [SMEM, ANY, VMEM, ANY, ANY, ANY, ANY], state, self.feed_state(), [sd((r, d))], scratch, 16, 4 * r * d * f, 12000000)

    def ff_b(self, i, flags, g, vec, own, other, own_d, other_d, y1, state):
        r, d, f = self.r, self.d, self.f
        scratch = [sd((r, d)), sd((r, d)), sd((d, f)), sd((f, d)), sd((r, f)), sd((r, d)), sd((r, d)), sd((r, f)), sd((r, d)), sd((8, d), F32)]
        return run(feed_backward, i, "feed_backward", [flags, g, vec, own, other, own_d, other_d, y1], [SMEM, ANY, VMEM] + [ANY] * 5, state, self.feed_state(), [], scratch, 16, 4 * r * d * f, 12000000)

    def att_b(self, i, flags, dx1, vec, own, other, sa, pb, state):
        n, r, k, d, h = self.n, self.r, self.k, self.d, self.h
        shapes = [sd((n, r, d)), sd((n, r, 3 * d)), sd((n, h, r, k)), sd((n, r, d)), sd((n, 8, d), F32)]
        scratch = [sd((r, d)), sd((r, d)), sd((d, 4 * d)), sd((h, r, k)), sd((r, d)), sd((r, d)), sd((k, 3 * d)), sd((r, d)), sd((r, 3 * d)), sd((h, r, k)), sd((r, d)), sd((8, d), F32)]
        return run(attend_backward, i, "attend_backward", [flags, dx1, vec, own, other, sa, pb], [SMEM, ANY, VMEM] + [ANY] * 4, state, shapes, [sd((r, d))], scratch, 20, 2 * r * d * 4 * d + 8 * h * r * k * HD, 12000000)


def swap(block, pairs):
    return lax.ppermute(block, "section", pairs)


def bias_rows(table, grid, rows, keys):
    heads = table.shape[0]
    side = 2 * grid - 1
    flipped = table[:, : side * side].reshape(heads, side, side)[:, ::-1, ::-1]
    by_col = jnp.stack([flipped[:, :, grid - 1 - c : side - c] for c in range(grid)], 1)
    by_col = by_col.reshape(heads, grid, side * grid)
    patches = grid * grid
    block = jnp.concatenate(
        [by_col[:, :, grid * (grid - 1 - r) : grid * (grid - 1 - r) + patches] for r in range(grid)], 1
    )
    upper = jnp.broadcast_to(table[:, side * side][:, None, None], (heads, 1, patches))
    left = jnp.broadcast_to(table[:, side * side + 1][:, None, None], (heads, patches, 1))
    corner = table[:, side * side + 2][:, None, None]
    full = jnp.concatenate([jnp.concatenate([corner, upper], 2), jnp.concatenate([left, block], 2)], 1)
    full = jnp.pad(full, ((0, 0), (0, rows - patches - 1), (0, 0)))
    return jnp.pad(full, ((0, 0), (0, 0), (0, keys - patches - 1)), constant_values=-1e30)


def table_sums(grad, grid):
    heads = grad.shape[0]
    side, patches = 2 * grid - 1, grid * grid
    block = grad[:, 1:, 1:]
    wide = side * grid
    by_col = 0.0
    for r in range(grid):
        at = grid * (grid - 1 - r)
        by_col = by_col + jnp.pad(block[:, r * grid : (r + 1) * grid], ((0, 0), (0, 0), (at, wide - at - patches)))
    by_col = by_col.reshape(heads, grid, side, grid)
    flipped = 0.0
    for c in range(grid):
        at = grid - 1 - c
        flipped = flipped + jnp.pad(by_col[:, c], ((0, 0), (0, 0), (at, side - at - grid)))
    inner = flipped[:, ::-1, ::-1].reshape(heads, side * side)
    tail = jnp.stack([jnp.sum(grad[:, 0, 1:], 1), jnp.sum(grad[:, 1:, 0], 1), grad[:, 0, 0]], 1)
    return jnp.concatenate([inner, tail], 1)


def ring_sum(jobs, axis):
    n = lax.axis_size(axis)
    if n > 16 or n % 2:
        return [
            lax.psum((own.astype(F32) + other.astype(F32)).astype(BF), axis) for own, other, streams in jobs
        ]
    order = list(range(0, n, 2)) + list(range(n - 1, 0, -2))
    place = [0] * n
    for k, device in enumerate(order):
        place[device] = k
    at = jnp.array(place, jnp.int32)[lax.axis_index(axis)]
    route = {
        1: [(order[k], order[(k + 1) % n]) for k in range(n)],
        -1: [(order[k], order[(k - 1) % n]) for k in range(n)],
    }
    lanes = []
    totals = []
    for number, (own, other, streams) in enumerate(jobs):
        tall, wide = own.shape[0] // n, own.shape[1] // streams
        totals.append(jnp.zeros(own.shape, BF))
        for s in range(streams):
            lanes.append((number, own, other, tall, wide, s, 1 if s % 2 == 0 else -1))

    def take(lane, chunk):
        number, own, other, tall, wide, s, way = lane
        corner = ((chunk % n) * tall, s * wide)
        left = lax.dynamic_slice(own, corner, (tall, wide)).astype(F32)
        return left + lax.dynamic_slice(other, corner, (tall, wide)).astype(F32)

    def put(lane, chunk, value):
        number, own, other, tall, wide, s, way = lane
        totals[number] = lax.dynamic_update_slice(totals[number], value, ((chunk % n) * tall, s * wide))

    held = [take(lane, at).astype(BF) for lane in lanes]
    for k in range(n - 1):
        for m, lane in enumerate(lanes):
            got = lax.ppermute(held[m], axis, route[lane[6]])
            held[m] = (got.astype(F32) + take(lane, at - lane[6] * (k + 1))).astype(BF)
    for m, lane in enumerate(lanes):
        put(lane, at + lane[6], held[m])
    for k in range(n - 1):
        for m, lane in enumerate(lanes):
            held[m] = lax.ppermute(held[m], axis, route[lane[6]])
            put(lane, at - lane[6] * k, held[m])
    return totals


def on_device(embeds, mask, cotangent, section_weight, down_weight, section_vectors, rel_table):
    sections = lax.axis_size("section")
    now = lax.axis_index("section")
    core, stage = now % 2, now // 2
    images, length, width = embeds.shape
    half = images // 2
    hidden = section_weight.shape[2]
    heads = rel_table.shape[1]
    rows, keys = -(-length // 16) * 16, -(-length // 128) * 128
    grid = math.isqrt(length - 1)
    both = [(s, s ^ 1) for s in range(sections)]
    to_low = [(s, s - 1) for s in range(1, sections, 2)]
    to_high = [(s, s + 1) for s in range(0, sections, 2)]
    onward = [(s, s + 2) for s in range(sections - 2)]
    back = [(s + 2, s) for s in range(sections - 2)]
    low = core == 0

    own_w, own_d, own_v, own_t = section_weight[0], down_weight[0], section_vectors[0], rel_table[0]
    other_v = swap(own_v, both)
    table = jnp.where(low, own_t, swap(own_t, to_high))
    other_w = swap(own_w, both)
    other_d = swap(own_d, to_low)
    vec_a, vec_f = jnp.where(low, own_v, other_v), jnp.where(low, other_v, own_v)
    bias = bias_rows(table, grid, rows, keys)

    def mine_of(block):
        return lax.dynamic_slice_in_dim(block, core * half, half, 0)

    cover = mine_of(mask)[:, :, None] == 1
    start = jnp.where(cover, vec_a[6].astype(BF), mine_of(embeds))
    pad = ((0, 0), (0, rows - length), (0, 0))
    start = jnp.pad(start, pad)
    upstream = jnp.pad(mine_of(cotangent), pad)

    kern = Kernels(half, rows, keys, width, hidden, heads)
    flags_a = jnp.stack([(stage == 0).astype(jnp.int32), core])
    flags_b = jnp.stack([(stage == 1).astype(jnp.int32), core])
    att, feed = None, None

    def forward(i, flags, x):
        nonlocal att, feed
        att, _ = kern.att_f(i, flags, x, vec_a, own_w, other_w, bias, att)
        feed, (send,) = kern.ff_f(i, flags, att[3], vec_f, own_w, other_w, own_d, other_d, feed)
        return send

    arrived = [swap(forward(i, flags_a, start), onward) for i in range(half)]
    for i in range(half):
        forward(i, flags_b, arrived[i])

    grads = None

    def backward(i, flags, g):
        nonlocal feed, grads
        feed, _ = kern.ff_b(i, flags, g, vec_f, own_w, other_w, own_d, other_d, att[3], feed)
        grads, (send,) = kern.att_b(i, flags, feed[7], vec_a, own_w, other_w, att[0], att[4], grads)
        return send

    returned = [swap(backward(i, flags_b, upstream), back) for i in range(half)]
    for i in range(half):
        backward(i, flags_a, returned[i])

    sa, a1, ctx, y1, pb = att
    lh0, lh1, rh0, rh1, gp, b2, y2, dx1, vgf = feed
    ea, dq, dl, dx0, vga = grads

    def flat(block):
        return block.reshape(half * rows, block.shape[2])

    sent_f = dot_tn(flat(rh0), flat(lh0)).astype(BF)
    got_f = swap(sent_f, both)
    own_f = dot_tn(flat(rh1), flat(lh1)).astype(BF)

    part = width // 2

    def att_part(which):
        left = lax.dynamic_slice_in_dim(flat(a1), which * part, part, 1)
        right = lax.dynamic_slice_in_dim(flat(ctx), which * part, part, 1)
        return jnp.concatenate([dot_tn(left, flat(dq)).astype(BF), dot_tn(right, flat(ea)).astype(BF)], 1)

    got_a = swap(att_part(1 - core), both)
    own_a = att_part(core)
    sum_f, sum_a = ring_sum([(own_f, got_f, 4), (own_a, got_a, 4)], "dp")

    from_f = swap(sum_f, to_high)
    from_a = swap(sum_a, to_low)
    grad_weight = jnp.where(low, jnp.concatenate([sum_a, from_a], 0), from_f).astype(F32)
    grad_down = jnp.where(low, 0.0, sum_f.astype(F32)).T

    rows_a = jnp.sum(vga, 0)
    token = jnp.sum(jnp.where(cover, dx0[:, :length].astype(F32), 0.0), (0, 1))
    rows_a = rows_a.at[6].add(jnp.where(stage == 0, token, 0.0))
    rows_f = jnp.sum(vgf, 0)
    rows_sum_ = jnp.where(low, rows_a, rows_f) + swap(jnp.where(low, rows_f, rows_a), both)
    scores = jnp.sum(dl[:, :, :length, :length].astype(F32), 0)
    sums = table_sums(scores, grid) * (HD ** 0.5)
    sums = jnp.where(low, sums + swap(sums, to_low), 0.0)
    grad_rows, grad_table = lax.psum((rows_sum_, sums), "dp")

    def gather_images(a_part, f_part):
        mine, theirs = jnp.where(low, a_part, f_part), jnp.where(low, f_part, a_part)
        got = swap(theirs, both)
        return jnp.concatenate([jnp.where(low, mine, got), jnp.where(low, got, mine)], 0)[:, :length]

    activations = gather_images(y1, y2)
    input_grads = gather_images(dx0, dx1).astype(F32)
    hide = (mask[:, :, None] == 1) & (now == 0)
    input_grads = jnp.where(hide, 0.0, input_grads)
    return (
        activations[None],
        input_grads[None],
        grad_weight[None],
        grad_down[None],
        grad_rows[None],
        grad_table[None],
    )


def solution(mesh):
    placed = (
        P("dp", None, None),
        P("dp", None),
        P("dp", None, None),
        P("section", None, None),
        P("section", None, None),
        P("section", None, None),
        P("section", None, None),
    )
    return jax.shard_map(
        on_device,
        mesh=mesh,
        in_specs=placed,
        out_specs=(
            P("section", "dp", None, None),
            P("section", "dp", None, None),
            P("section", None, None),
            P("section", None, None),
            P("section", None, None),
            P("section", None, None),
        ),
        check_vma=False,
    )
```

```python
import math
from functools import partial

import jax
import jax.numpy as jnp
from jax import lax
from jax.experimental import pallas as pl
from jax.experimental.pallas import tpu as pltpu
from jax.sharding import PartitionSpec as P

EPS = 1e-06
F32 = jnp.float32
BF = jnp.bfloat16
HD = 64
RING = 8
ANY = pl.BlockSpec(memory_space=pl.ANY)
VMEM = pl.BlockSpec(memory_space=pltpu.VMEM)
SMEM = pl.BlockSpec(memory_space=pltpu.SMEM)


def dot(left, right):
    return jnp.dot(left, right, preferred_element_type=F32)


def dot_nt(left, right):
    return lax.dot_general(left, right, (((1,), (1,)), ((), ())), preferred_element_type=F32)


def dot_tn(left, right):
    return lax.dot_general(left, right, (((0,), (0,)), ((), ())), preferred_element_type=F32)


def norm_stats(x):
    center = x - jnp.mean(x, -1, keepdims=True)
    rstd = lax.rsqrt(jnp.mean(center * center, -1, keepdims=True) + EPS)
    return center * rstd, rstd


def norm_back(g, da, xhat, rstd, gain):
    w = da * gain
    return g + rstd * (w - jnp.mean(w, -1, keepdims=True) - xhat * jnp.mean(w * xhat, -1, keepdims=True))


def rows_sum(v):
    return jnp.sum(v, 0, keepdims=True)


def gelu_parts(h):
    z = jnp.abs(h) * 0.7071067811865476
    t = 1.0 / (1.0 + 0.3275911 * z)
    gauss = jnp.exp(-0.5 * h * h)
    poly = t * (0.127414796 + t * (-0.142248368 + t * (0.7107068705 + t * (-0.7265760135 + t * 0.5307027145))))
    tail = poly * gauss
    phi = jnp.where(h >= 0.0, 1.0 - tail, tail)
    return h * phi, phi + h * (gauss * 0.3989422804014327)


class Copies:
    def __init__(self, sems):
        self.sems, self.used, self.out = sems, 0, []

    def start(self, src, dst):
        copy = pltpu.make_async_copy(src, dst, self.sems.at[self.used])
        self.used += 1
        copy.start()
        return copy

    def choose(self, first, a, b, dst):
        sem = self.sems.at[self.used]
        self.used += 1

        @pl.when(first)
        def _():
            pltpu.make_async_copy(a, dst, sem).start()

        @pl.when(jnp.logical_not(first))
        def _():
            pltpu.make_async_copy(b, dst, sem).start()

        return pltpu.make_async_copy(a, dst, sem)

    def store(self, src, dst):
        self.out.append(self.start(src, dst))

    def finish(self):
        for copy in self.out:
            copy.wait()


def image_of(ref, i):
    return ref.at[i] if len(ref.shape) == 3 else ref


def head_masks(scale):
    lane = lax.broadcasted_iota(jnp.int32, (1, 2 * HD), 1)
    low = jnp.where(lane < HD, scale, 0.0).astype(BF)
    high = jnp.where(lane < HD, 0.0, scale).astype(BF)
    return low, high


def attend_forward(i, refs_in, refs_state, refs_extra, scratch):
    flags, x_ref, vec_ref, own_ref, other_ref, bias_ref = refs_in
    x_ref = image_of(x_ref, i)
    sa, a1, ctx, y1, pb = refs_state
    x_v, w_v, bias_v, a_v, qkv_v, pb_v, c_v, b_v, y_v, sems = scratch
    rows, width = x_v.shape
    heads, keys = pb_v.shape[0], pb_v.shape[2]

    @pl.when(flags[0] == 1)
    def _():
        cp = Copies(sems)
        first = flags[1] == 0
        in_x = cp.start(x_ref, x_v)
        three = pl.ds(0, 3 * width)
        last = pl.ds(3 * width, width)
        in_w = cp.choose(first, own_ref.at[:, three], other_ref.at[:, three], w_v.at[:, three])
        in_b = cp.start(bias_ref, bias_v)
        in_p = cp.choose(first, own_ref.at[:, last], other_ref.at[:, last], w_v.at[:, last])
        in_x.wait()
        cp.store(x_v, sa.at[i, 0])
        x = x_v[...].astype(F32)
        xhat, rstd = norm_stats(x)
        a_v[...] = (xhat * vec_ref[0:1, :] + vec_ref[1:2, :]).astype(BF)
        cp.store(a_v, a1.at[i])
        qkv_v[rows:, :] = jnp.zeros((keys - rows, 3 * width), BF)
        in_w.wait()
        a = a_v[...]
        block = 256
        for j in range(3 * width // block):
            cols = slice(j * block, (j + 1) * block)
            part = dot(a, w_v[:, cols])
            kind, at = divmod(j * block, width)
            if kind == 0:
                part = part + vec_ref[4:5, at : at + block]
            if kind == 2:
                part = part + vec_ref[5:6, at : at + block]
            qkv_v[0:rows, cols] = part.astype(BF)
        for kind in range(3):
            cp.store(qkv_v.at[0:rows, pl.ds(kind * width, width)], sa.at[i, 1 + kind])
        in_b.wait()
        scaled = head_masks(HD ** (-0.5))
        plain = head_masks(1.0)
        for j in range(heads // 2):
            q = qkv_v[0:rows, j * 128 : (j + 1) * 128]
            k = qkv_v[:, width + j * 128 : width + (j + 1) * 128]
            u = qkv_v[:, 2 * width + j * 128 : 2 * width + (j + 1) * 128]
            total = None
            for t in range(2):
                s = dot_nt(q * scaled[t], k) + bias_v[2 * j + t]
                e = jnp.exp(s - jnp.max(s, -1, keepdims=True))
                p = (e * (1.0 / jnp.sum(e, -1, keepdims=True))).astype(BF)
                pb_v[2 * j + t] = p
                part = dot(p, u * plain[t])
                total = part if total is None else total + part
            c_v[:, j * 128 : (j + 1) * 128] = total.astype(BF)
        cp.store(pb_v, pb.at[i])
        cp.store(c_v, ctx.at[i])
        in_p.wait()
        b = dot(c_v[...], w_v[:, 3 * width :]) + vec_ref[3:4, :]
        b_v[...] = b.astype(BF)
        cp.store(b_v, sa.at[i, 4])
        y_v[...] = (x_v[...].astype(F32) + vec_ref[2:3, :] * b).astype(BF)
        cp.store(y_v, y1.at[i])
        cp.finish()


def feed_forward(i, refs_in, refs_state, refs_extra, scratch):
    flags, y1, vec_ref, own_ref, other_ref, own_d, other_d = refs_in
    g_all, dh_all, a2, ef, gp, b2, y2, dx1, vgf = refs_state
    (send,) = refs_extra
    x_v, w1_v, w2_v, a_v, g_v, gp_v, b_v, y_v, sems = scratch
    rows, width = x_v.shape
    hidden = g_v.shape[1]
    cuts = 4
    step = hidden // cuts

    @pl.when(flags[0] == 1)
    def _():
        cp = Copies(sems)
        first = flags[1] == 0
        in_x = cp.start(y1.at[i], x_v)
        in_1 = []
        for c in range(cuts):
            at = pl.ds(c * step, step)
            in_1.append(cp.choose(first, other_ref.at[:, at], own_ref.at[:, at], w1_v.at[:, at]))
        in_2 = cp.choose(first, other_d, own_d, w2_v)
        in_x.wait()
        xhat, rstd = norm_stats(x_v[...].astype(F32))
        a_v[...] = (xhat * vec_ref[0:1, :] + vec_ref[1:2, :]).astype(BF)
        cp.store(a_v, a2.at[i])
        a = a_v[...]
        block = 256
        for j in range(hidden // block):
            if j * block % step == 0:
                in_1[j * block // step].wait()
            row, at = divmod(j * block, width)
            cols = slice(j * block, (j + 1) * block)
            h = dot(a, w1_v[:, cols]) + vec_ref[4 + row : 5 + row, at : at + block]
            value, slope = gelu_parts(h)
            g_v[:, cols] = value.astype(BF)
            gp_v[:, cols] = slope.astype(BF)
        cp.store(g_v, g_all.at[i])
        cp.store(gp_v, gp.at[i])
        in_2.wait()
        b = dot(g_v[...], w2_v[...]) + vec_ref[3:4, :]
        b_v[...] = b.astype(BF)
        y_v[...] = (x_v[...].astype(F32) + vec_ref[2:3, :] * b).astype(BF)
        cp.store(y_v, send)
        cp.store(b_v, b2.at[i])
        cp.store(y_v, y2.at[i])
        cp.finish()


def feed_backward(i, refs_in, refs_state, refs_extra, scratch):
    flags, g_ref, vec_ref, own_ref, other_ref, own_d, other_d, y1 = refs_in
    g_all, dh_all, a2, ef, gp, b2, y2, dx1, vgf = refs_state
    g_ref = image_of(g_ref, i)
    x_v, gin_v, w1_v, w2_v, gp_v, b_v, e_v, dh_v, dx_v, vg_v, sems = scratch
    rows, width = x_v.shape
    hidden = dh_v.shape[1]
    cuts = 4
    step = hidden // cuts

    @pl.when(flags[0] == 1)
    def _():
        cp = Copies(sems)
        first = flags[1] == 0
        in_g = cp.start(g_ref, gin_v)
        in_2 = []
        for c in range(cuts):
            at = pl.ds(c * step, step)
            in_2.append(cp.choose(first, other_d.at[at], own_d.at[at], w2_v.at[at]))
        in_p = cp.start(gp.at[i], gp_v)
        in_b = cp.start(b2.at[i], b_v)
        in_x = cp.start(y1.at[i], x_v)
        in_1 = cp.choose(first, other_ref, own_ref, w1_v)
        in_g.wait()
        g = gin_v[...].astype(F32)
        scaled = g * vec_ref[2:3, :]
        e_v[...] = scaled.astype(BF)
        cp.store(e_v, ef.at[i])
        vg_v[3:4, :] = rows_sum(scaled)
        in_p.wait()
        e = e_v[...]
        block = 256
        for j in range(hidden // block):
            if j * block % step == 0:
                in_2[j * block // step].wait()
            row, at = divmod(j * block, width)
            cols = slice(j * block, (j + 1) * block)
            dh = dot_nt(e, w2_v[cols, :]) * gp_v[:, cols].astype(F32)
            dh_v[:, cols] = dh.astype(BF)
            vg_v[4 + row : 5 + row, at : at + block] = rows_sum(dh)
        cp.store(dh_v, dh_all.at[i])
        in_b.wait()
        vg_v[2:3, :] = rows_sum(gin_v[...].astype(F32) * b_v[...].astype(F32))
        in_x.wait()
        in_1.wait()
        da = dot_nt(dh_v[...], w1_v[...])
        xhat, rstd = norm_stats(x_v[...].astype(F32))
        vg_v[0:1, :] = rows_sum(da * xhat)
        vg_v[1:2, :] = rows_sum(da)
        dx = norm_back(gin_v[...].astype(F32), da, xhat, rstd, vec_ref[0:1, :])
        dx_v[...] = dx.astype(BF)
        cp.store(dx_v, dx1.at[i])
        cp.store(vg_v, vgf.at[i])
        cp.finish()


def attend_backward(i, refs_in, refs_state, refs_extra, scratch):
    flags, dx1, vec_ref, own_ref, other_ref, sa, pb = refs_in
    ea, dq, dl, dx0, vga = refs_state
    (send,) = refs_extra
    x_v, gin_v, w_v, pb_v, b_v, e_v, qkv_v, dc_v, dq_v, dl_v, dx_v, vg_v, sems = scratch
    rows, width = x_v.shape
    heads, keys = pb_v.shape[0], pb_v.shape[2]

    @pl.when(flags[0] == 1)
    def _():
        cp = Copies(sems)
        first = flags[1] == 0
        three = pl.ds(0, 3 * width)
        last = pl.ds(3 * width, width)
        in_g = cp.start(dx1.at[i], gin_v)
        in_p = cp.choose(first, own_ref.at[:, last], other_ref.at[:, last], w_v.at[:, last])
        ins = [cp.start(sa.at[i, 1 + kind], qkv_v.at[0:rows, pl.ds(kind * width, width)]) for kind in range(3)]
        in_pb = cp.start(pb.at[i], pb_v)
        in_b = cp.start(sa.at[i, 4], b_v)
        in_x = cp.start(sa.at[i, 0], x_v)
        in_w = cp.choose(first, own_ref.at[:, three], other_ref.at[:, three], w_v.at[:, three])
        qkv_v[rows:, :] = jnp.zeros((keys - rows, 3 * width), BF)
        in_g.wait()
        scaled = gin_v[...].astype(F32) * vec_ref[2:3, :]
        e_v[...] = scaled.astype(BF)
        cp.store(e_v, ea.at[i])
        vg_v[3:4, :] = rows_sum(scaled)
        vg_v[6:8, :] = jnp.zeros((2, width), F32)
        in_p.wait()
        dc_v[...] = dot_nt(e_v[...], w_v[:, 3 * width :]).astype(BF)
        for copy in ins:
            copy.wait()
        in_pb.wait()
        factor = HD ** (-0.5)
        plain = head_masks(1.0)
        for j in range(heads // 2):
            cols = slice(j * 128, (j + 1) * 128)
            q = qkv_v[0:rows, j * 128 : (j + 1) * 128]
            k = qkv_v[:, width + j * 128 : width + (j + 1) * 128]
            u = qkv_v[:, 2 * width + j * 128 : 2 * width + (j + 1) * 128]
            dc = dc_v[:, cols]
            dq_t, dk_t, du_t = None, None, None
            for t in range(2):
                dc_t = dc * plain[t]
                p = pb_v[2 * j + t]
                dp = dot_nt(dc_t, u)
                pf = p.astype(F32)
                wp = pf * dp
                ds = wp - pf * jnp.sum(wp, -1, keepdims=True)
                dlog = (ds * factor).astype(BF)
                dl_v[2 * j + t] = dlog
                du = dot_tn(p, dc_t)
                dqp = dot(dlog, k * plain[t])
                dkp = dot_tn(dlog, q * plain[t])
                dq_t = dqp if dq_t is None else dq_t + dqp
                dk_t = dkp if dk_t is None else dk_t + dkp
                du_t = du if du_t is None else du_t + du
            dq_v[:, j * 128 : (j + 1) * 128] = dq_t.astype(BF)
            dq_v[:, width + j * 128 : width + (j + 1) * 128] = dk_t[0:rows].astype(BF)
            dq_v[:, 2 * width + j * 128 : 2 * width + (j + 1) * 128] = du_t[0:rows].astype(BF)
            vg_v[4:5, cols] = rows_sum(dq_t)
            vg_v[5:6, cols] = rows_sum(du_t)
        cp.store(dl_v, dl.at[i])
        cp.store(dq_v, dq.at[i])
        in_b.wait()
        vg_v[2:3, :] = rows_sum(gin_v[...].astype(F32) * b_v[...].astype(F32))
        in_x.wait()
        in_w.wait()
        da = dot_nt(dq_v[...], w_v[:, 0 : 3 * width])
        xhat, rstd = norm_stats(x_v[...].astype(F32))
        vg_v[0:1, :] = rows_sum(da * xhat)
        vg_v[1:2, :] = rows_sum(da)
        dx = norm_back(gin_v[...].astype(F32), da, xhat, rstd, vec_ref[0:1, :])
        dx_v[...] = dx.astype(BF)
        cp.store(dx_v, send)
        cp.store(dx_v, dx0.at[i])
        cp.store(vg_v, vga.at[i])
        cp.finish()


def weight_parts(s, refs_in, refs_out, scratch):
    flags, g_all, dh_all, a2, ef, a1, ctx, dq, ea = refs_in
    sent, own = refs_out
    l1, r1, l2, r2, l3, r3, out1, out2, out3, sems = scratch
    width = l1.shape[2]
    chunks, tall = out1.shape[0], out1.shape[1]
    part = tall // 2
    cp = Copies(sems)
    core = flags[1]
    first = core == 0
    cols = pl.ds(s * width, width)
    g_s, dh_s = g_all.at[:, :, cols], dh_all.at[:, :, cols]
    ins = [
        cp.choose(first, g_s, a2, l1),
        cp.choose(first, ef, dh_s, r1),
        cp.start(a1, l3) if s < 3 else cp.start(ctx, l3),
        cp.start(dq.at[:, :, cols], r3) if s < 3 else cp.start(ea, r3),
        cp.choose(first, a2, g_s, l2),
        cp.choose(first, dh_s, ef, r2),
    ]

    def product(left, right, out):
        rows = left.shape[0] * left.shape[1]
        value = dot_tn(left[...].reshape(rows, width), right[...].reshape(rows, width)).astype(BF)
        out[...] = value.reshape(chunks, tall, width)

    ins[0].wait()
    ins[1].wait()
    product(l1, r1, out1)
    cp.store(out1, sent.at[:, 0:tall])
    ins[2].wait()
    ins[3].wait()
    product(l3, r3, out3)
    mine, theirs = pl.multiple_of(core * part, part), pl.multiple_of((1 - core) * part, part)
    cp.store(out3.at[:, pl.ds(theirs, part)], sent.at[:, pl.ds(tall, part)])
    cp.store(out3.at[:, pl.ds(mine, part)], own.at[:, pl.ds(tall, part)])
    ins[4].wait()
    ins[5].wait()
    product(l2, r2, out2)
    cp.store(out2, own.at[:, 0:tall])
    cp.finish()


def place_sums(refs_in, refs_out, scratch):
    flags, a_up, a_down, b_up, b_down = refs_in
    gw, gd = refs_out
    gw_v, gd_v, sems = scratch
    blocks, tall, width = gd_v.shape
    low = flags[0] == 0
    cp = Copies(sems)
    for way, (a_ref, b_ref) in enumerate(((a_up, b_up), (a_down, b_down))):
        chunk = flags[1 + way]
        row = pl.multiple_of(chunk * tall, tall)
        for k in range(blocks // 2):
            s = way * (blocks // 2) + k
            a = a_ref[k].astype(F32)
            gw_v[s] = jnp.where(low, a, b_ref[k].astype(F32))
            gd_v[s] = jnp.where(low, 0.0, a)
            cp.store(gw_v.at[s], gw.at[pl.ds(row, tall), pl.ds(s * width, width)])
            cp.store(gd_v.at[s], gd.at[pl.ds(pl.multiple_of(s * width + row, tall), tall)])
    cp.finish()


def bias_fill(grid, tail, by_col, out):
    heads, rows, keys = out.shape
    patches = grid * grid
    wide = by_col.shape[2]
    lane = lax.broadcasted_iota(jnp.int32, (1, keys), 1)
    for h in range(heads):
        corner, upper, left = tail[h, 2], tail[h, 0], tail[h, 1]
        out[h, patches + 1 :, :] = jnp.where(
            lax.broadcasted_iota(jnp.int32, (rows - patches - 1, keys), 1) <= patches, 0.0, -1e30
        )
        out[h, 0:1, :] = jnp.where(lane == 0, corner, jnp.where(lane <= patches, upper, -1e30))
        block = by_col[h]
        for r in range(grid):
            turned = pltpu.roll(block, (1 - grid * (grid - 1 - r)) % wide, 1)[0:grid, 0:keys]
            turned = jnp.where(lane == 0, left, jnp.where(lane <= patches, turned, -1e30))
            out[h, 1 + r * grid : 1 + (r + 1) * grid, :] = turned


def run(body, i, name, ins, specs, state, shapes, extra, scratch, sems, flops, moved):
    fresh = state is None
    n_in, n_state, n_extra = len(ins), len(shapes), len(extra)
    given = 0 if fresh else n_state

    def kernel(*refs):
        refs_in = refs[:n_in]
        outs = refs[n_in + given : n_in + given + n_state]
        more = refs[n_in + given + n_state : n_in + given + n_state + n_extra]
        body(i, refs_in, outs, more, refs[n_in + given + n_state + n_extra :])

    made = pl.pallas_call(
        kernel,
        out_shape=tuple(shapes) + tuple(extra),
        in_specs=list(specs) + [ANY] * given,
        out_specs=tuple([ANY] * (n_state + n_extra)),
        scratch_shapes=[pltpu.VMEM(s.shape, s.dtype) for s in scratch] + [pltpu.SemaphoreType.DMA((sems,))],
        input_output_aliases={} if fresh else {n_in + k: k for k in range(n_state)},
        compiler_params=pltpu.CompilerParams(vmem_limit_bytes=56 * 2**20),
        cost_estimate=pl.CostEstimate(flops=flops, bytes_accessed=moved, transcendentals=0),
        name=name,
    )(*ins, *([] if fresh else state))
    return list(made[:n_state]), list(made[n_state:])


def sd(shape, dtype=BF):
    return jax.ShapeDtypeStruct(shape, dtype)


class Kernels:
    def __init__(self, images, rows, keys, width, hidden, heads):
        self.n, self.r, self.k, self.d, self.f, self.h = images, rows, keys, width, hidden, heads

    def att_f(self, i, flags, x, vec, own, other, bias, state):
        n, r, k, d, h = self.n, self.r, self.k, self.d, self.h
        shapes = [sd((n, 5, r, d)), sd((n, r, d)), sd((n, r, d)), sd((n, r, d)), sd((n, h, r, k))]
        scratch = [sd((r, d)), sd((d, 4 * d)), sd((h, r, k), F32), sd((r, d)), sd((k, 3 * d)), sd((h, r, k)), sd((r, d)), sd((r, d)), sd((r, d))]
        return run(attend_forward, i, "attend_forward", [flags, x, vec, own, other, bias], [SMEM, ANY, VMEM, ANY, ANY, ANY], state, shapes, [], scratch, 16, 2 * r * d * 4 * d + 4 * h * r * k * HD, 12000000)

    def feed_state(self):
        n, r, d, f = self.n, self.r, self.d, self.f
        wide, narrow = sd((n, r, f)), sd((n, r, d))
        return [wide, wide, narrow, narrow, wide, narrow, narrow, narrow, sd((n, 8, d), F32)]

    def ff_f(self, i, flags, y1, vec, own, other, own_d, other_d, state):
        r, d, f = self.r, self.d, self.f
        scratch = [sd((r, d)), sd((d, f)), sd((f, d)), sd((r, d)), sd((r, f)), sd((r, f)), sd((r, d)), sd((r, d))]
        return run(feed_forward, i, "feed_forward", [flags, y1, vec, own, other, own_d, other_d], [SMEM, ANY, VMEM, ANY, ANY, ANY, ANY], state, self.feed_state(), [sd((r, d))], scratch, 16, 4 * r * d * f, 12000000)

    def ff_b(self, i, flags, g, vec, own, other, own_d, other_d, y1, state):
        r, d, f = self.r, self.d, self.f
        scratch = [sd((r, d)), sd((r, d)), sd((d, f)), sd((f, d)), sd((r, f)), sd((r, d)), sd((r, d)), sd((r, f)), sd((r, d)), sd((8, d), F32)]
        return run(feed_backward, i, "feed_backward", [flags, g, vec, own, other, own_d, other_d, y1], [SMEM, ANY, VMEM] + [ANY] * 5, state, self.feed_state(), [], scratch, 16, 4 * r * d * f, 12000000)

    def att_b(self, i, flags, dx1, vec, own, other, sa, pb, state):
        n, r, k, d, h = self.n, self.r, self.k, self.d, self.h
        shapes = [sd((n, r, d)), sd((n, r, 3 * d)), sd((n, h, r, k)), sd((n, r, d)), sd((n, 8, d), F32)]
        scratch = [sd((r, d)), sd((r, d)), sd((d, 4 * d)), sd((h, r, k)), sd((r, d)), sd((r, d)), sd((k, 3 * d)), sd((r, d)), sd((r, 3 * d)), sd((h, r, k)), sd((r, d)), sd((8, d), F32)]
        return run(attend_backward, i, "attend_backward", [flags, dx1, vec, own, other, sa, pb], [SMEM, ANY, VMEM] + [ANY] * 4, state, shapes, [sd((r, d))], scratch, 20, 2 * r * d * 4 * d + 8 * h * r * k * HD, 12000000)


    def parts(self, s, flags, g_all, dh_all, a2, ef, a1, ctx, dq, ea, chunks):
        n, r, d = self.n, self.r, self.d
        tall = d // chunks
        block = sd((n, r, d))
        out = sd((chunks, tall, d))
        scratch = [block] * 6 + [out] * 3
        made = pl.pallas_call(
            lambda *refs: weight_parts(s, refs[:9], refs[9:11], refs[11:]),
            out_shape=(sd((chunks, tall + tall // 2, d)), sd((chunks, tall + tall // 2, d))),
            in_specs=[SMEM] + [ANY] * 8,
            out_specs=(ANY, ANY),
            scratch_shapes=[pltpu.VMEM(v.shape, v.dtype) for v in scratch] + [pltpu.SemaphoreType.DMA((10,))],
            compiler_params=pltpu.CompilerParams(vmem_limit_bytes=56 * 2**20),
            cost_estimate=pl.CostEstimate(flops=6 * n * r * d * d, bytes_accessed=11000000, transcendentals=0),
            name="weight_parts",
        )(flags, g_all, dh_all, a2, ef, a1, ctx, dq, ea)
        return made

    def place(self, flags, a_up, a_down, b_up, b_down, state):
        d, f = self.d, self.f
        blocks, tall = 2 * a_up.shape[0], a_up.shape[1]
        given = 0 if state is None else 2
        scratch = [pltpu.VMEM((blocks, tall, d), F32)] * 2 + [pltpu.SemaphoreType.DMA((2 * blocks,))]
        return pl.pallas_call(
            lambda *refs: place_sums(refs[:5], refs[5 + given : 7 + given], refs[7 + given :]),
            out_shape=(sd((d, f), F32), sd((f, d), F32)),
            in_specs=[SMEM] + [VMEM] * 4 + [ANY] * given,
            out_specs=(ANY, ANY),
            scratch_shapes=scratch,
            input_output_aliases={5: 0, 6: 1} if given else {},
            compiler_params=pltpu.CompilerParams(vmem_limit_bytes=24 * 2**20),
            cost_estimate=pl.CostEstimate(flops=0, bytes_accessed=4000000, transcendentals=0),
            name="place_sums",
        )(flags, a_up, a_down, b_up, b_down, *(() if state is None else state))

    def bias(self, table, grid):
        heads = table.shape[0]
        side = 2 * grid - 1
        flipped = table[:, : side * side].reshape(heads, side, side)[:, ::-1, ::-1]
        by_col = jnp.stack([flipped[:, :, grid - 1 - c : side - c] for c in range(grid)], 1)
        by_col = by_col.reshape(heads, grid, side * grid)
        wide = -(-(side * grid) // 128) * 128
        by_col = jnp.pad(by_col, ((0, 0), (0, -grid % 8), (0, wide - side * grid)))
        return pl.pallas_call(
            partial(bias_fill, grid),
            out_shape=sd((heads, self.r, self.k), F32),
            in_specs=[SMEM, VMEM],
            out_specs=VMEM,
            compiler_params=pltpu.CompilerParams(vmem_limit_bytes=24 * 2**20),
            name="bias_fill",
        )(table[:, side * side :], by_col)


def swap(block, pairs):
    return lax.ppermute(block, "section", pairs)


def table_sums(grad, grid):
    heads = grad.shape[0]
    side, patches = 2 * grid - 1, grid * grid
    block = grad[:, 1:, 1:]
    wide = side * grid
    by_col = 0.0
    for r in range(grid):
        at = grid * (grid - 1 - r)
        by_col = by_col + jnp.pad(block[:, r * grid : (r + 1) * grid], ((0, 0), (0, 0), (at, wide - at - patches)))
    by_col = by_col.reshape(heads, grid, side, grid)
    flipped = 0.0
    for c in range(grid):
        at = grid - 1 - c
        flipped = flipped + jnp.pad(by_col[:, c], ((0, 0), (0, 0), (at, side - at - grid)))
    inner = flipped[:, ::-1, ::-1].reshape(heads, side * side)
    tail = jnp.stack([jnp.sum(grad[:, 0, 1:], 1), jnp.sum(grad[:, 1:, 0], 1), grad[:, 0, 0]], 1)
    return jnp.concatenate([inner, tail], 1)


def ring_order(n):
    return list(range(0, n, 2)) + list(range(n - 1, 0, -2))


def doubled_sum(block, axis):
    n = lax.axis_size(axis)
    step = 1
    while step < n:
        block = block + lax.ppermute(block, axis, [(k, k ^ step) for k in range(n)])
        step *= 2
    return block


def weight_sums(kern, blocks, low, core, both, to_low, to_high, sections):
    axis = "dp"
    n = lax.axis_size(axis)
    ringed = n == RING
    chunks = RING
    order = ring_order(n)
    flags = jnp.stack([core, core])
    locals_ = []
    for s in range(4):
        sent, own = kern.parts(s, flags, *blocks, chunks)
        locals_.append((own, swap(sent, both)))
    tall = kern.d // chunks
    if not ringed:
        sums = [lax.psum((own.astype(F32) + got.astype(F32)).astype(BF), axis) for own, got in locals_]
        first = jnp.stack([v[:, :tall] for v in sums])
        second = jnp.stack([v[:, tall:] for v in sums])
        got_first, got_second = swap(first, to_high), swap(second, to_low)
        kept = jnp.concatenate([second, got_second], 2)
        columns = jnp.where(low, kept, got_first).transpose(1, 2, 0, 3)
        grad_weight = columns.reshape(kern.d, kern.f).astype(F32)
        grad_down = jnp.where(low, 0.0, first.astype(F32)).reshape(kern.f, kern.d)
        return grad_weight, grad_down

    place = [0] * n
    for k, device in enumerate(order):
        place[device] = k
    at = jnp.array(place, jnp.int32)[lax.axis_index(axis)]
    ways = (1, 1, -1, -1)
    route = {w: [(order[k], order[(k + w) % n]) for k in range(n)] for w in (1, -1)}
    upper = {
        w: [(s * n + p, s * n + q) for s in range(1, sections, 2) for p, q in route[w]] for w in (1, -1)
    }

    def local(s, chunk):
        own, got = locals_[s]
        index = chunk % n
        left = lax.dynamic_index_in_dim(own, index, 0, False).astype(F32)
        return left + lax.dynamic_index_in_dim(got, index, 0, False).astype(F32)

    held = [local(s, at).astype(BF) for s in range(4)]
    for k in range(n - 1):
        for s in range(4):
            got = lax.ppermute(held[s], axis, route[ways[s]])
            held[s] = (got.astype(F32) + local(s, at - ways[s] * (k + 1))).astype(BF)
    first = jnp.stack([v[:tall] for v in held])
    second = jnp.stack([v[tall:] for v in held])
    got_first, got_second = swap(first, to_high), swap(second, to_low)
    kept = jnp.where(low, jnp.concatenate([second, got_second], 1), first)
    a = {1: kept[:2], -1: kept[2:]}
    b = {1: got_first[:2], -1: got_first[2:]}
    state = None
    for k in range(n):
        index = jnp.stack([core, (at + 1 - k) % n, (at - 1 + k) % n])
        state = kern.place(index, a[1], a[-1], b[1], b[-1], state)
        if k < n - 1:
            a = {w: lax.ppermute(a[w], axis, route[w]) for w in (1, -1)}
            b = {w: lax.ppermute(b[w], ("section", axis), upper[w]) for w in (1, -1)}
    return state


def on_device(embeds, mask, cotangent, section_weight, down_weight, section_vectors, rel_table):
    sections = lax.axis_size("section")
    now = lax.axis_index("section")
    core, stage = now % 2, now // 2
    images, length, width = embeds.shape
    half = images // 2
    hidden = section_weight.shape[2]
    heads = rel_table.shape[1]
    rows, keys = -(-length // 16) * 16, -(-length // 128) * 128
    grid = math.isqrt(length - 1)
    both = [(s, s ^ 1) for s in range(sections)]
    to_low = [(s, s - 1) for s in range(1, sections, 2)]
    to_high = [(s, s + 1) for s in range(0, sections, 2)]
    onward = [(s, s + 2) for s in range(sections - 2)]
    back = [(s + 2, s) for s in range(sections - 2)]
    low = core == 0

    own_w, own_d, own_v, own_t = section_weight[0], down_weight[0], section_vectors[0], rel_table[0]
    other_v = swap(own_v, both)
    table = jnp.where(low, own_t, swap(own_t, to_high))
    other_w = swap(own_w, both)
    other_d = swap(own_d, to_low)
    vec_a, vec_f = jnp.where(low, own_v, other_v), jnp.where(low, other_v, own_v)

    def mine_of(block):
        return lax.dynamic_slice_in_dim(block, core * half, half, 0)

    cover = mine_of(mask)[:, :, None] == 1
    start = jnp.where(cover, vec_a[6].astype(BF), mine_of(embeds))
    pad = ((0, 0), (0, rows - length), (0, 0))
    start = jnp.pad(start, pad)
    upstream = jnp.pad(mine_of(cotangent), pad)

    kern = Kernels(half, rows, keys, width, hidden, heads)
    bias = kern.bias(table, grid)
    flags_a = jnp.stack([(stage == 0).astype(jnp.int32), core])
    flags_b = jnp.stack([(stage == 1).astype(jnp.int32), core])
    att, feed = None, None

    def forward(i, flags, x):
        nonlocal att, feed
        att, _ = kern.att_f(i, flags, x, vec_a, own_w, other_w, bias, att)
        feed, (send,) = kern.ff_f(i, flags, att[3], vec_f, own_w, other_w, own_d, other_d, feed)
        return send

    arrived = [swap(forward(i, flags_a, start), onward) for i in range(half)]
    for i in range(half):
        forward(i, flags_b, arrived[i])

    grads = None

    def backward(i, flags, g):
        nonlocal feed, grads
        feed, _ = kern.ff_b(i, flags, g, vec_f, own_w, other_w, own_d, other_d, att[3], feed)
        grads, (send,) = kern.att_b(i, flags, feed[7], vec_a, own_w, other_w, att[0], att[4], grads)
        return send

    returned = [swap(backward(i, flags_b, upstream), back) for i in range(half)]
    for i in range(half):
        backward(i, flags_a, returned[i])

    sa, a1, ctx, y1, pb = att
    g_all, dh_all, a2, ef, gp, b2, y2, dx1, vgf = feed
    ea, dq, dl, dx0, vga = grads
    grad_weight, grad_down = weight_sums(
        kern, (g_all, dh_all, a2, ef, a1, ctx, dq, ea), low, core, both, to_low, to_high, sections
    )

    rows_a = jnp.sum(vga, 0)
    token = jnp.sum(jnp.where(cover, dx0[:, :length].astype(F32), 0.0), (0, 1))
    rows_a = rows_a.at[6].add(jnp.where(stage == 0, token, 0.0))
    rows_f = jnp.sum(vgf, 0)
    row_terms = jnp.where(low, rows_a, rows_f) + swap(jnp.where(low, rows_f, rows_a), both)
    scores = jnp.sum(dl[:, :, :length, :length].astype(F32), 0)
    sums = table_sums(scores, grid) * (HD ** 0.5)
    sums = jnp.where(low, sums + swap(sums, to_low), 0.0)
    grad_rows, grad_table = doubled_sum(row_terms, "dp"), doubled_sum(sums, "dp")

    def gather_images(a_part, f_part):
        mine, theirs = jnp.where(low, a_part, f_part), jnp.where(low, f_part, a_part)
        got = swap(theirs, both)
        return jnp.concatenate([jnp.where(low, mine, got), jnp.where(low, got, mine)], 0)[:, :length]

    activations = gather_images(y1, y2)
    input_grads = gather_images(dx0, dx1).astype(F32)
    hide = (mask[:, :, None] == 1) & (now == 0)
    input_grads = jnp.where(hide, 0.0, input_grads)
    return (
        activations[None],
        input_grads[None],
        grad_weight[None],
        grad_down[None],
        grad_rows[None],
        grad_table[None],
    )


def solution(mesh):
    placed = (
        P("dp", None, None),
        P("dp", None),
        P("dp", None, None),
        P("section", None, None),
        P("section", None, None),
        P("section", None, None),
        P("section", None, None),
    )
    return jax.shard_map(
        on_device,
        mesh=mesh,
        in_specs=placed,
        out_specs=(
            P("section", "dp", None, None),
            P("section", "dp", None, None),
            P("section", None, None),
            P("section", None, None),
            P("section", None, None),
            P("section", None, None),
        ),
        check_vma=False,
    )
```

```python
import math
from functools import partial

import jax
import jax.numpy as jnp
from jax import lax
from jax.experimental import pallas as pl
from jax.experimental.pallas import tpu as pltpu
from jax.sharding import PartitionSpec as P

EPS = 1e-06
F32 = jnp.float32
BF = jnp.bfloat16
HD = 64
RING = 8
ANY = pl.BlockSpec(memory_space=pl.ANY)
VMEM = pl.BlockSpec(memory_space=pltpu.VMEM)
SMEM = pl.BlockSpec(memory_space=pltpu.SMEM)


def dot(left, right):
    return jnp.dot(left, right, preferred_element_type=F32)


def dot_nt(left, right):
    return lax.dot_general(left, right, (((1,), (1,)), ((), ())), preferred_element_type=F32)


def dot_tn(left, right):
    return lax.dot_general(left, right, (((0,), (0,)), ((), ())), preferred_element_type=F32)


def norm_stats(x):
    center = x - jnp.mean(x, -1, keepdims=True)
    rstd = lax.rsqrt(jnp.mean(center * center, -1, keepdims=True) + EPS)
    return center * rstd, rstd


def norm_back(g, da, xhat, rstd, gain):
    w = da * gain
    return g + rstd * (w - jnp.mean(w, -1, keepdims=True) - xhat * jnp.mean(w * xhat, -1, keepdims=True))


def rows_sum(v):
    return jnp.sum(v, 0, keepdims=True)


def gelu_parts(h):
    z = jnp.abs(h) * 0.7071067811865476
    t = 1.0 / (1.0 + 0.3275911 * z)
    gauss = jnp.exp(-0.5 * h * h)
    poly = t * (0.127414796 + t * (-0.142248368 + t * (0.7107068705 + t * (-0.7265760135 + t * 0.5307027145))))
    tail = poly * gauss
    phi = jnp.where(h >= 0.0, 1.0 - tail, tail)
    return h * phi, phi + h * (gauss * 0.3989422804014327)


class Copies:
    def __init__(self, sems):
        self.sems, self.used, self.out = sems, 0, []

    def start(self, src, dst):
        copy = pltpu.make_async_copy(src, dst, self.sems.at[self.used])
        self.used += 1
        copy.start()
        return copy

    def choose(self, first, a, b, dst):
        sem = self.sems.at[self.used]
        self.used += 1

        @pl.when(first)
        def _():
            pltpu.make_async_copy(a, dst, sem).start()

        @pl.when(jnp.logical_not(first))
        def _():
            pltpu.make_async_copy(b, dst, sem).start()

        return pltpu.make_async_copy(a, dst, sem)

    def store(self, src, dst):
        self.out.append(self.start(src, dst))

    def finish(self):
        for copy in self.out:
            copy.wait()


def image_of(ref, i):
    return ref.at[i] if len(ref.shape) == 3 else ref


def head_masks(scale):
    lane = lax.broadcasted_iota(jnp.int32, (1, 2 * HD), 1)
    low = jnp.where(lane < HD, scale, 0.0).astype(BF)
    high = jnp.where(lane < HD, 0.0, scale).astype(BF)
    return low, high


def forward_image(i, refs_in, refs_state, refs_extra, scratch):
    flags, x_ref, vec_ref, vecf_ref, wa_ref, w1_ref, w2_ref, bias_ref = refs_in
    x_ref = image_of(x_ref, i)
    sa, a1, ctx, y1, pb, g_all, a2, gp, b2, y2 = refs_state
    (send,) = refs_extra
    x_v, qkv_v, pb_v, b_v, y_v, gp_v, bf_v, yf_v, sems = scratch
    rows, width = x_v.shape
    heads, keys = pb_v.shape[0], pb_v.shape[2]
    hidden = gp_v.shape[1]
    a_v, c_v, g_v, af_v = a1.at[i], ctx.at[i], g_all.at[i], a2.at[i]

    @pl.when(flags[0] == 1)
    def _():
        cp = Copies(sems)
        x_v[...] = x_ref[...]
        cp.store(x_v, sa.at[i, 0])
        xhat, rstd = norm_stats(x_v[...].astype(F32))
        a_v[...] = (xhat * vec_ref[0:1, :] + vec_ref[1:2, :]).astype(BF)
        qkv_v[rows:, :] = jnp.zeros((keys - rows, 3 * width), BF)
        a = a_v[...]
        block = 256
        for j in range(3 * width // block):
            cols = slice(j * block, (j + 1) * block)
            part = dot(a, wa_ref[:, cols])
            kind, at = divmod(j * block, width)
            if kind == 0:
                part = part + vec_ref[4:5, at : at + block]
            if kind == 2:
                part = part + vec_ref[5:6, at : at + block]
            qkv_v[0:rows, cols] = part.astype(BF)
        for kind in range(3):
            cp.store(qkv_v.at[0:rows, pl.ds(kind * width, width)], sa.at[i, 1 + kind])
        scaled = head_masks(HD ** (-0.5))
        plain = head_masks(1.0)
        for j in range(heads // 2):
            q = qkv_v[0:rows, j * 128 : (j + 1) * 128]
            k = qkv_v[:, width + j * 128 : width + (j + 1) * 128]
            u = qkv_v[:, 2 * width + j * 128 : 2 * width + (j + 1) * 128]
            total = None
            for t in range(2):
                s = dot_nt(q * scaled[t], k) + bias_ref[2 * j + t]
                e = jnp.exp(s - jnp.max(s, -1, keepdims=True))
                p = (e * (1.0 / jnp.sum(e, -1, keepdims=True))).astype(BF)
                pb_v[2 * j + t] = p
                part = dot(p, u * plain[t])
                total = part if total is None else total + part
            c_v[:, j * 128 : (j + 1) * 128] = total.astype(BF)
        cp.store(pb_v, pb.at[i])
        b = dot(c_v[...], wa_ref[:, 3 * width :]) + vec_ref[3:4, :]
        b_v[...] = b.astype(BF)
        cp.store(b_v, sa.at[i, 4])
        y_v[...] = (x_v[...].astype(F32) + vec_ref[2:3, :] * b).astype(BF)
        cp.store(y_v, y1.at[i])

        xhat, rstd = norm_stats(y_v[...].astype(F32))
        af_v[...] = (xhat * vecf_ref[0:1, :] + vecf_ref[1:2, :]).astype(BF)
        a = af_v[...]
        for j in range(hidden // block):
            row, at = divmod(j * block, width)
            cols = slice(j * block, (j + 1) * block)
            h = dot(a, w1_ref[:, cols]) + vecf_ref[4 + row : 5 + row, at : at + block]
            value, slope = gelu_parts(h)
            g_v[:, cols] = value.astype(BF)
            gp_v[:, cols] = slope.astype(BF)
        cp.store(gp_v, gp.at[i])
        b = dot(g_v[...], w2_ref[...]) + vecf_ref[3:4, :]
        yf_v[...] = (y_v[...].astype(F32) + vecf_ref[2:3, :] * b).astype(BF)
        send[...] = yf_v[...]
        cp.store(yf_v, y2.at[i])
        bf_v[...] = b.astype(BF)
        cp.store(bf_v, b2.at[i])
        cp.finish()


def backward_image(i, refs_in, refs_state, refs_extra, scratch):
    flags, g_ref, vec_ref, vecf_ref, wa_ref, w1_ref, w2_ref, sa, pb, y1, gp, b2 = refs_in
    g_ref = image_of(g_ref, i)
    dh_all, ef, dx1, vgf, ea, dq, dl, dx0, vga = refs_state
    (send,) = refs_extra
    (gin_v, gp_v, bf_v, xf_v, qkv_v, pb_v, b_v, x_v, dx_v, vgf_v, dc_v, dl_v, dx0_v, vg_v, sems) = scratch
    e_v, dh_v, ea_v, dq_v = ef.at[i], dh_all.at[i], ea.at[i], dq.at[i]
    rows, width = x_v.shape
    heads, keys = pb_v.shape[0], pb_v.shape[2]
    hidden = dh_v.shape[1]

    @pl.when(flags[0] == 1)
    def _():
        cp = Copies(sems)
        in_gp = cp.start(gp.at[i], gp_v)
        in_bf = cp.start(b2.at[i], bf_v)
        in_xf = cp.start(y1.at[i], xf_v)
        ins = [cp.start(sa.at[i, 1 + kind], qkv_v.at[0:rows, pl.ds(kind * width, width)]) for kind in range(3)]
        in_pb = cp.start(pb.at[i], pb_v)
        in_b = cp.start(sa.at[i, 4], b_v)
        in_x = cp.start(sa.at[i, 0], x_v)
        qkv_v[rows:, :] = jnp.zeros((keys - rows, 3 * width), BF)
        vg_v[6:8, :] = jnp.zeros((2, width), F32)
        gin_v[...] = g_ref[...]
        scaled = gin_v[...].astype(F32) * vecf_ref[2:3, :]
        e_v[...] = scaled.astype(BF)
        vgf_v[3:4, :] = rows_sum(scaled)
        in_gp.wait()
        e = e_v[...]
        block = 256
        for j in range(hidden // block):
            row, at = divmod(j * block, width)
            cols = slice(j * block, (j + 1) * block)
            dh = dot_nt(e, w2_ref[cols, :]) * gp_v[:, cols].astype(F32)
            dh_v[:, cols] = dh.astype(BF)
            vgf_v[4 + row : 5 + row, at : at + block] = rows_sum(dh)
        in_bf.wait()
        in_xf.wait()
        vgf_v[2:3, :] = rows_sum(gin_v[...].astype(F32) * bf_v[...].astype(F32))
        da = dot_nt(dh_v[...], w1_ref[...])
        xhat, rstd = norm_stats(xf_v[...].astype(F32))
        vgf_v[0:1, :] = rows_sum(da * xhat)
        vgf_v[1:2, :] = rows_sum(da)
        cp.store(vgf_v, vgf.at[i])
        dx_v[...] = norm_back(gin_v[...].astype(F32), da, xhat, rstd, vecf_ref[0:1, :]).astype(BF)
        cp.store(dx_v, dx1.at[i])

        scaled = dx_v[...].astype(F32) * vec_ref[2:3, :]
        ea_v[...] = scaled.astype(BF)
        vg_v[3:4, :] = rows_sum(scaled)
        dc_v[...] = dot_nt(ea_v[...], wa_ref[:, 3 * width :]).astype(BF)
        for copy in ins:
            copy.wait()
        in_pb.wait()
        factor = HD ** (-0.5)
        plain = head_masks(1.0)
        for j in range(heads // 2):
            cols = slice(j * 128, (j + 1) * 128)
            q = qkv_v[0:rows, j * 128 : (j + 1) * 128]
            k = qkv_v[:, width + j * 128 : width + (j + 1) * 128]
            u = qkv_v[:, 2 * width + j * 128 : 2 * width + (j + 1) * 128]
            dc = dc_v[:, cols]
            dq_t, dk_t, du_t = None, None, None
            for t in range(2):
                dc_t = dc * plain[t]
                p = pb_v[2 * j + t]
                dp = dot_nt(dc_t, u)
                pf = p.astype(F32)
                wp = pf * dp
                ds = wp - pf * jnp.sum(wp, -1, keepdims=True)
                dlog = (ds * factor).astype(BF)
                dl_v[2 * j + t] = dlog
                du = dot_tn(p, dc_t)
                dqp = dot(dlog, k * plain[t])
                dkp = dot_tn(dlog, q * plain[t])
                dq_t = dqp if dq_t is None else dq_t + dqp
                dk_t = dkp if dk_t is None else dk_t + dkp
                du_t = du if du_t is None else du_t + du
            dq_v[:, j * 128 : (j + 1) * 128] = dq_t.astype(BF)
            dq_v[:, width + j * 128 : width + (j + 1) * 128] = dk_t[0:rows].astype(BF)
            dq_v[:, 2 * width + j * 128 : 2 * width + (j + 1) * 128] = du_t[0:rows].astype(BF)
            vg_v[4:5, cols] = rows_sum(dq_t)
            vg_v[5:6, cols] = rows_sum(du_t)
        cp.store(dl_v, dl.at[i])
        in_b.wait()
        in_x.wait()
        vg_v[2:3, :] = rows_sum(dx_v[...].astype(F32) * b_v[...].astype(F32))
        da = dot_nt(dq_v[...], wa_ref[:, 0 : 3 * width])
        xhat, rstd = norm_stats(x_v[...].astype(F32))
        dx0_v[...] = norm_back(dx_v[...].astype(F32), da, xhat, rstd, vec_ref[0:1, :]).astype(BF)
        send[...] = dx0_v[...]
        cp.store(dx0_v, dx0.at[i])
        vg_v[0:1, :] = rows_sum(da * xhat)
        vg_v[1:2, :] = rows_sum(da)
        cp.store(vg_v, vga.at[i])
        cp.finish()


def load_weights(refs_in, refs_out, scratch):
    flags, own_ref, other_ref, own_d, other_d = refs_in
    wa_ref, w1_ref, w2_ref = refs_out
    first = flags[1] == 0
    cp = Copies(scratch[0])
    for copy in (
        cp.choose(first, own_ref, other_ref, wa_ref),
        cp.choose(first, other_ref, own_ref, w1_ref),
        cp.choose(first, other_d, own_d, w2_ref),
    ):
        copy.wait()


def weight_parts(ups, refs_in, sents, owns, scratch):
    flags, g_all, dh_all, a2, ef, a1, ctx, dq, ea = refs_in
    sent_v, own_v, sems = scratch
    width = a2.shape[2]
    chunks, tall = own_v.shape[1], a2.shape[2] // own_v.shape[1]
    part = tall // 2
    cp = Copies(sems)
    core, at = flags[0], flags[1]
    low = core == 0
    cuts = 2
    block, group = width // cuts, chunks // cuts
    rows = a2.shape[0] * a2.shape[1]

    def product(left, right, first_col, second_col, put):
        rhs = right[:, :, second_col : second_col + width].reshape(rows, width)

        def one(k, none):
            start = pl.multiple_of(first_col + k * block, 128)
            lhs = left[:, :, pl.ds(start, block)].reshape(rows, block)
            put(pl.ds(k * group, group), dot_tn(lhs, rhs).astype(BF).reshape(group, tall, width))
            return none

        lax.fori_loop(0, cuts, one, 0)

    def share(turn, s, which, target):
        def put(group, value):
            target[turn % 2, group, 0:tall] = value

        @pl.when(core == which)
        def _():
            product(a2, dh_all, 0, s * width, put)

        @pl.when(core != which)
        def _():
            product(g_all, ef, s * width, 0, put)

    def put_both(turn, group, value):
        sent_v[turn % 2, group, tall:] = jnp.where(low, value[:, part:], value[:, :part])
        own_v[turn % 2, group, tall:] = jnp.where(low, value[:, :part], value[:, part:])

    def store(turn, s, source, target):
        for chunk in range(chunks):
            slot = (at - chunk if ups[s] else chunk - at) & (chunks - 1)
            cp.store(source.at[turn % 2, chunk], target.at[slot])

    for turn, s in enumerate((0, 2, 1, 3)):
        if turn >= 2:
            for copy in cp.out[: 2 * chunks]:
                copy.wait()
            cp.out = cp.out[2 * chunks :]
        if s < 3:
            product(a1, dq, 0, s * width, partial(put_both, turn))
        else:
            product(ctx, ea, 0, 0, partial(put_both, turn))
        share(turn, s, 1, sent_v)
        store(turn, s, sent_v, sents[s])
        share(turn, s, 0, own_v)
        store(turn, s, own_v, owns[s])
    cp.finish()


def table_fold(grid, dl, by_col, edge, dl_v, sems):
    images, heads, rows, keys = dl.shape
    patches = grid * grid
    wide = by_col.shape[2]
    copies = []
    for h in range(heads):
        copy = pltpu.make_async_copy(dl.at[:, h], dl_v.at[h], sems.at[h])
        copy.start()
        copies.append(copy)
    lane = lax.broadcasted_iota(jnp.int32, (1, keys), 1)
    inner = lane > 0
    for h in range(heads):
        copies[h].wait()
        total = dl_v[h, 0].astype(F32)
        for i in range(1, images):
            total = total + dl_v[h, i].astype(F32)
        edge[h, 0:1, :] = total[0:1]
        edge[h, 1:2, :] = jnp.broadcast_to(jnp.sum(total[1 : 1 + patches, 0:1], 0, keepdims=True), (1, keys))
        block = jnp.where(inner, total, 0.0)
        sums = None
        for r in range(grid):
            part = block[1 + r * grid : 1 + (r + 1) * grid]
            part = jnp.concatenate([part, jnp.zeros((grid, wide - keys), F32)], 1)
            part = pltpu.roll(part, (grid * (grid - 1 - r) - 1) % wide, 1)
            sums = part if sums is None else sums + part
        by_col[h] = sums


def place_sums(refs_in, refs_out, scratch):
    flags, a_up, a_down, b_up, b_down = refs_in
    gw, gd = refs_out
    gw_v, gd_v, sems = scratch
    blocks, tall, width = gd_v.shape
    low = flags[0] == 0
    cp = Copies(sems)
    for way, (a_ref, b_ref) in enumerate(((a_up, b_up), (a_down, b_down))):
        chunk = flags[1 + way]
        row = pl.multiple_of(chunk * tall, tall)
        for k in range(blocks // 2):
            s = way * (blocks // 2) + k
            a = a_ref[k].astype(F32)
            gw_v[s] = jnp.where(low, a, b_ref[k].astype(F32))
            gd_v[s] = jnp.where(low, 0.0, a)
            cp.store(gw_v.at[s], gw.at[pl.ds(row, tall), pl.ds(s * width, width)])
            cp.store(gd_v.at[s], gd.at[pl.ds(pl.multiple_of(s * width + row, tall), tall)])
    cp.finish()


def bias_fill(grid, tail, by_col, out):
    heads, rows, keys = out.shape
    patches = grid * grid
    wide = by_col.shape[2]
    lane = lax.broadcasted_iota(jnp.int32, (1, keys), 1)
    for h in range(heads):
        corner, upper, left = tail[h, 2], tail[h, 0], tail[h, 1]
        out[h, patches + 1 :, :] = jnp.where(
            lax.broadcasted_iota(jnp.int32, (rows - patches - 1, keys), 1) <= patches, 0.0, -1e30
        )
        out[h, 0:1, :] = jnp.where(lane == 0, corner, jnp.where(lane <= patches, upper, -1e30))
        block = by_col[h]
        for r in range(grid):
            turned = pltpu.roll(block, (1 - grid * (grid - 1 - r)) % wide, 1)[0:grid, 0:keys]
            turned = jnp.where(lane == 0, left, jnp.where(lane <= patches, turned, -1e30))
            out[h, 1 + r * grid : 1 + (r + 1) * grid, :] = turned


def run(body, i, name, ins, specs, state, shapes, extra, scratch, sems, flops, moved):
    fresh = state is None
    ins = [in_hbm(v) if spec is ANY else v for v, spec in zip(ins, specs)]
    n_in, n_state, n_extra = len(ins), len(shapes), len(extra)
    given = 0 if fresh else n_state

    def kernel(*refs):
        refs_in = refs[:n_in]
        outs = refs[n_in + given : n_in + given + n_state]
        more = refs[n_in + given + n_state : n_in + given + n_state + n_extra]
        body(i, refs_in, outs, more, refs[n_in + given + n_state + n_extra :])

    made = pl.pallas_call(
        kernel,
        out_shape=tuple(shapes) + tuple(extra),
        in_specs=list(specs) + [ANY] * given,
        out_specs=tuple(VMEM if in_vmem(v) else ANY for v in [*shapes, *extra]),
        scratch_shapes=[pltpu.VMEM(s.shape, s.dtype) for s in scratch] + [pltpu.SemaphoreType.DMA((sems,))],
        input_output_aliases={} if fresh else {n_in + k: k for k in range(n_state)},
        compiler_params=pltpu.CompilerParams(vmem_limit_bytes=16 * 2**20),
        cost_estimate=pl.CostEstimate(flops=flops, bytes_accessed=moved, transcendentals=0),
        name=name,
    )(*ins, *([] if fresh else state))
    return list(made[:n_state]), list(made[n_state:])


def in_vmem(shape):
    return shape.memory_space == pltpu.VMEM


def pinned(block):
    return pltpu.with_memory_space_constraint(block, pltpu.VMEM)


def in_hbm(block):
    return pltpu.with_memory_space_constraint(block, pltpu.HBM)


def far(shape, dtype=BF):
    return pltpu.HBM(shape, dtype)


def sd(shape, dtype=BF):
    return jax.ShapeDtypeStruct(shape, dtype)


class Kernels:
    def __init__(self, images, rows, keys, width, hidden, heads):
        self.n, self.r, self.k, self.d, self.f, self.h = images, rows, keys, width, hidden, heads

    def weights(self, flags, own, other, own_d, other_d):
        d, f = self.d, self.f
        return pl.pallas_call(
            lambda *refs: load_weights(refs[:5], refs[5:8], refs[8:]),
            out_shape=(pltpu.VMEM((d, f), BF), pltpu.VMEM((d, f), BF), pltpu.VMEM((f, d), BF)),
            in_specs=[SMEM] + [ANY] * 4,
            out_specs=(VMEM, VMEM, VMEM),
            scratch_shapes=[pltpu.SemaphoreType.DMA((3,))],
            compiler_params=pltpu.CompilerParams(vmem_limit_bytes=4 * 2**20),
            name="load_weights",
        )(flags, *[in_hbm(v) for v in (own, other, own_d, other_d)])

    def forward(self, i, flags, x, vec_a, vec_f, weights, bias, state):
        n, r, k, d, f, h = self.n, self.r, self.k, self.d, self.f, self.h
        narrow, wide = far((n, r, d)), far((n, r, f))
        held = pltpu.VMEM((n, r, d), BF)
        shapes = [far((n, 5, r, d)), held, held, narrow, far((n, h, r, k)), pltpu.VMEM((n, r, f), BF), held, wide, narrow, narrow]
        row, high = sd((r, d)), sd((r, f))
        scratch = [row, sd((k, 3 * d)), sd((h, r, k)), row, row, high, row, row]
        ins = [flags, pinned(x), vec_a, vec_f, *[pinned(w) for w in weights], pinned(bias)]
        flops = 2 * r * d * 4 * d + 4 * h * r * k * HD + 4 * r * d * f
        return run(forward_image, i, "forward_image", ins, [SMEM] + [VMEM] * 7, state, shapes, [pltpu.VMEM((r, d), BF)], scratch, 20, flops, 12000000)

    def backward(self, i, flags, g, vec_a, vec_f, weights, kept, state):
        n, r, k, d, f, h = self.n, self.r, self.k, self.d, self.f, self.h
        narrow = far((n, r, d))
        sums = far((n, 8, d), F32)
        held = pltpu.VMEM((n, r, d), BF)
        shapes = [pltpu.VMEM((n, r, f), BF), held, narrow, sums, held, pltpu.VMEM((n, r, 3 * d), BF), far((n, h, r, k)), narrow, sums]
        row, high, pairs, vec = sd((r, d)), sd((r, f)), sd((h, r, k)), sd((8, d), F32)
        scratch = [row, high, row, row, sd((k, 3 * d)), pairs, row, row, row, vec, row, pairs, row, vec]
        sa, a1, ctx, y1, pb, g_all, a2, gp, b2, y2 = kept
        ins = [flags, pinned(g), vec_a, vec_f, *[pinned(w) for w in weights], sa, pb, y1, gp, b2]
        flops = 2 * r * d * 4 * d + 8 * h * r * k * HD + 4 * r * d * f
        return run(backward_image, i, "backward_image", ins, [SMEM] + [VMEM] * 6 + [ANY] * 5, state, shapes, [pltpu.VMEM((r, d), BF)], scratch, 24, flops, 12000000)

    def parts(self, ups, flags, blocks, chunks):
        d = self.d
        tall = d // chunks
        both = (chunks, tall + tall // 2, d)
        made = pl.pallas_call(
            lambda *refs: weight_parts(ups, refs[:9], refs[9:13], refs[13:17], refs[17:]),
            out_shape=(far(both),) * 8,
            in_specs=[SMEM] + [VMEM] * 8,
            out_specs=(ANY,) * 8,
            scratch_shapes=[pltpu.VMEM((2, *both), BF)] * 2 + [pltpu.SemaphoreType.DMA((8 * chunks,))],
            compiler_params=pltpu.CompilerParams(vmem_limit_bytes=28 * 2**20),
            cost_estimate=pl.CostEstimate(flops=1, bytes_accessed=1, transcendentals=0),
            name="weight_parts",
        )(flags, *[pinned(v) for v in blocks])
        return made[:4], made[4:]

    def table(self, dl, grid):
        n, heads, rows, keys = dl.shape
        side = 2 * grid - 1
        wide = -(-(side * grid) // 128) * 128
        by_col, edge = pl.pallas_call(
            partial(table_fold, grid),
            out_shape=(sd((heads, grid, wide), F32), sd((heads, 2, keys), F32)),
            in_specs=[ANY],
            out_specs=(VMEM, VMEM),
            scratch_shapes=[pltpu.VMEM((heads, n, rows, keys), BF), pltpu.SemaphoreType.DMA((heads,))],
            compiler_params=pltpu.CompilerParams(vmem_limit_bytes=24 * 2**20),
            name="table_fold",
        )(in_hbm(dl))
        by_col = by_col[:, :, : side * grid].reshape(heads, grid, side, grid)
        flipped = 0.0
        for c in range(grid):
            at = grid - 1 - c
            flipped = flipped + jnp.pad(by_col[:, c], ((0, 0), (0, 0), (at, side - at - grid)))
        inner = flipped[:, ::-1, ::-1].reshape(heads, side * side)
        patches = grid * grid
        tail = jnp.stack([jnp.sum(edge[:, 0, 1 : 1 + patches], 1), edge[:, 1, 0], edge[:, 0, 0]], 1)
        return jnp.concatenate([inner, tail], 1)

    def place(self, flags, a_up, a_down, b_up, b_down, state):
        d, f = self.d, self.f
        blocks, tall = 2 * a_up.shape[0], a_up.shape[1]
        given = 0 if state is None else 2
        scratch = [pltpu.VMEM((blocks, tall, d), F32)] * 2 + [pltpu.SemaphoreType.DMA((2 * blocks,))]
        return pl.pallas_call(
            lambda *refs: place_sums(refs[:5], refs[5 + given : 7 + given], refs[7 + given :]),
            out_shape=(sd((d, f), F32), sd((f, d), F32)),
            in_specs=[SMEM] + [VMEM] * 4 + [ANY] * given,
            out_specs=(ANY, ANY),
            scratch_shapes=scratch,
            input_output_aliases={5: 0, 6: 1} if given else {},
            compiler_params=pltpu.CompilerParams(vmem_limit_bytes=24 * 2**20),
            cost_estimate=pl.CostEstimate(flops=0, bytes_accessed=1, transcendentals=0),
            name="place_sums",
        )(flags, a_up, a_down, b_up, b_down, *(() if state is None else state))

    def bias(self, table, grid):
        heads = table.shape[0]
        side = 2 * grid - 1
        flipped = table[:, : side * side].reshape(heads, side, side)[:, ::-1, ::-1]
        by_col = jnp.stack([flipped[:, :, grid - 1 - c : side - c] for c in range(grid)], 1)
        by_col = by_col.reshape(heads, grid, side * grid)
        wide = -(-(side * grid) // 128) * 128
        by_col = jnp.pad(by_col, ((0, 0), (0, -grid % 8), (0, wide - side * grid)))
        return pl.pallas_call(
            partial(bias_fill, grid),
            out_shape=pltpu.VMEM((heads, self.r, self.k), F32),
            in_specs=[SMEM, VMEM],
            out_specs=VMEM,
            compiler_params=pltpu.CompilerParams(vmem_limit_bytes=24 * 2**20),
            name="bias_fill",
        )(table[:, side * side :], by_col)


def swap(block, pairs):
    return lax.ppermute(block, "section", pairs)


def ring_order(n):
    return list(range(0, n, 2)) + list(range(n - 1, 0, -2))


def doubled_sum(block, axis):
    n = lax.axis_size(axis)
    step = 1
    while step < n:
        block = block + lax.ppermute(block, axis, [(k, k ^ step) for k in range(n)])
        step *= 2
    return block


def weight_shares(kern, blocks, core, both):
    n = lax.axis_size("dp")
    ringed = n == RING
    place = [0] * n
    for k, device in enumerate(ring_order(n)):
        place[device] = k
    at = jnp.array(place, jnp.int32)[lax.axis_index("dp")] if ringed else jnp.int32(0)
    flags = jnp.stack([core, at])
    sents, owns = kern.parts([ringed, ringed, False, False], flags, blocks, RING)
    got = {s: swap(sents[s], both) for s in (0, 2, 1, 3)}
    return [(owns[s], got[s]) for s in range(4)], at


def weight_sums(kern, locals_, at, small, low, core, to_low, to_high, sections):
    axis = "dp"
    n = lax.axis_size(axis)
    ringed = n == RING
    chunks = RING
    order = ring_order(n)
    tall = kern.d // chunks
    if not ringed:
        sums = [lax.psum((own.astype(F32) + got.astype(F32)).astype(BF), axis) for own, got in locals_]
        first = jnp.stack([v[:, :tall] for v in sums])
        second = jnp.stack([v[:, tall:] for v in sums])
        got_first, got_second = swap(first, to_high), swap(second, to_low)
        kept = jnp.concatenate([second, got_second], 2)
        columns = jnp.where(low, kept, got_first).transpose(1, 2, 0, 3)
        grad_weight = columns.reshape(kern.d, kern.f).astype(F32)
        grad_down = jnp.where(low, 0.0, first.astype(F32)).reshape(kern.f, kern.d)
        return grad_weight, grad_down, doubled_sum(small, axis)

    route = {w: [(order[k], order[(k + w) % n]) for k in range(n)] for w in (1, -1)}
    upper = {
        w: [(s * n + p, s * n + q) for s in range(1, sections, 2) for p, q in route[w]] for w in (1, -1)
    }
    held = [None] * 4
    for k in range(n):
        for s in (0, 2, 1, 3):
            own, other = locals_[s]
            total = own[k].astype(F32) + other[k].astype(F32)
            if k > 0:
                total = total + lax.ppermute(held[s], axis, route[1 if s < 2 else -1]).astype(F32)
            held[s] = total.astype(BF)
    first = jnp.stack([v[:tall] for v in held])
    second = jnp.stack([v[tall:] for v in held])
    got_first, got_second = swap(first, to_high), swap(second, to_low)
    kept = jnp.where(low, jnp.concatenate([second, got_second], 1), first)
    a = {1: kept[:2], -1: kept[2:]}
    b = {1: got_first[:2], -1: got_first[2:]}
    state = None
    step, other = 1, None
    for k in range(n):
        index = jnp.stack([core, (at + 1 - k) & (n - 1), (at - 1 + k) & (n - 1)])
        if k < n - 1:
            next_a = {w: lax.ppermute(a[w], axis, route[w]) for w in (1, -1)}
            next_b = {w: lax.ppermute(b[w], ("section", axis), upper[w]) for w in (1, -1)}
        state = kern.place(index, a[1], a[-1], b[1], b[-1], state)
        if k < n - 1:
            if k % 2 == 0 and step < n:
                other = lax.ppermute(small, axis, [(d, d ^ step) for d in range(n)])
                step *= 2
            if k % 2 == 1 and other is not None:
                small, other = small + other, None
            a, b, state, small = lax.optimization_barrier((next_a, next_b, state, small))
    return (*state, small)


def on_device(embeds, mask, cotangent, section_weight, down_weight, section_vectors, rel_table):
    sections = lax.axis_size("section")
    now = lax.axis_index("section")
    core, stage = now % 2, now // 2
    images, length, width = embeds.shape
    half = images // 2
    hidden = section_weight.shape[2]
    heads = rel_table.shape[1]
    rows, keys = -(-length // 16) * 16, -(-length // 128) * 128
    grid = math.isqrt(length - 1)
    both = [(s, s ^ 1) for s in range(sections)]
    to_low = [(s, s - 1) for s in range(1, sections, 2)]
    to_high = [(s, s + 1) for s in range(0, sections, 2)]
    onward = [(s, s + 2) for s in range(sections - 2)]
    back = [(s + 2, s) for s in range(sections - 2)]
    low = core == 0

    own_w, own_d, own_v, own_t = section_weight[0], down_weight[0], section_vectors[0], rel_table[0]
    other_v = swap(own_v, both)
    table = jnp.where(low, own_t, swap(own_t, to_high))
    other_w = swap(own_w, both)
    other_d = swap(own_d, to_low)
    vec_a, vec_f = jnp.where(low, own_v, other_v), jnp.where(low, other_v, own_v)

    def mine_of(block):
        return lax.dynamic_slice_in_dim(block, core * half, half, 0)

    cover = mine_of(mask)[:, :, None] == 1
    start = jnp.where(cover, vec_a[6].astype(BF), mine_of(embeds))
    pad = ((0, 0), (0, rows - length), (0, 0))
    start = jnp.pad(start, pad)
    upstream = jnp.pad(mine_of(cotangent), pad)

    kern = Kernels(half, rows, keys, width, hidden, heads)
    bias = kern.bias(table, grid)
    flags_a = jnp.stack([(stage == 0).astype(jnp.int32), core])
    flags_b = jnp.stack([(stage == 1).astype(jnp.int32), core])
    weights = kern.weights(flags_a, own_w, other_w, own_d, other_d)
    kept, grads = None, None

    def forward(i, flags, x):
        nonlocal kept
        kept, (send,) = kern.forward(i, flags, x, vec_a, vec_f, weights, bias, kept)
        return send

    arrived = [swap(forward(i, flags_a, start), onward) for i in range(half)]
    for i in range(half):
        forward(i, flags_b, arrived[i])

    def backward(i, flags, g):
        nonlocal grads
        grads, (send,) = kern.backward(i, flags, g, vec_a, vec_f, weights, kept, grads)
        return send

    returned = [swap(backward(i, flags_b, upstream), back) for i in range(half)]
    for i in range(half):
        backward(i, flags_a, returned[i])

    sa, a1, ctx, y1, pb, g_all, a2, gp, b2, y2 = kept
    dh_all, ef, dx1, vgf, ea, dq, dl, dx0, vga = grads
    shares, at = weight_shares(kern, (g_all, dh_all, a2, ef, a1, ctx, dq, ea), core, both)
    own_parts, vga, vgf, dl, dx0, dx1 = lax.optimization_barrier(([v[0] for v in shares], vga, vgf, dl, dx0, dx1))
    shares = [(own, other) for own, (_, other) in zip(own_parts, shares)]
    rows_a = jnp.sum(vga, 0)
    token = jnp.sum(jnp.where(cover, dx0[:, :length].astype(F32), 0.0), (0, 1))
    rows_a = rows_a.at[6].add(jnp.where(stage == 0, token, 0.0))
    rows_f = jnp.sum(vgf, 0)
    row_terms = jnp.where(low, rows_a, rows_f) + swap(jnp.where(low, rows_f, rows_a), both)
    sums = kern.table(dl, grid) * (HD ** 0.5)
    sums = jnp.where(low, sums + swap(sums, to_low), 0.0)
    entries = sums.shape[1]
    wide = -(-entries // 128) * 128
    small = jnp.concatenate([row_terms.reshape(-1), jnp.pad(sums, ((0, 0), (0, wide - entries))).reshape(-1)])
    grad_weight, grad_down, small = weight_sums(
        kern,
        shares,
        at,
        small.reshape(-1, 128),
        low, core, to_low, to_high, sections
    )

    small = small.reshape(-1)
    grad_rows = small[: 8 * width].reshape(8, width)
    grad_table = small[8 * width :].reshape(heads, wide)[:, :entries]

    def gather_images(a_part, f_part):
        mine, theirs = jnp.where(low, a_part, f_part), jnp.where(low, f_part, a_part)
        got = swap(theirs, both)
        return jnp.concatenate([jnp.where(low, mine, got), jnp.where(low, got, mine)], 0)[:, :length]

    activations = gather_images(y1, y2)
    input_grads = gather_images(dx0, dx1).astype(F32)
    hide = (mask[:, :, None] == 1) & (now == 0)
    input_grads = jnp.where(hide, 0.0, input_grads)
    return (
        activations[None],
        input_grads[None],
        grad_weight[None],
        grad_down[None],
        grad_rows[None],
        grad_table[None],
    )


def solution(mesh):
    placed = (
        P("dp", None, None),
        P("dp", None),
        P("dp", None, None),
        P("section", None, None),
        P("section", None, None),
        P("section", None, None),
        P("section", None, None),
    )
    return jax.shard_map(
        on_device,
        mesh=mesh,
        in_specs=placed,
        out_specs=(
            P("section", "dp", None, None),
            P("section", "dp", None, None),
            P("section", None, None),
            P("section", None, None),
            P("section", None, None),
            P("section", None, None),
        ),
        check_vma=False,
    )
```

```python
import math
from functools import partial

import jax
import jax.numpy as jnp
from jax import lax
from jax.experimental import pallas as pl
from jax.experimental.pallas import tpu as pltpu
from jax.sharding import PartitionSpec as P

EPS = 1e-06
F32 = jnp.float32
BF = jnp.bfloat16
HD = 64
RING = 8
ANY = pl.BlockSpec(memory_space=pl.ANY)
VMEM = pl.BlockSpec(memory_space=pltpu.VMEM)
SMEM = pl.BlockSpec(memory_space=pltpu.SMEM)


def dot(left, right):
    return jnp.dot(left, right, preferred_element_type=F32)


def dot_nt(left, right):
    return lax.dot_general(left, right, (((1,), (1,)), ((), ())), preferred_element_type=F32)


def dot_tn(left, right):
    return lax.dot_general(left, right, (((0,), (0,)), ((), ())), preferred_element_type=F32)


def norm_stats(x):
    center = x - jnp.mean(x, -1, keepdims=True)
    rstd = lax.rsqrt(jnp.mean(center * center, -1, keepdims=True) + EPS)
    return center * rstd, rstd


def norm_back(g, da, xhat, rstd, gain):
    w = da * gain
    return g + rstd * (w - jnp.mean(w, -1, keepdims=True) - xhat * jnp.mean(w * xhat, -1, keepdims=True))


def rows_sum(v):
    return jnp.sum(v, 0, keepdims=True)


def gelu_parts(h):
    phi = 0.5 + 0.5 * lax.erf(h * 0.7071067811865476)
    return h * phi, phi + h * (jnp.exp(-0.5 * h * h) * 0.3989422804014327)


class Copies:
    def __init__(self, sems):
        self.sems, self.used, self.out = sems, 0, []

    def start(self, src, dst):
        copy = pltpu.make_async_copy(src, dst, self.sems.at[self.used])
        self.used += 1
        copy.start()
        return copy

    def choose(self, first, a, b, dst):
        return self.either(first, (a, dst), (b, dst))

    def either(self, first, one, two):
        sem = self.sems.at[self.used]
        self.used += 1

        @pl.when(first)
        def _():
            pltpu.make_async_copy(*one, sem).start()

        @pl.when(jnp.logical_not(first))
        def _():
            pltpu.make_async_copy(*two, sem).start()

        return pltpu.make_async_copy(*one, sem)

    def store(self, src, dst):
        self.out.append(self.start(src, dst))

    def store_choose(self, first, src, a, b):
        self.out.append(self.either(first, (src, a), (src, b)))

    def finish(self):
        for copy in self.out:
            copy.wait()


def image_of(ref, i):
    return ref.at[i] if len(ref.shape) == 3 else ref


def head_masks(scale):
    lane = lax.broadcasted_iota(jnp.int32, (1, 2 * HD), 1)
    low = jnp.where(lane < HD, scale, 0.0).astype(BF)
    high = jnp.where(lane < HD, 0.0, scale).astype(BF)
    return low, high


def forward_image(i, refs_in, refs_state, refs_extra, scratch):
    flags, x_ref, vec_ref, vecf_ref, bias_ref = refs_in[:5]
    loading = len(refs_in) > 8
    wa_ref, w1_ref, w2_ref = refs_extra[1:] if loading else refs_in[5:]
    x_ref = image_of(x_ref, i)
    sa, a1, ctx, y1, pb, g_all, a2, gp, b2, keep, give = refs_state
    core_first = flags[1] == 0
    send = refs_extra[0]
    x_v, qkv_v, pb_v, b_v, y_v, gp_v, bf_v, yf_v, sems = scratch
    rows, width = x_v.shape
    heads, keys = pb_v.shape[0], pb_v.shape[2]
    hidden = gp_v.shape[1]
    a_v, c_v, g_v, af_v = a1.at[i], ctx.at[i], g_all.at[i], a2.at[i]
    cp = Copies(sems)
    ready = []
    if loading:
        own_ref, other_ref, own_d, other_d = refs_in[5:]
        first = flags[1] == 0
        ready = [
            cp.choose(first, own_ref, other_ref, wa_ref),
            cp.choose(first, other_ref, own_ref, w1_ref),
            cp.choose(first, other_d, own_d, w2_ref),
        ]

        @pl.when(flags[0] == 0)
        def _():
            for copy in ready:
                copy.wait()

    @pl.when(flags[0] == 1)
    def _():
        x_v[...] = x_ref[...]
        cp.store(x_v, sa.at[i, 0])
        xhat, rstd = norm_stats(x_v[...].astype(F32))
        a_v[...] = (xhat * vec_ref[0:1, :] + vec_ref[1:2, :]).astype(BF)
        qkv_v[rows:, :] = jnp.zeros((keys - rows, 3 * width), BF)
        a = a_v[...]
        block = 256
        if loading:
            ready[0].wait()
        for j in range(3 * width // block):
            cols = slice(j * block, (j + 1) * block)
            part = dot(a, wa_ref[:, cols])
            kind, at = divmod(j * block, width)
            if kind == 0:
                part = part + vec_ref[4:5, at : at + block]
            if kind == 2:
                part = part + vec_ref[5:6, at : at + block]
            qkv_v[0:rows, cols] = part.astype(BF)
        for kind in range(3):
            cp.store(qkv_v.at[0:rows, pl.ds(kind * width, width)], sa.at[i, 1 + kind])
        scaled = head_masks(HD ** (-0.5))
        plain = head_masks(1.0)
        for j in range(heads // 2):
            q = qkv_v[0:rows, j * 128 : (j + 1) * 128]
            k = qkv_v[:, width + j * 128 : width + (j + 1) * 128]
            u = qkv_v[:, 2 * width + j * 128 : 2 * width + (j + 1) * 128]
            soft = []
            for t in range(2):
                s = dot_nt(q * scaled[t], k) + bias_ref[2 * j + t]
                e = jnp.exp(s - jnp.max(s, -1, keepdims=True))
                p = (e * (1.0 / jnp.sum(e, -1, keepdims=True))).astype(BF)
                pb_v[2 * j + t] = p
                soft.append(p)
            total = dot(jnp.concatenate(soft, 1), jnp.concatenate([u * plain[0], u * plain[1]], 0))
            c_v[:, j * 128 : (j + 1) * 128] = total.astype(BF)
        cp.store(pb_v, pb.at[i])
        b = dot(c_v[...], wa_ref[:, 3 * width :]) + vec_ref[3:4, :]
        b_v[...] = b.astype(BF)
        cp.store(b_v, sa.at[i, 4])
        y_v[...] = (x_v[...].astype(F32) + vec_ref[2:3, :] * b).astype(BF)
        cp.store(y_v, y1.at[i])
        cp.store_choose(core_first, y_v, keep.at[i], give.at[i])

        xhat, rstd = norm_stats(y_v[...].astype(F32))
        af_v[...] = (xhat * vecf_ref[0:1, :] + vecf_ref[1:2, :]).astype(BF)
        a = af_v[...]
        if loading:
            ready[1].wait()
        for j in range(hidden // block):
            row, at = divmod(j * block, width)
            cols = slice(j * block, (j + 1) * block)
            h = dot(a, w1_ref[:, cols]) + vecf_ref[4 + row : 5 + row, at : at + block]
            value, slope = gelu_parts(h)
            g_v[:, cols] = value.astype(BF)
            gp_v[:, cols] = slope.astype(BF)
        cp.store(gp_v, gp.at[i])
        if loading:
            ready[2].wait()
        b = dot(g_v[...], w2_ref[...]) + vecf_ref[3:4, :]
        yf_v[...] = (y_v[...].astype(F32) + vecf_ref[2:3, :] * b).astype(BF)
        send[...] = yf_v[...]
        cp.store_choose(core_first, yf_v, give.at[i], keep.at[i])
        bf_v[...] = b.astype(BF)
        cp.store(bf_v, b2.at[i])
        cp.finish()


def backward_image(i, refs_in, refs_state, refs_extra, scratch):
    flags, g_ref, vec_ref, vecf_ref, wa_ref, w1_ref, w2_ref, hide_ref, sa, pb, y1, gp, b2 = refs_in
    g_ref = image_of(g_ref, i)
    dh_all, ef, keep, vgf, ea, dq, dl, give, vga = refs_state
    core_first = flags[1] == 0
    (send,) = refs_extra
    (gin_v, gp_v, bf_v, xf_v, qkv_v, pb_v, b_v, x_v, dx_v, vgf_v, dc_v, dl_v, dx0_v, vg_v, sems) = scratch
    e_v, dh_v, ea_v, dq_v = ef.at[i], dh_all.at[i], ea.at[i], dq.at[i]
    rows, width = x_v.shape
    heads, keys = pb_v.shape[0], pb_v.shape[2]
    hidden = dh_v.shape[1]

    @pl.when(flags[0] == 1)
    def _():
        cp = Copies(sems)
        in_gp = cp.start(gp.at[i], gp_v)
        in_bf = cp.start(b2.at[i], bf_v)
        in_xf = cp.start(y1.at[i], xf_v)
        ins = [cp.start(sa.at[i, 1 + kind], qkv_v.at[0:rows, pl.ds(kind * width, width)]) for kind in range(3)]
        in_pb = cp.start(pb.at[i], pb_v)
        in_b = cp.start(sa.at[i, 4], b_v)
        in_x = cp.start(sa.at[i, 0], x_v)
        qkv_v[rows:, :] = jnp.zeros((keys - rows, 3 * width), BF)
        vg_v[7:8, :] = jnp.zeros((1, width), F32)
        gin_v[...] = g_ref[...]
        scaled = gin_v[...].astype(F32) * vecf_ref[2:3, :]
        e_v[...] = scaled.astype(BF)
        vgf_v[3:4, :] = rows_sum(scaled)
        in_gp.wait()
        e = e_v[...]
        block = 256
        for j in range(hidden // block):
            row, at = divmod(j * block, width)
            cols = slice(j * block, (j + 1) * block)
            dh = dot_nt(e, w2_ref[cols, :]) * gp_v[:, cols].astype(F32)
            dh_v[:, cols] = dh.astype(BF)
            vgf_v[4 + row : 5 + row, at : at + block] = rows_sum(dh)
        in_bf.wait()
        in_xf.wait()
        vgf_v[2:3, :] = rows_sum(gin_v[...].astype(F32) * bf_v[...].astype(F32))
        da = dot_nt(dh_v[...], w1_ref[...])
        xhat, rstd = norm_stats(xf_v[...].astype(F32))
        vgf_v[0:1, :] = rows_sum(da * xhat)
        vgf_v[1:2, :] = rows_sum(da)
        cp.store(vgf_v, vgf.at[i])
        dx_v[...] = norm_back(gin_v[...].astype(F32), da, xhat, rstd, vecf_ref[0:1, :]).astype(BF)
        cp.store_choose(core_first, dx_v, give.at[i], keep.at[i])

        scaled = dx_v[...].astype(F32) * vec_ref[2:3, :]
        ea_v[...] = scaled.astype(BF)
        vg_v[3:4, :] = rows_sum(scaled)
        dc_v[...] = dot_nt(ea_v[...], wa_ref[:, 3 * width :]).astype(BF)
        for copy in ins:
            copy.wait()
        in_pb.wait()
        factor = HD ** (-0.5)
        plain = head_masks(1.0)
        for j in range(heads // 2):
            cols = slice(j * 128, (j + 1) * 128)
            q = qkv_v[0:rows, j * 128 : (j + 1) * 128]
            k = qkv_v[:, width + j * 128 : width + (j + 1) * 128]
            u = qkv_v[:, 2 * width + j * 128 : 2 * width + (j + 1) * 128]
            dc = dc_v[:, cols]
            dcs = jnp.concatenate([dc * plain[0], dc * plain[1]], 0)
            probs = pb_v[2 * j : 2 * j + 2].reshape(2 * rows, keys)
            dp = dot_nt(dcs, u)
            pf = probs.astype(F32)
            wp = pf * dp
            ds = wp - pf * jnp.sum(wp, -1, keepdims=True)
            dlog = (ds * factor).astype(BF)
            dl_v[2 * j : 2 * j + 2] = dlog.reshape(2, rows, keys)
            du_t = dot_tn(probs, dcs)
            dq_t = dot(
                jnp.concatenate([dlog[:rows], dlog[rows:]], 1),
                jnp.concatenate([k * plain[0], k * plain[1]], 0),
            )
            dk_t = dot_tn(dlog, jnp.concatenate([q * plain[0], q * plain[1]], 0))
            dq_v[:, j * 128 : (j + 1) * 128] = dq_t.astype(BF)
            dq_v[:, width + j * 128 : width + (j + 1) * 128] = dk_t[0:rows].astype(BF)
            dq_v[:, 2 * width + j * 128 : 2 * width + (j + 1) * 128] = du_t[0:rows].astype(BF)
            vg_v[4:5, cols] = rows_sum(dq_t)
            vg_v[5:6, cols] = rows_sum(du_t)
        cp.store(dl_v, dl.at[i])
        in_b.wait()
        in_x.wait()
        vg_v[2:3, :] = rows_sum(dx_v[...].astype(F32) * b_v[...].astype(F32))
        da = dot_nt(dq_v[...], wa_ref[:, 0 : 3 * width])
        xhat, rstd = norm_stats(x_v[...].astype(F32))
        dx = norm_back(dx_v[...].astype(F32), da, xhat, rstd, vec_ref[0:1, :])
        send[...] = dx.astype(BF)
        hidden_rows = hide_ref[i] > 0.0
        dx0_v[...] = jnp.where(hidden_rows, 0.0, dx).astype(BF)
        vg_v[6:7, :] = rows_sum(jnp.where(hidden_rows, dx, 0.0))
        cp.store_choose(core_first, dx0_v, keep.at[i], give.at[i])
        vg_v[0:1, :] = rows_sum(da * xhat)
        vg_v[1:2, :] = rows_sum(da)
        cp.store(vg_v, vga.at[i])
        cp.finish()


def weight_parts(ups, refs_in, sents, owns, scratch):
    flags, g_all, dh_all, a2, ef, a1, ctx, dq, ea = refs_in
    sent_v, own_v, sems = scratch
    width = a2.shape[2]
    chunks, tall = own_v.shape[1], a2.shape[2] // own_v.shape[1]
    part = tall // 2
    cp = Copies(sems)
    core, at = flags[0], flags[1]
    low = core == 0
    cuts = 1
    block, group = width // cuts, chunks // cuts
    rows = a2.shape[0] * a2.shape[1]

    def product(left, right, first_col, second_col, put):
        rhs = right[:, :, second_col : second_col + width].reshape(rows, width)

        for k in range(cuts):
            start = first_col + k * block
            lhs = left[:, :, start : start + block].reshape(rows, block)
            put(pl.ds(k * group, group), dot_tn(lhs, rhs).astype(BF).reshape(group, tall, width))

    def share(turn, s, which, target):
        def put(group, value):
            target[turn % 2, group, 0:tall] = value

        @pl.when(core == which)
        def _():
            product(a2, dh_all, 0, s * width, put)

        @pl.when(core != which)
        def _():
            product(g_all, ef, s * width, 0, put)

    def put_both(turn, group, value):
        sent_v[turn % 2, group, tall:] = jnp.where(low, value[:, part:], value[:, :part])
        own_v[turn % 2, group, tall:] = jnp.where(low, value[:, :part], value[:, part:])

    def store(turn, s, source, target):
        for chunk in range(chunks):
            slot = (at - chunk if ups[s] else chunk - at) & (chunks - 1)
            cp.store(source.at[turn % 2, chunk], target.at[slot])

    for turn, s in enumerate((0, 2, 1, 3)):
        if turn >= 2:
            for copy in cp.out[: 2 * chunks]:
                copy.wait()
            cp.out = cp.out[2 * chunks :]
        if s < 3:
            product(a1, dq, 0, s * width, partial(put_both, turn))
        else:
            product(ctx, ea, 0, 0, partial(put_both, turn))
        share(turn, s, 1, sent_v)
        store(turn, s, sent_v, sents[s])
        share(turn, s, 0, own_v)
        store(turn, s, own_v, owns[s])
    cp.finish()


def join_images(refs_in, out, scratch):
    flags, keep_ref, got_ref = refs_in
    all_v, sems = scratch
    half = keep_ref.shape[0]
    cp = Copies(sems)
    low = flags[0] == 0
    copies = [
        cp.choose(low, keep_ref, got_ref, all_v.at[0:half]),
        cp.choose(low, got_ref, keep_ref, all_v.at[half : 2 * half]),
    ]
    for copy in copies:
        copy.wait()
    length, size = out.shape[0], 16
    for at in range(0, length, size):
        n = min(size, length - at)
        block = jnp.swapaxes(all_v[:, at : at + size, :].astype(F32), 0, 1)
        out[at : at + n] = block[:n].astype(out.dtype)


def table_fold(grid, dl, out, dl_v, sems):
    images, heads, rows, keys = dl.shape
    patches, side = grid * grid, 2 * grid - 1
    wide = -(-(side * grid) // 128) * 128 + 128
    copies = []
    for h in range(heads):
        copy = pltpu.make_async_copy(dl.at[:, h], dl_v.at[h], sems.at[h])
        copy.start()
        copies.append(copy)
    lane = lax.broadcasted_iota(jnp.int32, (1, keys), 1)
    narrow = lax.broadcasted_iota(jnp.int32, (1, 256), 1)
    last = lax.broadcasted_iota(jnp.int32, (1, out.shape[1]), 1)
    for h in range(heads):
        copies[h].wait()
        total = dl_v[h, 0].astype(F32)
        for i in range(1, images):
            total = total + dl_v[h, i].astype(F32)
        block = jnp.where(lane > 0, total, 0.0)
        sums = None
        for r in range(grid):
            part = block[1 + r * grid : 1 + (r + 1) * grid]
            part = jnp.concatenate([part, jnp.zeros((grid, wide - keys), F32)], 1)
            part = pltpu.roll(part, (grid * (grid - 1 - r) - 1) % wide, 1)
            sums = part if sums is None else sums + part
        tiles = [jnp.zeros((grid, 128), F32) for _ in range(out.shape[1] // 128 + 1)]
        for a in range(side):
            at, to = a * side // 128, a * grid // 128 * 128
            start = a * grid - to
            inside = (narrow >= start) & (narrow < start + grid)
            window = jnp.where(inside, sums[:, to : to + 256], 0.0)
            turned = pltpu.roll(window, (a * side + grid - 1 - at * 128 - start) % 256, 1)
            tiles[at] = tiles[at] + turned[:, :128]
            tiles[at + 1] = tiles[at + 1] + turned[:, 128:]
        slid = jnp.concatenate(tiles[:-1], 1)
        flat = slid[0:1]
        for c in range(1, grid):
            flat = flat + pltpu.roll(slid[c : c + 1], out.shape[1] - c, 1)
        upper = jnp.sum(jnp.where(lane > 0, total[0:1], 0.0), 1, keepdims=True)
        left = jnp.sum(total[1 : 1 + patches, 0:1], 0, keepdims=True)
        for k, value in enumerate((upper, left, total[0:1, 0:1])):
            flat = jnp.where(last == side * side + k, value, flat)
        out[h : h + 1, :] = flat


def place_sums(refs_in, refs_out, scratch):
    flags, a_up, a_down, b_up, b_down = refs_in
    gw, gd = refs_out
    gw_v, gd_v, sems = scratch
    blocks, tall, width = gd_v.shape
    low = flags[0] == 0
    cp = Copies(sems)
    for way, (a_ref, b_ref) in enumerate(((a_up, b_up), (a_down, b_down))):
        chunk = flags[1 + way]
        row = pl.multiple_of(chunk * tall, tall)
        for k in range(blocks // 2):
            s = way * (blocks // 2) + k
            a = a_ref[k].astype(F32)
            gw_v[s] = jnp.where(low, a, b_ref[k].astype(F32))
            gd_v[s] = jnp.where(low, 0.0, a)
            cp.store(gw_v.at[s], gw.at[pl.ds(row, tall), pl.ds(s * width, width)])
            cp.store(gd_v.at[s], gd.at[pl.ds(pl.multiple_of(s * width + row, tall), tall)])
    cp.finish()


def bias_fill(grid, tail, flipped, out):
    heads, rows, keys = out.shape
    patches, side = grid * grid, 2 * grid - 1
    wide = -(-(side * grid) // 128) * 128
    high = -(-grid // 8) * 8
    lane = lax.broadcasted_iota(jnp.int32, (1, keys), 1)
    narrow = lax.broadcasted_iota(jnp.int32, (1, 128), 1)
    for h in range(heads):
        corner, upper, left = tail[h, 2], tail[h, 0], tail[h, 1]
        out[h, patches + 1 :, :] = jnp.where(
            lax.broadcasted_iota(jnp.int32, (rows - patches - 1, keys), 1) <= patches, 0.0, -1e30
        )
        out[h, 0:1, :] = jnp.where(lane == 0, corner, jnp.where(lane <= patches, upper, -1e30))
        slid = jnp.broadcast_to(flipped[h : h + 1, :], (high, flipped.shape[1]))
        slid = pltpu.roll(slid, 0, 1, stride=1, stride_axis=0)
        tiles = [jnp.zeros((high, 128), F32) for _ in range(wide // 128)]
        for a in range(side):
            at, to = a * side // 128 * 128, a * grid // 128
            start = a * grid - to * 128
            turned = pltpu.roll(slid[:, at : at + 256], (start - (a * side + grid - 1 - at)) % 256, 1)
            for k in range(2):
                if 128 * k < start + grid and start < 128 * (k + 1):
                    inside = (narrow >= start - 128 * k) & (narrow < start + grid - 128 * k)
                    tiles[to + k] = jnp.where(inside, turned[:, 128 * k : 128 * (k + 1)], tiles[to + k])
        block = jnp.concatenate(tiles, 1)
        for r in range(grid):
            turned = pltpu.roll(block, (1 - grid * (grid - 1 - r)) % wide, 1)[0:grid, 0:keys]
            turned = jnp.where(lane == 0, left, jnp.where(lane <= patches, turned, -1e30))
            out[h, 1 + r * grid : 1 + (r + 1) * grid, :] = turned


def run(body, i, name, ins, specs, state, shapes, extra, scratch, sems, flops, moved):
    fresh = state is None
    ins = [in_hbm(v) if spec is ANY else v for v, spec in zip(ins, specs)]
    n_in, n_state, n_extra = len(ins), len(shapes), len(extra)
    given = 0 if fresh else n_state

    def kernel(*refs):
        refs_in = refs[:n_in]
        outs = refs[n_in + given : n_in + given + n_state]
        more = refs[n_in + given + n_state : n_in + given + n_state + n_extra]
        body(i, refs_in, outs, more, refs[n_in + given + n_state + n_extra :])

    made = pl.pallas_call(
        kernel,
        out_shape=tuple(shapes) + tuple(extra),
        in_specs=list(specs) + [ANY] * given,
        out_specs=tuple(VMEM if in_vmem(v) else ANY for v in [*shapes, *extra]),
        scratch_shapes=[pltpu.VMEM(s.shape, s.dtype) for s in scratch] + [pltpu.SemaphoreType.DMA((sems,))],
        input_output_aliases={} if fresh else {n_in + k: k for k in range(n_state)},
        compiler_params=pltpu.CompilerParams(vmem_limit_bytes=16 * 2**20),
        cost_estimate=pl.CostEstimate(flops=flops, bytes_accessed=moved, transcendentals=0),
        name=name,
    )(*ins, *([] if fresh else state))
    return list(made[:n_state]), list(made[n_state:])


def in_vmem(shape):
    return shape.memory_space == pltpu.VMEM


def pinned(block):
    return pltpu.with_memory_space_constraint(block, pltpu.VMEM)


def in_hbm(block):
    return pltpu.with_memory_space_constraint(block, pltpu.HBM)


def far(shape, dtype=BF):
    return pltpu.HBM(shape, dtype)


def sd(shape, dtype=BF):
    return jax.ShapeDtypeStruct(shape, dtype)


class Kernels:
    def __init__(self, images, rows, keys, width, hidden, heads):
        self.n, self.r, self.k, self.d, self.f, self.h = images, rows, keys, width, hidden, heads

    def forward(self, i, flags, x, vec_a, vec_f, weights, bias, state):
        n, r, k, d, f, h = self.n, self.r, self.k, self.d, self.f, self.h
        narrow, wide = far((n, r, d)), far((n, r, f))
        held = pltpu.VMEM((n, r, d), BF)
        shapes = [far((n, 5, r, d)), held, held, narrow, far((n, h, r, k)), pltpu.VMEM((n, r, f), BF), held, wide, narrow, narrow, narrow]
        row, high = sd((r, d)), sd((r, f))
        scratch = [row, sd((k, 3 * d)), sd((h, r, k)), row, row, high, row, row]
        ins, specs = [flags, pinned(x), vec_a, vec_f, pinned(bias)], [SMEM] + [VMEM] * 4
        extra = [pltpu.VMEM((r, d), BF)]
        if len(weights) > 3:
            ins, specs = ins + list(weights), specs + [ANY] * 4
            extra += [pltpu.VMEM((d, f), BF), pltpu.VMEM((d, f), BF), pltpu.VMEM((f, d), BF)]
        else:
            ins, specs = ins + [pinned(w) for w in weights], specs + [VMEM] * 3
        flops = 2 * r * d * 4 * d + 4 * h * r * k * HD + 4 * r * d * f
        return run(forward_image, i, "forward_image", ins, specs, state, shapes, extra, scratch, 20, flops, 12000000)

    def backward(self, i, flags, g, vec_a, vec_f, weights, hide, kept, state):
        n, r, k, d, f, h = self.n, self.r, self.k, self.d, self.f, self.h
        narrow = far((n, r, d))
        sums = far((n, 8, d), F32)
        held = pltpu.VMEM((n, r, d), BF)
        shapes = [pltpu.VMEM((n, r, f), BF), held, narrow, sums, held, pltpu.VMEM((n, r, 3 * d), BF), far((n, h, r, k)), narrow, sums]
        row, high, pairs, vec = sd((r, d)), sd((r, f)), sd((h, r, k)), sd((8, d), F32)
        scratch = [row, high, row, row, sd((k, 3 * d)), pairs, row, row, row, vec, row, pairs, row, vec]
        sa, a1, ctx, y1, pb, g_all, a2, gp, b2 = kept[:9]
        ins = [flags, pinned(g), vec_a, vec_f, *[pinned(w) for w in weights], hide, sa, pb, y1, gp, b2]
        flops = 2 * r * d * 4 * d + 8 * h * r * k * HD + 4 * r * d * f
        return run(backward_image, i, "backward_image", ins, [SMEM] + [VMEM] * 7 + [ANY] * 5, state, shapes, [pltpu.VMEM((r, d), BF)], scratch, 24, flops, 12000000)

    def parts(self, ups, flags, blocks, chunks):
        n, r, d = self.n, self.r, self.d
        tall = d // chunks
        both = (chunks, tall + tall // 2, d)
        made = pl.pallas_call(
            lambda *refs: weight_parts(ups, refs[:9], refs[9:13], refs[13:17], refs[17:]),
            out_shape=(far(both),) * 8,
            in_specs=[SMEM] + [VMEM] * 8,
            out_specs=(ANY,) * 8,
            scratch_shapes=[pltpu.VMEM((2, *both), BF)] * 2 + [pltpu.SemaphoreType.DMA((8 * chunks,))],
            compiler_params=pltpu.CompilerParams(vmem_limit_bytes=16 * 2**20),
            cost_estimate=pl.CostEstimate(flops=24 * n * r * d * d, bytes_accessed=14000000, transcendentals=0),
            name="weight_parts",
        )(flags, *[pinned(v) for v in blocks])
        return made[:4], made[4:]

    def join(self, flags, keep, got, length, dtype):
        n, r, d = keep.shape
        return pl.pallas_call(
            lambda *refs: join_images(refs[:3], refs[3], refs[4:]),
            out_shape=sd((length, 2 * n, d), dtype),
            in_specs=[SMEM] + [ANY] * 2,
            out_specs=VMEM,
            scratch_shapes=[pltpu.VMEM((2 * n, r, d), BF), pltpu.SemaphoreType.DMA((2,))],
            compiler_params=pltpu.CompilerParams(vmem_limit_bytes=16 * 2**20),
            cost_estimate=pl.CostEstimate(flops=0, bytes_accessed=10000000, transcendentals=0),
            name="join_images",
        )(flags, in_hbm(keep), in_hbm(got))

    def table(self, dl, grid):
        n, heads, rows, keys = dl.shape
        side = 2 * grid - 1
        wide = -(-(side * side + 3 + grid) // 128) * 128
        flat = pl.pallas_call(
            partial(table_fold, grid),
            out_shape=sd((heads, wide), F32),
            in_specs=[ANY],
            out_specs=VMEM,
            scratch_shapes=[pltpu.VMEM((heads, n, rows, keys), BF), pltpu.SemaphoreType.DMA((heads,))],
            compiler_params=pltpu.CompilerParams(vmem_limit_bytes=16 * 2**20),
            cost_estimate=pl.CostEstimate(flops=0, bytes_accessed=8000000, transcendentals=0),
            name="table_fold",
        )(in_hbm(dl))
        return flat

    def place(self, flags, a_up, a_down, b_up, b_down, state):
        d, f = self.d, self.f
        blocks, tall = 2 * a_up.shape[0], a_up.shape[1]
        given = 0 if state is None else 2
        scratch = [pltpu.VMEM((blocks, tall, d), F32)] * 2 + [pltpu.SemaphoreType.DMA((2 * blocks,))]
        return pl.pallas_call(
            lambda *refs: place_sums(refs[:5], refs[5 + given : 7 + given], refs[7 + given :]),
            out_shape=(sd((d, f), F32), sd((f, d), F32)),
            in_specs=[SMEM] + [VMEM] * 4 + [ANY] * given,
            out_specs=(ANY, ANY),
            scratch_shapes=scratch,
            input_output_aliases={5: 0, 6: 1} if given else {},
            compiler_params=pltpu.CompilerParams(vmem_limit_bytes=16 * 2**20),
            cost_estimate=pl.CostEstimate(flops=0, bytes_accessed=4000000, transcendentals=0),
            name="place_sums",
        )(flags, a_up, a_down, b_up, b_down, *(() if state is None else state))

    def bias(self, table, grid):
        heads = table.shape[0]
        side = 2 * grid - 1
        flipped = table[:, : side * side][:, ::-1]
        flipped = jnp.pad(flipped, ((0, 0), (0, -side * side % 128 + 128)))
        return pl.pallas_call(
            partial(bias_fill, grid),
            out_shape=pltpu.VMEM((heads, self.r, self.k), F32),
            in_specs=[SMEM, VMEM],
            out_specs=VMEM,
            compiler_params=pltpu.CompilerParams(vmem_limit_bytes=16 * 2**20),
            name="bias_fill",
        )(table[:, side * side :], flipped)


def swap(block, pairs):
    return lax.ppermute(block, "section", pairs)


def ring_order(n):
    return list(range(0, n, 2)) + list(range(n - 1, 0, -2))


def ring_place():
    n = lax.axis_size("dp")
    place = [0] * n
    for k, device in enumerate(ring_order(n)):
        place[device] = k
    return jnp.array(place, jnp.int32)[lax.axis_index("dp")] if n == RING else jnp.int32(0)


def weight_shares(kern, flags, blocks, both):
    ringed = lax.axis_size("dp") == RING
    sents, owns = kern.parts([ringed, ringed, False, False], flags, blocks, RING)
    got = {s: swap(sents[s], both) for s in (0, 2, 1, 3)}
    return [(owns[s], got[s]) for s in range(4)]


def weight_sums(kern, locals_, at, carry, tasks, low, core, to_low, to_high, sections):
    axis = "dp"
    n = lax.axis_size(axis)
    ringed = n == RING
    chunks = RING
    order = ring_order(n)
    tall = kern.d // chunks
    if not ringed:
        sums = [lax.psum((own.astype(F32) + got.astype(F32)).astype(BF), axis) for own, got in locals_]
        first = jnp.stack([v[:, :tall] for v in sums])
        second = jnp.stack([v[:, tall:] for v in sums])
        got_first, got_second = swap(first, to_high), swap(second, to_low)
        kept = jnp.concatenate([second, got_second], 2)
        columns = jnp.where(low, kept, got_first).transpose(1, 2, 0, 3)
        grad_weight = columns.reshape(kern.d, kern.f).astype(F32)
        grad_down = jnp.where(low, 0.0, first.astype(F32)).reshape(kern.f, kern.d)
        for task in tasks:
            carry, waiting = task(carry)
            if waiting is not None:
                carry = {**carry, **waiting}
        return grad_weight, grad_down, carry

    route = {w: [(order[k], order[(k + w) % n]) for k in range(n)] for w in (1, -1)}
    upper = {
        w: [(s * n + p, s * n + q) for s in range(1, sections, 2) for p, q in route[w]] for w in (1, -1)
    }
    held = [None] * 4
    for k in range(n):
        for s in (0, 2, 1, 3):
            own, other = locals_[s]
            total = own[k].astype(F32) + other[k].astype(F32)
            if k > 0:
                total = total + lax.ppermute(held[s], axis, route[1 if s < 2 else -1]).astype(F32)
            held[s] = total.astype(BF)
    first = jnp.stack([v[:tall] for v in held])
    second = jnp.stack([v[tall:] for v in held])
    got_first, got_second = swap(first, to_high), swap(second, to_low)
    kept = jnp.where(low, jnp.concatenate([second, got_second], 1), first)
    a = {1: kept[:2], -1: kept[2:]}
    b = {1: got_first[:2], -1: got_first[2:]}
    a, b, carry = lax.optimization_barrier((a, b, carry))
    state = None
    for k in range(n):
        index = jnp.stack([core, (at + 1 - k) & (n - 1), (at - 1 + k) & (n - 1)])
        if k < n - 1:
            next_a = {w: lax.ppermute(a[w], axis, route[w]) for w in (1, -1)}
            next_b = {w: lax.ppermute(b[w], ("section", axis), upper[w]) for w in (1, -1)}
        state = kern.place(index, a[1], a[-1], b[1], b[-1], state)
        waiting = None
        if k < len(tasks):
            carry, waiting = tasks[k](carry)
        if k < n - 1:
            a, b, state, carry = lax.optimization_barrier((next_a, next_b, state, carry))
        if waiting is not None:
            carry = {**carry, **waiting}
    return (*state, carry)


def on_device(embeds, mask, cotangent, section_weight, down_weight, section_vectors, rel_table):
    sections = lax.axis_size("section")
    now = lax.axis_index("section")
    core, stage = now % 2, now // 2
    images, length, width = embeds.shape
    half = images // 2
    hidden = section_weight.shape[2]
    heads = rel_table.shape[1]
    rows, keys = -(-length // 16) * 16, -(-length // 128) * 128
    grid = math.isqrt(length - 1)
    both = [(s, s ^ 1) for s in range(sections)]
    to_low = [(s, s - 1) for s in range(1, sections, 2)]
    to_high = [(s, s + 1) for s in range(0, sections, 2)]
    onward = [(s, s + 2) for s in range(sections - 2)]
    back = [(s + 2, s) for s in range(sections - 2)]
    low = core == 0

    own_w, own_d, own_v, own_t = section_weight[0], down_weight[0], section_vectors[0], rel_table[0]
    other_v = swap(own_v, both)
    table = jnp.where(low, own_t, swap(own_t, to_high))
    other_w = swap(own_w, both)
    other_d = swap(own_d, to_low)
    vec_a, vec_f = jnp.where(low, own_v, other_v), jnp.where(low, other_v, own_v)

    def mine_of(block):
        return lax.dynamic_slice_in_dim(block, core * half, half, 0)

    cover = mine_of(mask)[:, :, None] == 1
    start = jnp.where(cover, vec_a[6].astype(BF), mine_of(embeds))
    pad = ((0, 0), (0, rows - length), (0, 0))
    start = jnp.pad(start, pad)
    hide = jnp.pad((cover & (stage == 0)).astype(F32), pad)
    upstream = jnp.pad(mine_of(cotangent), pad)

    kern = Kernels(half, rows, keys, width, hidden, heads)
    at = ring_place()
    flags_p = jnp.stack([core, at])
    table, flags_p, at = lax.optimization_barrier((table, flags_p, at))
    bias = kern.bias(table, grid)
    flags_a = jnp.stack([(stage == 0).astype(jnp.int32), core])
    flags_b = jnp.stack([(stage == 1).astype(jnp.int32), core])
    weights = [own_w, other_w, own_d, other_d]
    kept, grads = None, None

    def forward(i, flags, x):
        nonlocal kept, weights
        kept, made = kern.forward(i, flags, x, vec_a, vec_f, weights, bias, kept)
        weights = made[1:] or weights
        return made[0]

    arrived = [swap(forward(i, flags_a, start), onward) for i in range(half)]
    for i in range(half):
        forward(i, flags_b, arrived[i])

    def backward(i, flags, g):
        nonlocal grads
        grads, (send,) = kern.backward(i, flags, g, vec_a, vec_f, weights, hide, kept, grads)
        return send

    returned = [swap(backward(i, flags_b, upstream), back) for i in range(half)]
    for i in range(half):
        backward(i, flags_a, returned[i])

    sa, a1, ctx, y1, pb, g_all, a2, gp, b2, keep_y, give_y = kept
    dh_all, ef, keep_x, vgf, ea, dq, dl, give_x, vga = grads
    blocks = (g_all, dh_all, a2, ef, a1, ctx, dq, ea)
    shares = weight_shares(kern, flags_p, blocks, both)
    own_parts, vga, vgf, dl, keep_x, give_x, keep_y, give_y = lax.optimization_barrier(
        ([v[0] for v in shares], vga, vgf, dl, keep_x, give_x, keep_y, give_y)
    )
    shares = [(own, other) for own, (_, other) in zip(own_parts, shares)]
    dp = lax.axis_size("dp")

    def mine_and_theirs(a_part, f_part):
        return jnp.where(low, a_part, f_part), jnp.where(low, f_part, a_part)

    def vector_sums(carry):
        return mine_and_theirs(jnp.sum(carry["vga"], 0), jnp.sum(carry["vgf"], 0))

    def rest(carry, *used):
        return {k: v for k, v in carry.items() if k not in used}

    def swap_y(carry):
        return rest(carry, "give_y"), {"got_y": swap(carry["give_y"], both)}

    def start_sums(carry):
        mine, theirs = vector_sums(carry)
        sums = kern.table(carry["dl"], grid)
        flat = jnp.concatenate([jnp.where(low, sums, 0.0).reshape(-1, 128), mine.reshape(-1, 128)])
        away = jnp.concatenate([jnp.where(low, 0.0, sums).reshape(-1, 128), theirs.reshape(-1, 128)])
        return {"small": flat, **rest(carry, "dl", "vga", "vgf")}, {"got": swap(away, both)}

    def doubling(step):
        def task(carry):
            small = carry["small"] + carry["got"]
            got = lax.ppermute(small, "dp", [(d, d ^ step) for d in range(dp)])
            return {**rest(carry, "got"), "small": small}, {"got": got}

        return task

    def join_y(carry):
        joined = kern.join(flags_a[1:], carry["keep_y"], carry["got_y"], length, BF)
        return {"y": joined, **rest(carry, "keep_y", "got_y", "give_x")}, {"got_x": swap(carry["give_x"], both)}

    def join_x(carry):
        joined = kern.join(flags_a[1:], carry["keep_x"], carry["got_x"], length, F32)
        return {"x": joined, **rest(carry, "keep_x", "got_x")}, None

    steps = [doubling(1 << k) for k in range(dp.bit_length() - 1)]
    tasks = [swap_y, start_sums, join_y, steps[0], join_x, *steps[1:]]
    grad_weight, grad_down, carry = weight_sums(
        kern,
        shares,
        at,
        {"dl": dl, "vga": vga, "vgf": vgf, "keep_y": keep_y, "give_y": give_y, "keep_x": keep_x, "give_x": give_x},
        tasks,
        low,
        core,
        to_low,
        to_high,
        sections,
    )
    small = carry["small"] + carry["got"]
    cut = small.shape[0] - 8 * width // 128
    grad_rows = small[cut:].reshape(8, width)
    flat = small[:cut].reshape(heads, -1)[:, : own_t.shape[1]] * (HD ** 0.5)
    pairs = own_t.shape[1] - 3
    grad_table = jnp.concatenate([flat[:, :pairs][:, ::-1], flat[:, pairs:]], 1)
    activations = carry["y"].transpose(1, 0, 2)
    input_grads = carry["x"].transpose(1, 0, 2)
    return (
        activations[None],
        input_grads[None],
        grad_weight[None],
        grad_down[None],
        grad_rows[None],
        jnp.where(low, grad_table, 0.0)[None],
    )


def solution(mesh):
    placed = (
        P("dp", None, None),
        P("dp", None),
        P("dp", None, None),
        P("section", None, None),
        P("section", None, None),
        P("section", None, None),
        P("section", None, None),
    )
    return jax.shard_map(
        on_device,
        mesh=mesh,
        in_specs=placed,
        out_specs=(
            P("section", "dp", None, None),
            P("section", "dp", None, None),
            P("section", None, None),
            P("section", None, None),
            P("section", None, None),
            P("section", None, None),
        ),
        check_vma=False,
    )
```

```python
import math
from functools import partial

import jax
import jax.numpy as jnp
from jax import lax
from jax.experimental import pallas as pl
from jax.experimental.pallas import tpu as pltpu
from jax.sharding import PartitionSpec as P

EPS = 1e-06
F32 = jnp.float32
BF = jnp.bfloat16
HD = 64
RING = 8
ANY = pl.BlockSpec(memory_space=pl.ANY)
VMEM = pl.BlockSpec(memory_space=pltpu.VMEM)
SMEM = pl.BlockSpec(memory_space=pltpu.SMEM)


def dot(left, right):
    return jnp.dot(left, right, preferred_element_type=F32)


def dot_nt(left, right):
    return lax.dot_general(left, right, (((1,), (1,)), ((), ())), preferred_element_type=F32)


def dot_tn(left, right):
    return lax.dot_general(left, right, (((0,), (0,)), ((), ())), preferred_element_type=F32)


def norm_stats(x):
    center = x - jnp.mean(x, -1, keepdims=True)
    rstd = lax.rsqrt(jnp.mean(center * center, -1, keepdims=True) + EPS)
    return center * rstd, rstd


def norm_back(g, da, xhat, rstd, gain):
    w = da * gain
    return g + rstd * (w - jnp.mean(w, -1, keepdims=True) - xhat * jnp.mean(w * xhat, -1, keepdims=True))


def rows_sum(v):
    return jnp.sum(v, 0, keepdims=True)


def gelu_parts(h):
    phi = 0.5 + 0.5 * lax.erf(h * 0.7071067811865476)
    return h * phi, phi + h * (jnp.exp(-0.5 * h * h) * 0.3989422804014327)


def loop(count, body):
    def one(k, none):
        body(k)
        return none

    lax.fori_loop(0, count, one, 0)


def cols_at(index, step, offset=0, size=None):
    return pl.ds(pl.multiple_of(offset + index * step, 128), size or step)


class Copies:
    def __init__(self, sems):
        self.sems, self.used, self.out = sems, 0, []

    def start(self, src, dst):
        copy = pltpu.make_async_copy(src, dst, self.sems.at[self.used])
        self.used += 1
        copy.start()
        return copy

    def choose(self, first, a, b, dst):
        return self.either(first, (a, dst), (b, dst))

    def either(self, first, one, two):
        sem = self.sems.at[self.used]
        self.used += 1

        @pl.when(first)
        def _():
            pltpu.make_async_copy(*one, sem).start()

        @pl.when(jnp.logical_not(first))
        def _():
            pltpu.make_async_copy(*two, sem).start()

        return pltpu.make_async_copy(*one, sem)

    def store(self, src, dst):
        self.out.append(self.start(src, dst))

    def finish(self):
        for copy in self.out:
            copy.wait()


def image_of(ref, i):
    return ref.at[i] if len(ref.shape) == 3 else ref


def head_masks(scale):
    lane = lax.broadcasted_iota(jnp.int32, (1, 2 * HD), 1)
    low = jnp.where(lane < HD, scale, 0.0).astype(BF)
    high = jnp.where(lane < HD, 0.0, scale).astype(BF)
    return low, high


def forward_image(i, refs_in, refs_state, refs_extra, scratch):
    flags, x_ref, vec_ref, vecf_ref, bias_ref = refs_in[:5]
    loading = len(refs_in) > 8
    wa_ref, w1_ref, w2_ref = refs_extra[1:] if loading else refs_in[5:]
    x_ref = image_of(x_ref, i)
    sa, a1, ctx, y1, pb, g_all, a2, gp, b2, out_y = refs_state
    send = refs_extra[0]
    x_v, qkv_v, pb_v, b_v, y_v, gp_v, bf_v, yf_v, sems = scratch
    rows, width = x_v.shape
    heads, keys = pb_v.shape[0], pb_v.shape[2]
    hidden = gp_v.shape[1]
    a_v, c_v, g_v, af_v = a1.at[i], ctx.at[i], g_all.at[i], a2.at[i]
    cp = Copies(sems)
    ready = []
    if loading:
        own_ref, other_ref, own_d, other_d = refs_in[5:]
        first = flags[1] == 0
        ready = [
            cp.choose(first, own_ref, other_ref, wa_ref),
            cp.choose(first, other_ref, own_ref, w1_ref),
            cp.choose(first, other_d, own_d, w2_ref),
        ]

        @pl.when(flags[0] == 0)
        def _():
            for copy in ready:
                copy.wait()

    @pl.when(flags[0] == 1)
    def _():
        x_v[...] = x_ref[...]
        cp.store(x_v, sa.at[i, 0])
        xhat, rstd = norm_stats(x_v[...].astype(F32))
        a_v[...] = (xhat * vec_ref[0:1, :] + vec_ref[1:2, :]).astype(BF)
        qkv_v[rows:, :] = jnp.zeros((keys - rows, 3 * width), BF)
        a = a_v[...]
        block = 256
        if loading:
            ready[0].wait()
        for j in range(3 * width // block):
            cols = slice(j * block, (j + 1) * block)
            part = dot(a, wa_ref[:, cols])
            kind, at = divmod(j * block, width)
            if kind == 0:
                part = part + vec_ref[4:5, at : at + block]
            if kind == 2:
                part = part + vec_ref[5:6, at : at + block]
            qkv_v[0:rows, cols] = part.astype(BF)
        for kind in range(3):
            cp.store(qkv_v.at[0:rows, pl.ds(kind * width, width)], sa.at[i, 1 + kind])
        scaled = head_masks(HD ** (-0.5))
        plain = head_masks(1.0)

        def some_heads(n):
            for pair in range(3):
                j = n * 3 + pair
                q = qkv_v[0:rows, cols_at(j, 128)]
                k = qkv_v[:, cols_at(j, 128, width)]
                u = qkv_v[:, cols_at(j, 128, 2 * width)]
                soft = []
                for t in range(2):
                    s = dot_nt(q * scaled[t], k) + bias_ref[2 * j + t]
                    e = jnp.exp(s - jnp.max(s, -1, keepdims=True))
                    p = (e * (1.0 / jnp.sum(e, -1, keepdims=True))).astype(BF)
                    pb_v[2 * j + t] = p
                    soft.append(p)
                total = dot(jnp.concatenate(soft, 1), jnp.concatenate([u * plain[0], u * plain[1]], 0))
                c_v[:, cols_at(j, 128)] = total.astype(BF)

        loop(heads // 2 // 3, some_heads)
        cp.store(pb_v, pb.at[i])
        b = dot(c_v[...], wa_ref[:, 3 * width :]) + vec_ref[3:4, :]
        b_v[...] = b.astype(BF)
        cp.store(b_v, sa.at[i, 4])
        y_v[...] = (x_v[...].astype(F32) + vec_ref[2:3, :] * b).astype(BF)
        cp.store(y_v, y1.at[i])
        cp.store(y_v, out_y.at[flags[1], i])

        xhat, rstd = norm_stats(y_v[...].astype(F32))
        af_v[...] = (xhat * vecf_ref[0:1, :] + vecf_ref[1:2, :]).astype(BF)
        a = af_v[...]
        if loading:
            ready[1].wait()

        def some_hidden(n):
            for k in range(width // block):
                cols = cols_at(n, width, k * block, block)
                h = dot(a, w1_ref[:, cols]) + vecf_ref[pl.ds(4 + n, 1), k * block : (k + 1) * block]
                value, slope = gelu_parts(h)
                g_v[:, cols] = value.astype(BF)
                gp_v[:, cols] = slope.astype(BF)

        loop(hidden // width, some_hidden)
        cp.store(gp_v, gp.at[i])
        if loading:
            ready[2].wait()
        b = dot(g_v[...], w2_ref[...]) + vecf_ref[3:4, :]
        yf_v[...] = (y_v[...].astype(F32) + vecf_ref[2:3, :] * b).astype(BF)
        send[...] = yf_v[...]
        cp.store(yf_v, out_y.at[1 - flags[1], i])
        bf_v[...] = b.astype(BF)
        cp.store(bf_v, b2.at[i])
        cp.finish()


def backward_image(i, refs_in, refs_state, refs_extra, scratch):
    flags, g_ref, vec_ref, vecf_ref, wa_ref, w1_ref, w2_ref, hide_ref, sa, pb, y1, gp, b2 = refs_in
    g_ref = image_of(g_ref, i)
    dh_all, ef, vgf, ea, dq, dl, out_x, vga = refs_state
    (send,) = refs_extra
    (gin_v, gp_v, bf_v, xf_v, qkv_v, pb_v, b_v, x_v, dx_v, vgf_v, dc_v, dl_v, dx0_v, vg_v, sems) = scratch
    e_v, dh_v, ea_v, dq_v = ef.at[i], dh_all.at[i], ea.at[i], dq.at[i]
    rows, width = x_v.shape
    heads, keys = pb_v.shape[0], pb_v.shape[2]
    hidden = dh_v.shape[1]

    @pl.when(flags[0] == 1)
    def _():
        cp = Copies(sems)
        in_gp = cp.start(gp.at[i], gp_v)
        in_bf = cp.start(b2.at[i], bf_v)
        in_xf = cp.start(y1.at[i], xf_v)
        ins = [cp.start(sa.at[i, 1 + kind], qkv_v.at[0:rows, pl.ds(kind * width, width)]) for kind in range(3)]
        in_pb = cp.start(pb.at[i], pb_v)
        in_b = cp.start(sa.at[i, 4], b_v)
        in_x = cp.start(sa.at[i, 0], x_v)
        qkv_v[rows:, :] = jnp.zeros((keys - rows, 3 * width), BF)
        vg_v[7:8, :] = jnp.zeros((1, width), F32)
        gin_v[...] = g_ref[...]
        scaled = gin_v[...].astype(F32) * vecf_ref[2:3, :]
        e_v[...] = scaled.astype(BF)
        vgf_v[3:4, :] = rows_sum(scaled)
        in_gp.wait()
        e = e_v[...]
        block = 256
        for j in range(hidden // block):
            row, at = divmod(j * block, width)
            cols = slice(j * block, (j + 1) * block)
            dh = dot_nt(e, w2_ref[cols, :]) * gp_v[:, cols].astype(F32)
            dh_v[:, cols] = dh.astype(BF)
            vgf_v[4 + row : 5 + row, at : at + block] = rows_sum(dh)
        in_bf.wait()
        in_xf.wait()
        vgf_v[2:3, :] = rows_sum(gin_v[...].astype(F32) * bf_v[...].astype(F32))
        da = dot_nt(dh_v[...], w1_ref[...])
        xhat, rstd = norm_stats(xf_v[...].astype(F32))
        vgf_v[0:1, :] = rows_sum(da * xhat)
        vgf_v[1:2, :] = rows_sum(da)
        cp.store(vgf_v, vgf.at[i])
        dx_v[...] = norm_back(gin_v[...].astype(F32), da, xhat, rstd, vecf_ref[0:1, :]).astype(BF)
        cp.store(dx_v, out_x.at[1 - flags[1], i])

        scaled = dx_v[...].astype(F32) * vec_ref[2:3, :]
        ea_v[...] = scaled.astype(BF)
        vg_v[3:4, :] = rows_sum(scaled)
        dc_v[...] = dot_nt(ea_v[...], wa_ref[:, 3 * width :]).astype(BF)
        for copy in ins:
            copy.wait()
        in_pb.wait()
        factor = HD ** (-0.5)
        plain = head_masks(1.0)

        def some_heads(n):
            for pair in range(3):
                j = n * 3 + pair
                cols = cols_at(j, 128)
                q = qkv_v[0:rows, cols_at(j, 128)]
                k = qkv_v[:, cols_at(j, 128, width)]
                u = qkv_v[:, cols_at(j, 128, 2 * width)]
                dc = dc_v[:, cols]
                dcs = jnp.concatenate([dc * plain[0], dc * plain[1]], 0)
                probs = pb_v[pl.ds(2 * j, 2)].reshape(2 * rows, keys)
                dp = dot_nt(dcs, u)
                pf = probs.astype(F32)
                wp = pf * dp
                ds = wp - pf * jnp.sum(wp, -1, keepdims=True)
                dlog = (ds * factor).astype(BF)
                dl_v[pl.ds(2 * j, 2)] = dlog.reshape(2, rows, keys)
                du_t = dot_tn(probs, dcs)
                dq_t = dot(
                    jnp.concatenate([dlog[:rows], dlog[rows:]], 1),
                    jnp.concatenate([k * plain[0], k * plain[1]], 0),
                )
                dk_t = dot_tn(dlog, jnp.concatenate([q * plain[0], q * plain[1]], 0))
                dq_v[:, cols_at(j, 128)] = dq_t.astype(BF)
                dq_v[:, cols_at(j, 128, width)] = dk_t[0:rows].astype(BF)
                dq_v[:, cols_at(j, 128, 2 * width)] = du_t[0:rows].astype(BF)
                vg_v[4:5, cols] = rows_sum(dq_t)
                vg_v[5:6, cols] = rows_sum(du_t)

        loop(heads // 2 // 3, some_heads)
        cp.store(dl_v, dl.at[i])
        in_b.wait()
        in_x.wait()
        vg_v[2:3, :] = rows_sum(dx_v[...].astype(F32) * b_v[...].astype(F32))
        da = dot_nt(dq_v[...], wa_ref[:, 0 : 3 * width])
        xhat, rstd = norm_stats(x_v[...].astype(F32))
        dx = norm_back(dx_v[...].astype(F32), da, xhat, rstd, vec_ref[0:1, :])
        send[...] = dx.astype(BF)
        hidden_rows = hide_ref[i] > 0.0
        dx0_v[...] = jnp.where(hidden_rows, 0.0, dx).astype(BF)
        vg_v[6:7, :] = rows_sum(jnp.where(hidden_rows, dx, 0.0))
        cp.store(dx0_v, out_x.at[flags[1], i])
        vg_v[0:1, :] = rows_sum(da * xhat)
        vg_v[1:2, :] = rows_sum(da)
        cp.store(vg_v, vga.at[i])
        cp.finish()


def weight_parts(ups, refs_in, sents, owns, scratch):
    flags, g_all, dh_all, a2, ef, a1, ctx, dq, ea = refs_in
    sent_v, own_v, sems = scratch
    width = a2.shape[2]
    chunks, tall = own_v.shape[1], a2.shape[2] // own_v.shape[1]
    part = tall // 2
    cp = Copies(sems)
    core, at = flags[0], flags[1]
    low = core == 0
    cuts = 1
    block, group = width // cuts, chunks // cuts
    rows = a2.shape[0] * a2.shape[1]

    def product(left, right, first_col, second_col, put):
        rhs = right[:, :, second_col : second_col + width].reshape(rows, width)

        for k in range(cuts):
            start = first_col + k * block
            lhs = left[:, :, start : start + block].reshape(rows, block)
            put(pl.ds(k * group, group), dot_tn(lhs, rhs).astype(BF).reshape(group, tall, width))

    def share(turn, s, which, target):
        def put(group, value):
            target[turn % 2, group, 0:tall] = value

        @pl.when(core == which)
        def _():
            product(a2, dh_all, 0, s * width, put)

        @pl.when(core != which)
        def _():
            product(g_all, ef, s * width, 0, put)

    def put_both(turn, group, value):
        sent_v[turn % 2, group, tall:] = jnp.where(low, value[:, part:], value[:, :part])
        own_v[turn % 2, group, tall:] = jnp.where(low, value[:, :part], value[:, part:])

    def store(turn, s, source, target):
        for chunk in range(chunks):
            slot = (at - chunk if ups[s] else chunk - at) & (chunks - 1)
            cp.store(source.at[turn % 2, chunk], target.at[slot])

    for turn, s in enumerate((0, 2, 1, 3)):
        if turn >= 2:
            for copy in cp.out[: 2 * chunks]:
                copy.wait()
            cp.out = cp.out[2 * chunks :]
        if s < 3:
            product(a1, dq, 0, s * width, partial(put_both, turn))
        else:
            product(ctx, ea, 0, 0, partial(put_both, turn))
        share(turn, s, 1, sent_v)
        store(turn, s, sent_v, sents[s])
        share(turn, s, 0, own_v)
        store(turn, s, own_v, owns[s])
    cp.finish()


def join_images(refs_in, out, scratch):
    flags, pair_ref, got_ref = refs_in
    keep_ref = pair_ref.at[0]
    all_v, sems = scratch
    half = got_ref.shape[0]
    cp = Copies(sems)
    low = flags[0] == 0
    copies = [
        cp.choose(low, keep_ref, got_ref, all_v.at[0:half]),
        cp.choose(low, got_ref, keep_ref, all_v.at[half : 2 * half]),
    ]
    for copy in copies:
        copy.wait()
    length, size = out.shape[0], 16
    for at in range(0, length, size):
        n = min(size, length - at)
        block = jnp.swapaxes(all_v[:, at : at + size, :].astype(F32), 0, 1)
        out[at : at + n] = block[:n].astype(out.dtype)


def small_sums(grid, flags, dl, vga, vgf, mine, theirs, flat_v, dl_v, sems):
    table_fold(grid, dl, flat_v, dl_v, sems)
    heads = flat_v.shape[0]
    low = flags[0] == 0
    table = flat_v[...]
    rows_a, rows_f = vga[0], vgf[0]
    for i in range(1, vga.shape[0]):
        rows_a, rows_f = rows_a + vga[i], rows_f + vgf[i]
    for out, here in ((mine, low), (theirs, jnp.logical_not(low))):
        out[...] = jnp.zeros(out.shape, F32)
        out[8 : 8 + heads, :] = jnp.where(here, table, 0.0)
        out[0:8, :] = jnp.where(here, rows_a, rows_f)


def table_fold(grid, dl, out, dl_v, sems):
    images, heads, rows, keys = dl.shape
    patches, side = grid * grid, 2 * grid - 1
    wide = -(-(side * grid) // 128) * 128 + 128
    copies = []
    for h in range(heads):
        copy = pltpu.make_async_copy(dl.at[:, h], dl_v.at[h], sems.at[h])
        copy.start()
        copies.append(copy)
    lane = lax.broadcasted_iota(jnp.int32, (1, keys), 1)
    narrow = lax.broadcasted_iota(jnp.int32, (1, 256), 1)
    last = lax.broadcasted_iota(jnp.int32, (1, out.shape[1]), 1)
    for h in range(heads):
        copies[h].wait()
        total = dl_v[h, 0].astype(F32)
        for i in range(1, images):
            total = total + dl_v[h, i].astype(F32)
        block = jnp.where(lane > 0, total, 0.0)
        sums = None
        for r in range(grid):
            part = block[1 + r * grid : 1 + (r + 1) * grid]
            part = jnp.concatenate([part, jnp.zeros((grid, wide - keys), F32)], 1)
            part = pltpu.roll(part, (grid * (grid - 1 - r) - 1) % wide, 1)
            sums = part if sums is None else sums + part
        tiles = [jnp.zeros((grid, 128), F32) for _ in range(out.shape[1] // 128 + 1)]
        for a in range(side):
            at, to = a * side // 128, a * grid // 128 * 128
            start = a * grid - to
            inside = (narrow >= start) & (narrow < start + grid)
            window = jnp.where(inside, sums[:, to : to + 256], 0.0)
            turned = pltpu.roll(window, (a * side + grid - 1 - at * 128 - start) % 256, 1)
            tiles[at] = tiles[at] + turned[:, :128]
            tiles[at + 1] = tiles[at + 1] + turned[:, 128:]
        slid = jnp.concatenate(tiles[:-1], 1)
        flat = slid[0:1]
        for c in range(1, grid):
            flat = flat + pltpu.roll(slid[c : c + 1], out.shape[1] - c, 1)
        upper = jnp.sum(jnp.where(lane > 0, total[0:1], 0.0), 1, keepdims=True)
        left = jnp.sum(total[1 : 1 + patches, 0:1], 0, keepdims=True)
        for k, value in enumerate((upper, left, total[0:1, 0:1])):
            flat = jnp.where(last == side * side + k, value, flat)
        out[h : h + 1, :] = flat


def turn_chunks(refs_in, refs_out):
    flags, held, got = refs_in[0], refs_in[1:5], refs_in[5]
    tall = refs_out[0].shape[1]
    part = tall // 2
    low = flags[0] == 0
    for s in range(4):
        a, b = refs_out[s // 2], refs_out[2 + s // 2]
        k = s % 2
        first = got[s, 0:tall]
        b[k] = first
        a[k, 0:part] = jnp.where(low, held[s][tall:], held[s][0:part])
        a[k, part:] = jnp.where(low, got[s, tall:], held[s][part:tall])


def place_sums(refs_in, refs_out, scratch):
    flags, a_up, a_down, b_up, b_down = refs_in
    gw, gd = refs_out
    gw_v, gd_v, sems = scratch
    blocks, tall, width = gd_v.shape
    low = flags[0] == 0
    cp = Copies(sems)
    for way, (a_ref, b_ref) in enumerate(((a_up, b_up), (a_down, b_down))):
        row = pl.multiple_of(flags[1 + way] * tall, tall)
        for k in range(blocks // 2):
            s = way * (blocks // 2) + k
            a = a_ref[k].astype(F32)
            gw_v[s] = jnp.where(low, a, b_ref[k].astype(F32))
            gd_v[s] = jnp.where(low, 0.0, a)
            cp.store(gw_v.at[s], gw.at[pl.ds(row, tall), pl.ds(s * width, width)])
            cp.store(gd_v.at[s], gd.at[pl.ds(pl.multiple_of(s * width + row, tall), tall)])
    cp.finish()


def bias_fill(grid, tail, flipped, out):
    heads, rows, keys = out.shape
    patches, side = grid * grid, 2 * grid - 1
    wide = -(-(side * grid) // 128) * 128
    high = -(-grid // 8) * 8
    lane = lax.broadcasted_iota(jnp.int32, (1, keys), 1)
    narrow = lax.broadcasted_iota(jnp.int32, (1, 128), 1)
    for h in range(heads):
        corner, upper, left = tail[h, 2], tail[h, 0], tail[h, 1]
        out[h, patches + 1 :, :] = jnp.where(
            lax.broadcasted_iota(jnp.int32, (rows - patches - 1, keys), 1) <= patches, 0.0, -1e30
        )
        out[h, 0:1, :] = jnp.where(lane == 0, corner, jnp.where(lane <= patches, upper, -1e30))
        slid = jnp.broadcast_to(flipped[h : h + 1, :], (high, flipped.shape[1]))
        slid = pltpu.roll(slid, 0, 1, stride=1, stride_axis=0)
        tiles = [jnp.zeros((high, 128), F32) for _ in range(wide // 128)]
        for a in range(side):
            at, to = a * side // 128 * 128, a * grid // 128
            start = a * grid - to * 128
            turned = pltpu.roll(slid[:, at : at + 256], (start - (a * side + grid - 1 - at)) % 256, 1)
            for k in range(2):
                if 128 * k < start + grid and start < 128 * (k + 1):
                    inside = (narrow >= start - 128 * k) & (narrow < start + grid - 128 * k)
                    tiles[to + k] = jnp.where(inside, turned[:, 128 * k : 128 * (k + 1)], tiles[to + k])
        block = jnp.concatenate(tiles, 1)
        for r in range(grid):
            turned = pltpu.roll(block, (1 - grid * (grid - 1 - r)) % wide, 1)[0:grid, 0:keys]
            turned = jnp.where(lane == 0, left, jnp.where(lane <= patches, turned, -1e30))
            out[h, 1 + r * grid : 1 + (r + 1) * grid, :] = turned


def run(body, i, name, ins, specs, state, shapes, extra, scratch, sems, flops, moved):
    fresh = state is None
    ins = [in_hbm(v) if spec is ANY else v for v, spec in zip(ins, specs)]
    n_in, n_state, n_extra = len(ins), len(shapes), len(extra)
    given = 0 if fresh else n_state

    def kernel(*refs):
        refs_in = refs[:n_in]
        outs = refs[n_in + given : n_in + given + n_state]
        more = refs[n_in + given + n_state : n_in + given + n_state + n_extra]
        body(i, refs_in, outs, more, refs[n_in + given + n_state + n_extra :])

    made = pl.pallas_call(
        kernel,
        out_shape=tuple(shapes) + tuple(extra),
        in_specs=list(specs) + [ANY] * given,
        out_specs=tuple(VMEM if in_vmem(v) else ANY for v in [*shapes, *extra]),
        scratch_shapes=[pltpu.VMEM(s.shape, s.dtype) for s in scratch] + [pltpu.SemaphoreType.DMA((sems,))],
        input_output_aliases={} if fresh else {n_in + k: k for k in range(n_state)},
        compiler_params=pltpu.CompilerParams(vmem_limit_bytes=16 * 2**20),
        cost_estimate=pl.CostEstimate(flops=flops, bytes_accessed=moved, transcendentals=0),
        name=name,
    )(*ins, *([] if fresh else state))
    return list(made[:n_state]), list(made[n_state:])


def in_vmem(shape):
    return shape.memory_space == pltpu.VMEM


def pinned(block):
    return pltpu.with_memory_space_constraint(block, pltpu.VMEM)


def in_hbm(block):
    return pltpu.with_memory_space_constraint(block, pltpu.HBM)


def far(shape, dtype=BF):
    return pltpu.HBM(shape, dtype)


def sd(shape, dtype=BF):
    return jax.ShapeDtypeStruct(shape, dtype)


class Kernels:
    def __init__(self, images, rows, keys, width, hidden, heads):
        self.n, self.r, self.k, self.d, self.f, self.h = images, rows, keys, width, hidden, heads

    def forward(self, i, flags, x, vec_a, vec_f, weights, bias, state):
        n, r, k, d, f, h = self.n, self.r, self.k, self.d, self.f, self.h
        narrow, wide = far((n, r, d)), far((n, r, f))
        held = pltpu.VMEM((n, r, d), BF)
        shapes = [far((n, 5, r, d)), held, held, narrow, far((n, h, r, k)), pltpu.VMEM((n, r, f), BF), held, wide, narrow, far((2, n, r, d))]
        row, high = sd((r, d)), sd((r, f))
        scratch = [row, sd((k, 3 * d)), sd((h, r, k)), row, row, high, row, row]
        ins, specs = [flags, pinned(x), vec_a, vec_f, pinned(bias)], [SMEM] + [VMEM] * 4
        extra = [pltpu.VMEM((r, d), BF)]
        if len(weights) > 3:
            ins, specs = ins + list(weights), specs + [ANY] * 4
            extra += [pltpu.VMEM((d, f), BF), pltpu.VMEM((d, f), BF), pltpu.VMEM((f, d), BF)]
        else:
            ins, specs = ins + [pinned(w) for w in weights], specs + [VMEM] * 3
        flops = 2 * r * d * 4 * d + 4 * h * r * k * HD + 4 * r * d * f
        return run(forward_image, i, "forward_image", ins, specs, state, shapes, extra, scratch, 20, flops, 12000000)

    def backward(self, i, flags, g, vec_a, vec_f, weights, hide, kept, state):
        n, r, k, d, f, h = self.n, self.r, self.k, self.d, self.f, self.h
        narrow = far((n, r, d))
        sums = far((n, 8, d), F32)
        held = pltpu.VMEM((n, r, d), BF)
        shapes = [pltpu.VMEM((n, r, f), BF), held, sums, held, pltpu.VMEM((n, r, 3 * d), BF), far((n, h, r, k)), far((2, n, r, d)), sums]
        row, high, pairs, vec = sd((r, d)), sd((r, f)), sd((h, r, k)), sd((8, d), F32)
        scratch = [row, high, row, row, sd((k, 3 * d)), pairs, row, row, row, vec, row, pairs, row, vec]
        sa, a1, ctx, y1, pb, g_all, a2, gp, b2 = kept[:9]
        ins = [flags, pinned(g), vec_a, vec_f, *[pinned(w) for w in weights], hide, sa, pb, y1, gp, b2]
        flops = 2 * r * d * 4 * d + 8 * h * r * k * HD + 4 * r * d * f
        return run(backward_image, i, "backward_image", ins, [SMEM] + [VMEM] * 7 + [ANY] * 5, state, shapes, [pltpu.VMEM((r, d), BF)], scratch, 24, flops, 12000000)

    def parts(self, ups, flags, blocks, chunks):
        n, r, d = self.n, self.r, self.d
        tall = d // chunks
        both = (chunks, tall + tall // 2, d)
        made = pl.pallas_call(
            lambda *refs: weight_parts(ups, refs[:9], refs[9:13], refs[13:17], refs[17:]),
            out_shape=(far(both),) * 8,
            in_specs=[SMEM] + [VMEM] * 8,
            out_specs=(ANY,) * 8,
            scratch_shapes=[pltpu.VMEM((2, *both), BF)] * 2 + [pltpu.SemaphoreType.DMA((8 * chunks,))],
            compiler_params=pltpu.CompilerParams(vmem_limit_bytes=16 * 2**20),
            cost_estimate=pl.CostEstimate(flops=24 * n * r * d * d, bytes_accessed=14000000, transcendentals=0),
            name="weight_parts",
        )(flags, *[pinned(v) for v in blocks])
        return made[:4], made[4:]

    def join(self, flags, pair, got, length, dtype):
        n, r, d = got.shape
        return pl.pallas_call(
            lambda *refs: join_images(refs[:3], refs[3], refs[4:]),
            out_shape=sd((length, 2 * n, d), dtype),
            in_specs=[SMEM] + [ANY] * 2,
            out_specs=VMEM,
            scratch_shapes=[pltpu.VMEM((2 * n, r, d), BF), pltpu.SemaphoreType.DMA((2,))],
            compiler_params=pltpu.CompilerParams(vmem_limit_bytes=16 * 2**20),
            cost_estimate=pl.CostEstimate(flops=0, bytes_accessed=10000000, transcendentals=0),
            name="join_images",
        )(flags, in_hbm(pair), in_hbm(got))

    def smalls(self, flags, dl, vga, vgf, grid):
        n, heads, rows, keys = dl.shape
        d = self.d
        out = sd((8 + -(-heads // 8) * 8, d), F32)
        return pl.pallas_call(
            partial(small_sums, grid),
            out_shape=(out, out),
            in_specs=[SMEM, ANY, VMEM, VMEM],
            out_specs=(VMEM, VMEM),
            scratch_shapes=[
                pltpu.VMEM((heads, d), F32),
                pltpu.VMEM((heads, n, rows, keys), BF),
                pltpu.SemaphoreType.DMA((heads,)),
            ],
            compiler_params=pltpu.CompilerParams(vmem_limit_bytes=16 * 2**20),
            cost_estimate=pl.CostEstimate(flops=0, bytes_accessed=12000000, transcendentals=0),
            name="small_sums",
        )(flags, in_hbm(dl), vga, vgf)

    def turn(self, core, held, got):
        d = self.d
        out = sd((2, d // RING, d))
        made = pl.pallas_call(
            lambda *refs: turn_chunks(refs[:6], refs[6:]),
            out_shape=(out,) * 4,
            in_specs=[SMEM] + [VMEM] * 5,
            out_specs=(VMEM,) * 4,
            compiler_params=pltpu.CompilerParams(vmem_limit_bytes=16 * 2**20),
            cost_estimate=pl.CostEstimate(flops=0, bytes_accessed=3000000, transcendentals=0),
            name="turn_chunks",
        )(core.reshape(1), *held, got)
        return list(made[:2]), list(made[2:])

    def place(self, flags, mine, got, state):
        d, f = self.d, self.f
        blocks, tall = 2 * mine[0].shape[0], d // RING
        given = 0 if state is None else 2
        scratch = [pltpu.VMEM((blocks, tall, d), F32)] * 2 + [pltpu.SemaphoreType.DMA((2 * blocks,))]
        return pl.pallas_call(
            lambda *refs: place_sums(refs[:5], refs[5 + given : 7 + given], refs[7 + given :]),
            out_shape=(sd((d, f), F32), sd((f, d), F32)),
            in_specs=[SMEM] + [VMEM] * 4 + [ANY] * given,
            out_specs=(ANY, ANY),
            scratch_shapes=scratch,
            input_output_aliases={5: 0, 6: 1} if given else {},
            compiler_params=pltpu.CompilerParams(vmem_limit_bytes=16 * 2**20),
            cost_estimate=pl.CostEstimate(flops=0, bytes_accessed=4000000, transcendentals=0),
            name="place_sums",
        )(flags, *mine, *got, *(() if state is None else state))

    def bias(self, table, grid):
        heads = table.shape[0]
        side = 2 * grid - 1
        flipped = table[:, : side * side][:, ::-1]
        flipped = jnp.pad(flipped, ((0, 0), (0, -side * side % 128 + 128)))
        return pl.pallas_call(
            partial(bias_fill, grid),
            out_shape=pltpu.VMEM((heads, self.r, self.k), F32),
            in_specs=[SMEM, VMEM],
            out_specs=VMEM,
            compiler_params=pltpu.CompilerParams(vmem_limit_bytes=16 * 2**20),
            name="bias_fill",
        )(table[:, side * side :], flipped)


def swap(block, pairs):
    return lax.ppermute(block, "section", pairs)


def ring_order(n):
    return list(range(0, n, 2)) + list(range(n - 1, 0, -2))


def ring_place():
    n = lax.axis_size("dp")
    place = [0] * n
    for k, device in enumerate(ring_order(n)):
        place[device] = k
    return jnp.array(place, jnp.int32)[lax.axis_index("dp")] if n == RING else jnp.int32(0)


def weight_shares(kern, flags, blocks, both):
    ringed = lax.axis_size("dp") == RING
    sents, owns = kern.parts([ringed, ringed, False, False], flags, blocks, RING)
    got = {s: swap(sents[s], both) for s in (0, 2, 1, 3)}
    return [(owns[s], got[s]) for s in range(4)]


def weight_sums(kern, locals_, at, carry, early, tasks, low, core, both, to_low, to_high, sections):
    axis = "dp"
    n = lax.axis_size(axis)
    ringed = n == RING
    chunks = RING
    order = ring_order(n)
    tall = kern.d // chunks
    if not ringed:
        sums = [lax.psum((own.astype(F32) + got.astype(F32)).astype(BF), axis) for own, got in locals_]
        first = jnp.stack([v[:, :tall] for v in sums])
        second = jnp.stack([v[:, tall:] for v in sums])
        got_first, got_second = swap(first, to_high), swap(second, to_low)
        kept = jnp.concatenate([second, got_second], 2)
        columns = jnp.where(low, kept, got_first).transpose(1, 2, 0, 3)
        grad_weight = columns.reshape(kern.d, kern.f).astype(F32)
        grad_down = jnp.where(low, 0.0, first.astype(F32)).reshape(kern.f, kern.d)
        for task in [*early.values(), *tasks.values()]:
            carry, waiting = task(carry)
            if waiting is not None:
                carry = {**carry, **waiting}
        return grad_weight, grad_down, carry

    route = {w: [(order[k], order[(k + w) % n]) for k in range(n)] for w in (1, -1)}
    upper = {
        w: [(s * n + p, s * n + q) for s in range(1, sections, 2) for p, q in route[w]] for w in (1, -1)
    }
    held = [None] * 4
    waiting = None
    for k in range(n):
        if k in early:
            if held[3] is not None:
                held[3], carry = lax.optimization_barrier((held[3], carry))
            if waiting is not None:
                carry = {**carry, **waiting}
            carry, waiting = early[k](carry)
        for s in (0, 2, 1, 3):
            own, other = locals_[s]
            total = own[k].astype(F32) + other[k].astype(F32)
            if k > 0:
                total = total + lax.ppermute(held[s], axis, route[1 if s < 2 else -1]).astype(F32)
            held[s] = total.astype(BF)
    a, b = kern.turn(core, held, swap(jnp.stack(held), both))
    a, b, carry = lax.optimization_barrier((a, b, carry))
    state, waiting = None, None
    for k in range(n):
        index = jnp.stack([core, (at + 1 - k) & (n - 1), (at - 1 + k) & (n - 1)])
        if k < n - 1:
            if state is not None:
                a[0], state, carry = lax.optimization_barrier((a[0], state, carry))
            next_a = [lax.ppermute(v, axis, route[w]) for v, w in zip(a, (1, -1))]
            next_b = [lax.ppermute(v, ("section", axis), upper[w]) for v, w in zip(b, (1, -1))]
        if k in tasks:
            carry, waiting = tasks[k](carry)
        state = kern.place(index, a, b, state)
        if k < n - 1:
            a, b = next_a, next_b
    return (*state, carry)


def on_device(embeds, mask, cotangent, section_weight, down_weight, section_vectors, rel_table):
    sections = lax.axis_size("section")
    now = lax.axis_index("section")
    core, stage = now % 2, now // 2
    images, length, width = embeds.shape
    half = images // 2
    hidden = section_weight.shape[2]
    heads = rel_table.shape[1]
    rows, keys = -(-length // 16) * 16, -(-length // 128) * 128
    grid = math.isqrt(length - 1)
    both = [(s, s ^ 1) for s in range(sections)]
    to_low = [(s, s - 1) for s in range(1, sections, 2)]
    to_high = [(s, s + 1) for s in range(0, sections, 2)]
    onward = [(s, s + 2) for s in range(sections - 2)]
    back = [(s + 2, s) for s in range(sections - 2)]
    low = core == 0

    own_w, own_d, own_v, own_t = section_weight[0], down_weight[0], section_vectors[0], rel_table[0]
    other_v = swap(own_v, both)
    table = jnp.where(low, own_t, swap(own_t, to_high))
    other_w = swap(own_w, both)
    other_d = swap(own_d, to_low)
    vec_a, vec_f = jnp.where(low, own_v, other_v), jnp.where(low, other_v, own_v)

    def mine_of(block):
        return lax.dynamic_slice_in_dim(block, core * half, half, 0)

    cover = mine_of(mask)[:, :, None] == 1
    start = jnp.where(cover, vec_a[6].astype(BF), mine_of(embeds))
    pad = ((0, 0), (0, rows - length), (0, 0))
    start = jnp.pad(start, pad)
    hide = jnp.pad((cover & (stage == 0)).astype(F32), pad)
    upstream = jnp.pad(mine_of(cotangent), pad)

    kern = Kernels(half, rows, keys, width, hidden, heads)
    at = ring_place()
    flags_p = jnp.stack([core, at])
    table, flags_p, at = lax.optimization_barrier((table, flags_p, at))
    bias = kern.bias(table, grid)
    flags_a = jnp.stack([(stage == 0).astype(jnp.int32), core])
    flags_b = jnp.stack([(stage == 1).astype(jnp.int32), core])
    weights = [own_w, other_w, own_d, other_d]
    kept, grads = None, None

    def forward(i, flags, x):
        nonlocal kept, weights
        kept, made = kern.forward(i, flags, x, vec_a, vec_f, weights, bias, kept)
        weights = made[1:] or weights
        return made[0]

    arrived = [swap(forward(i, flags_a, start), onward) for i in range(half)]
    for i in range(half):
        forward(i, flags_b, arrived[i])

    def backward(i, flags, g):
        nonlocal grads
        grads, (send,) = kern.backward(i, flags, g, vec_a, vec_f, weights, hide, kept, grads)
        return send

    returned = [swap(backward(i, flags_b, upstream), back) for i in range(half)]
    for i in range(half):
        backward(i, flags_a, returned[i])

    sa, a1, ctx, y1, pb, g_all, a2, gp, b2, out_y = kept
    dh_all, ef, vgf, ea, dq, dl, out_x, vga = grads
    blocks = (g_all, dh_all, a2, ef, a1, ctx, dq, ea)
    shares = weight_shares(kern, flags_p, blocks, both)
    own_parts, vga, vgf, dl, out_x, out_y = lax.optimization_barrier(
        ([v[0] for v in shares], vga, vgf, dl, out_x, out_y)
    )
    shares = [(own, other) for own, (_, other) in zip(own_parts, shares)]
    dp = lax.axis_size("dp")

    def rest(carry, *used):
        return {k: v for k, v in carry.items() if k not in used}

    def swap_y(carry):
        return carry, {"got_y": swap(carry["out_y"][1], both)}

    def fold(carry):
        mine, away = kern.smalls(flags_p, carry["dl"], carry["vga"], carry["vgf"], grid)
        traded = {"got": away, "got_y": carry["out_y"][1], "got_x": carry["out_x"][1]}
        return {"small": mine, **rest(carry, "dl", "vga", "vgf")}, {k: swap(v, both) for k, v in traded.items()}

    def doubling(step):
        def task(carry):
            small = carry["small"] + carry["got"]
            got = lax.ppermute(small, "dp", [(d, d ^ step) for d in range(dp)])
            return {**rest(carry, "got"), "small": small}, {"got": got}

        return task

    def join_y(carry):
        joined = kern.join(flags_a[1:], carry["out_y"], carry["got_y"], length, BF)
        return {"y": joined, **rest(carry, "out_y", "got_y")}, None

    def join_x(carry):
        joined = kern.join(flags_a[1:], carry["out_x"], carry["got_x"], length, F32)
        return {"x": joined, **rest(carry, "out_x", "got_x")}, None

    def both_of(one, two):
        def task(carry):
            carry, waiting = one(carry)
            carry, more = two(carry)
            return carry, {**(waiting or {}), **(more or {})}

        return task

    def add_last(carry):
        return {"small": carry["small"] + carry["got"], **rest(carry, "small", "got")}, None

    def finish(carry):
        small = carry["small"]
        flat = small[8 : 8 + heads, : own_t.shape[1]] * (HD ** 0.5)
        pairs = own_t.shape[1] - 3
        table = jnp.concatenate([flat[:, :pairs][:, ::-1], flat[:, pairs:]], 1)
        return {"rows": small[:8], "table": jnp.where(low, table, 0.0), **rest(carry, "small")}, None

    steps = [doubling(1 << k) for k in range(dp.bit_length() - 1)]
    early = dict(enumerate([fold, *steps, add_last]))
    if len(steps) == 3:
        early = dict(zip((0, 1, 2, 4, 5), early.values()))
    tasks = {3: join_y, 4: finish, 6: join_x}
    grad_weight, grad_down, carry = weight_sums(
        kern,
        shares,
        at,
        {"dl": dl, "vga": vga, "vgf": vgf, "out_y": out_y, "out_x": out_x},
        early,
        tasks,
        low,
        core,
        both,
        to_low,
        to_high,
        sections,
    )
    activations = carry["y"].transpose(1, 0, 2)
    input_grads = carry["x"].transpose(1, 0, 2)
    return (
        activations[None],
        input_grads[None],
        grad_weight[None],
        grad_down[None],
        carry["rows"][None],
        carry["table"][None],
    )


def solution(mesh):
    placed = (
        P("dp", None, None),
        P("dp", None),
        P("dp", None, None),
        P("section", None, None),
        P("section", None, None),
        P("section", None, None),
        P("section", None, None),
    )
    return jax.shard_map(
        on_device,
        mesh=mesh,
        in_specs=placed,
        out_specs=(
            P("section", "dp", None, None),
            P("section", "dp", None, None),
            P("section", None, None),
            P("section", None, None),
            P("section", None, None),
            P("section", None, None),
        ),
        check_vma=False,
    )
```

```python
import math
from functools import partial

import jax
import jax.numpy as jnp
from jax import lax
from jax.experimental import pallas as pl
from jax.experimental.pallas import tpu as pltpu
from jax.sharding import PartitionSpec as P

EPS = 1e-06
F32 = jnp.float32
BF = jnp.bfloat16
HD = 64
RING = 8
ANY = pl.BlockSpec(memory_space=pl.ANY)
VMEM = pl.BlockSpec(memory_space=pltpu.VMEM)
SMEM = pl.BlockSpec(memory_space=pltpu.SMEM)


def dot(left, right):
    return jnp.dot(left, right, preferred_element_type=F32)


def dot_nt(left, right):
    return lax.dot_general(left, right, (((1,), (1,)), ((), ())), preferred_element_type=F32)


def dot_tn(left, right):
    return lax.dot_general(left, right, (((0,), (0,)), ((), ())), preferred_element_type=F32)


def norm_stats(x):
    center = x - jnp.mean(x, -1, keepdims=True)
    rstd = lax.rsqrt(jnp.mean(center * center, -1, keepdims=True) + EPS)
    return center * rstd, rstd


def norm_back(g, da, xhat, rstd, gain):
    w = da * gain
    return g + rstd * (w - jnp.mean(w, -1, keepdims=True) - xhat * jnp.mean(w * xhat, -1, keepdims=True))


def rows_sum(v):
    return jnp.sum(v, 0, keepdims=True)


def gelu_parts(h):
    phi = 0.5 + 0.5 * lax.erf(h * 0.7071067811865476)
    return h * phi, phi + h * (jnp.exp(-0.5 * h * h) * 0.3989422804014327)


def loop(count, body):
    def one(k, none):
        body(k)
        return none

    lax.fori_loop(0, count, one, 0)


def cols_at(index, step, offset=0, size=None):
    return pl.ds(pl.multiple_of(offset + index * step, 128), size or step)


class Copies:
    def __init__(self, sems):
        self.sems, self.used, self.out = sems, 0, []

    def start(self, src, dst):
        copy = pltpu.make_async_copy(src, dst, self.sems.at[self.used])
        self.used += 1
        copy.start()
        return copy

    def choose(self, first, a, b, dst):
        return self.either(first, (a, dst), (b, dst))

    def either(self, first, one, two):
        sem = self.sems.at[self.used]
        self.used += 1

        @pl.when(first)
        def _():
            pltpu.make_async_copy(*one, sem).start()

        @pl.when(jnp.logical_not(first))
        def _():
            pltpu.make_async_copy(*two, sem).start()

        return pltpu.make_async_copy(*one, sem)

    def store(self, src, dst):
        self.out.append(self.start(src, dst))

    def finish(self):
        for copy in self.out:
            copy.wait()


def image_of(ref, i):
    return ref.at[i] if len(ref.shape) == 3 else ref


def head_masks(scale):
    lane = lax.broadcasted_iota(jnp.int32, (1, 2 * HD), 1)
    low = jnp.where(lane < HD, scale, 0.0).astype(BF)
    high = jnp.where(lane < HD, 0.0, scale).astype(BF)
    return low, high


def forward_image(i, refs_in, refs_state, refs_extra, scratch):
    flags, x_ref, vec_ref, vecf_ref, bias_ref = refs_in[:5]
    loading = len(refs_in) > 8
    wa_ref, w1_ref, w2_ref = refs_extra[1:] if loading else refs_in[5:]
    x_ref = image_of(x_ref, i)
    sa, a1, ctx, y1, pb, g_all, a2, gp, b2, out_y = refs_state
    send = refs_extra[0]
    x_v, qkv_v, pb_v, b_v, y_v, gp_v, bf_v, yf_v, sems = scratch
    rows, width = x_v.shape
    heads, keys = pb_v.shape[0], pb_v.shape[2]
    hidden = gp_v.shape[1]
    a_v, c_v, g_v, af_v = a1.at[i], ctx.at[i], g_all.at[i], a2.at[i]
    cp = Copies(sems)
    ready = []
    if loading:
        own_ref, other_ref, own_d, other_d = refs_in[5:]
        first = flags[1] == 0
        ready = [
            cp.choose(first, own_ref, other_ref, wa_ref),
            cp.choose(first, other_ref, own_ref, w1_ref),
            cp.choose(first, other_d, own_d, w2_ref),
        ]

        @pl.when(flags[0] == 0)
        def _():
            for copy in ready:
                copy.wait()

    @pl.when(flags[0] == 1)
    def _():
        x_v[...] = x_ref[...]
        cp.store(x_v, sa.at[i, 0])
        xhat, rstd = norm_stats(x_v[...].astype(F32))
        a_v[...] = (xhat * vec_ref[0:1, :] + vec_ref[1:2, :]).astype(BF)
        qkv_v[rows:, :] = jnp.zeros((keys - rows, 3 * width), BF)
        a = a_v[...]
        block = 256
        if loading:
            ready[0].wait()
        for j in range(3 * width // block):
            cols = slice(j * block, (j + 1) * block)
            part = dot(a, wa_ref[:, cols])
            kind, at = divmod(j * block, width)
            if kind == 0:
                part = part + vec_ref[4:5, at : at + block]
            if kind == 2:
                part = part + vec_ref[5:6, at : at + block]
            qkv_v[0:rows, cols] = part.astype(BF)
        for kind in range(3):
            cp.store(qkv_v.at[0:rows, pl.ds(kind * width, width)], sa.at[i, 1 + kind])
        scaled = head_masks(HD ** (-0.5))
        plain = head_masks(1.0)

        def some_heads(n):
            for pair in range(3):
                j = n * 3 + pair
                q = qkv_v[0:rows, cols_at(j, 128)]
                k = qkv_v[:, cols_at(j, 128, width)]
                u = qkv_v[:, cols_at(j, 128, 2 * width)]
                soft = []
                for t in range(2):
                    s = dot_nt(q * scaled[t], k) + bias_ref[2 * j + t]
                    e = jnp.exp(s - jnp.max(s, -1, keepdims=True))
                    p = (e * (1.0 / jnp.sum(e, -1, keepdims=True))).astype(BF)
                    pb_v[2 * j + t] = p
                    soft.append(p)
                total = dot(jnp.concatenate(soft, 1), jnp.concatenate([u * plain[0], u * plain[1]], 0))
                c_v[:, cols_at(j, 128)] = total.astype(BF)

        loop(heads // 2 // 3, some_heads)
        cp.store(pb_v, pb.at[i])
        b = dot(c_v[...], wa_ref[:, 3 * width :]) + vec_ref[3:4, :]
        b_v[...] = b.astype(BF)
        cp.store(b_v, sa.at[i, 4])
        y_v[...] = (x_v[...].astype(F32) + vec_ref[2:3, :] * b).astype(BF)
        cp.store(y_v, y1.at[i])
        cp.store(y_v, out_y.at[flags[1], i])

        xhat, rstd = norm_stats(y_v[...].astype(F32))
        af_v[...] = (xhat * vecf_ref[0:1, :] + vecf_ref[1:2, :]).astype(BF)
        a = af_v[...]
        if loading:
            ready[1].wait()

        def some_hidden(n):
            for k in range(width // block):
                cols = cols_at(n, width, k * block, block)
                h = dot(a, w1_ref[:, cols]) + vecf_ref[pl.ds(4 + n, 1), k * block : (k + 1) * block]
                value, slope = gelu_parts(h)
                g_v[:, cols] = value.astype(BF)
                gp_v[:, cols] = slope.astype(BF)

        loop(hidden // width, some_hidden)
        cp.store(gp_v, gp.at[i])
        if loading:
            ready[2].wait()
        b = dot(g_v[...], w2_ref[...]) + vecf_ref[3:4, :]
        yf_v[...] = (y_v[...].astype(F32) + vecf_ref[2:3, :] * b).astype(BF)
        send[...] = yf_v[...]
        cp.store(yf_v, out_y.at[1 - flags[1], i])
        bf_v[...] = b.astype(BF)
        cp.store(bf_v, b2.at[i])
        cp.finish()


def backward_image(i, refs_in, refs_state, refs_extra, scratch):
    flags, g_ref, vec_ref, vecf_ref, wa_ref, w1_ref, w2_ref, hide_ref, sa, pb, y1, gp, b2 = refs_in
    g_ref = image_of(g_ref, i)
    dh_all, ef, vgf, ea, dq, dl, out_x, vga = refs_state
    (send,) = refs_extra
    (gin_v, gp_v, bf_v, xf_v, qkv_v, pb_v, b_v, x_v, dx_v, vgf_v, dc_v, dl_v, dx0_v, vg_v, sems) = scratch
    e_v, dh_v, ea_v, dq_v = ef.at[i], dh_all.at[i], ea.at[i], dq.at[i]
    rows, width = x_v.shape
    heads, keys = pb_v.shape[0], pb_v.shape[2]
    hidden = dh_v.shape[1]

    @pl.when(flags[0] == 1)
    def _():
        cp = Copies(sems)
        in_gp = cp.start(gp.at[i], gp_v)
        in_bf = cp.start(b2.at[i], bf_v)
        in_xf = cp.start(y1.at[i], xf_v)
        ins = [cp.start(sa.at[i, 1 + kind], qkv_v.at[0:rows, pl.ds(kind * width, width)]) for kind in range(3)]
        in_pb = cp.start(pb.at[i], pb_v)
        in_b = cp.start(sa.at[i, 4], b_v)
        in_x = cp.start(sa.at[i, 0], x_v)
        qkv_v[rows:, :] = jnp.zeros((keys - rows, 3 * width), BF)
        vg_v[7:8, :] = jnp.zeros((1, width), F32)
        gin_v[...] = g_ref[...]
        scaled = gin_v[...].astype(F32) * vecf_ref[2:3, :]
        e_v[...] = scaled.astype(BF)
        vgf_v[3:4, :] = rows_sum(scaled)
        in_gp.wait()
        e = e_v[...]
        block = 256
        for j in range(hidden // block):
            row, at = divmod(j * block, width)
            cols = slice(j * block, (j + 1) * block)
            dh = dot_nt(e, w2_ref[cols, :]) * gp_v[:, cols].astype(F32)
            dh_v[:, cols] = dh.astype(BF)
            vgf_v[4 + row : 5 + row, at : at + block] = rows_sum(dh)
        in_bf.wait()
        in_xf.wait()
        vgf_v[2:3, :] = rows_sum(gin_v[...].astype(F32) * bf_v[...].astype(F32))
        da = dot_nt(dh_v[...], w1_ref[...])
        xhat, rstd = norm_stats(xf_v[...].astype(F32))
        vgf_v[0:1, :] = rows_sum(da * xhat)
        vgf_v[1:2, :] = rows_sum(da)
        cp.store(vgf_v, vgf.at[i])
        dx_v[...] = norm_back(gin_v[...].astype(F32), da, xhat, rstd, vecf_ref[0:1, :]).astype(BF)
        cp.store(dx_v, out_x.at[1 - flags[1], i])

        scaled = dx_v[...].astype(F32) * vec_ref[2:3, :]
        ea_v[...] = scaled.astype(BF)
        vg_v[3:4, :] = rows_sum(scaled)
        dc_v[...] = dot_nt(ea_v[...], wa_ref[:, 3 * width :]).astype(BF)
        for copy in ins:
            copy.wait()
        in_pb.wait()
        factor = HD ** (-0.5)
        plain = head_masks(1.0)

        def some_heads(n):
            for pair in range(3):
                j = n * 3 + pair
                cols = cols_at(j, 128)
                q = qkv_v[0:rows, cols_at(j, 128)]
                k = qkv_v[:, cols_at(j, 128, width)]
                u = qkv_v[:, cols_at(j, 128, 2 * width)]
                dc = dc_v[:, cols]
                dcs = jnp.concatenate([dc * plain[0], dc * plain[1]], 0)
                probs = pb_v[pl.ds(2 * j, 2)].reshape(2 * rows, keys)
                dp = dot_nt(dcs, u)
                pf = probs.astype(F32)
                wp = pf * dp
                ds = wp - pf * jnp.sum(wp, -1, keepdims=True)
                dlog = (ds * factor).astype(BF)
                dl_v[pl.ds(2 * j, 2)] = dlog.reshape(2, rows, keys)
                du_t = dot_tn(probs, dcs)
                dq_t = dot(
                    jnp.concatenate([dlog[:rows], dlog[rows:]], 1),
                    jnp.concatenate([k * plain[0], k * plain[1]], 0),
                )
                dk_t = dot_tn(dlog, jnp.concatenate([q * plain[0], q * plain[1]], 0))
                dq_v[:, cols_at(j, 128)] = dq_t.astype(BF)
                dq_v[:, cols_at(j, 128, width)] = dk_t[0:rows].astype(BF)
                dq_v[:, cols_at(j, 128, 2 * width)] = du_t[0:rows].astype(BF)
                vg_v[4:5, cols] = rows_sum(dq_t)
                vg_v[5:6, cols] = rows_sum(du_t)

        loop(heads // 2 // 3, some_heads)
        cp.store(dl_v, dl.at[i])
        in_b.wait()
        in_x.wait()
        vg_v[2:3, :] = rows_sum(dx_v[...].astype(F32) * b_v[...].astype(F32))
        da = dot_nt(dq_v[...], wa_ref[:, 0 : 3 * width])
        xhat, rstd = norm_stats(x_v[...].astype(F32))
        dx = norm_back(dx_v[...].astype(F32), da, xhat, rstd, vec_ref[0:1, :])
        send[...] = dx.astype(BF)
        hidden_rows = hide_ref[i] > 0.0
        dx0_v[...] = jnp.where(hidden_rows, 0.0, dx).astype(BF)
        vg_v[6:7, :] = rows_sum(jnp.where(hidden_rows, dx, 0.0))
        cp.store(dx0_v, out_x.at[flags[1], i])
        vg_v[0:1, :] = rows_sum(da * xhat)
        vg_v[1:2, :] = rows_sum(da)
        cp.store(vg_v, vga.at[i])
        cp.finish()


def weight_parts(ups, refs_in, sents, owns, scratch):
    flags, g_all, dh_all, a2, ef, a1, ctx, dq, ea = refs_in
    sent_v, own_v, sems = scratch
    width = a2.shape[2]
    chunks, tall = own_v.shape[1], a2.shape[2] // own_v.shape[1]
    part = tall // 2
    cp = Copies(sems)
    core, at = flags[0], flags[1]
    low = core == 0
    cuts = 1
    block, group = width // cuts, chunks // cuts
    rows = a2.shape[0] * a2.shape[1]

    def product(left, right, first_col, second_col, put):
        rhs = right[:, :, second_col : second_col + width].reshape(rows, width)

        for k in range(cuts):
            start = first_col + k * block
            lhs = left[:, :, start : start + block].reshape(rows, block)
            put(pl.ds(k * group, group), dot_tn(lhs, rhs).astype(BF).reshape(group, tall, width))

    def share(turn, s, which, target):
        def put(group, value):
            target[turn % 2, group, 0:tall] = value

        @pl.when(core == which)
        def _():
            product(a2, dh_all, 0, s * width, put)

        @pl.when(core != which)
        def _():
            product(g_all, ef, s * width, 0, put)

    def put_both(turn, group, value):
        sent_v[turn % 2, group, tall:] = jnp.where(low, value[:, part:], value[:, :part])
        own_v[turn % 2, group, tall:] = jnp.where(low, value[:, :part], value[:, part:])

    def store(turn, s, source, target):
        for chunk in range(chunks):
            slot = (at - chunk if ups[s] else chunk - at) & (chunks - 1)
            cp.store(source.at[turn % 2, chunk], target.at[slot])

    for turn, s in enumerate((0, 2, 1, 3)):
        if turn >= 2:
            for copy in cp.out[: 2 * chunks]:
                copy.wait()
            cp.out = cp.out[2 * chunks :]
        if s < 3:
            product(a1, dq, 0, s * width, partial(put_both, turn))
        else:
            product(ctx, ea, 0, 0, partial(put_both, turn))
        share(turn, s, 1, sent_v)
        store(turn, s, sent_v, sents[s])
        share(turn, s, 0, own_v)
        store(turn, s, own_v, owns[s])
    cp.finish()


def join_images(refs_in, out, scratch):
    flags, pair_ref, got_ref = refs_in
    keep_ref = pair_ref.at[0]
    all_v, sems = scratch
    half = got_ref.shape[0]
    cp = Copies(sems)
    low = flags[0] == 0
    copies = [
        cp.choose(low, keep_ref, got_ref, all_v.at[0:half]),
        cp.choose(low, got_ref, keep_ref, all_v.at[half : 2 * half]),
    ]
    for copy in copies:
        copy.wait()
    length, size = out.shape[0], 16
    for at in range(0, length, size):
        n = min(size, length - at)
        block = jnp.swapaxes(all_v[:, at : at + size, :].astype(F32), 0, 1)
        out[at : at + n] = block[:n].astype(out.dtype)


def small_sums(grid, flags, dl, vga, vgf, mine, theirs, flat_v, dl_v, sems):
    table_fold(grid, dl, flat_v, dl_v, sems)
    heads = flat_v.shape[0]
    low = flags[0] == 0
    table = flat_v[...]
    rows_a, rows_f = vga[0], vgf[0]
    for i in range(1, vga.shape[0]):
        rows_a, rows_f = rows_a + vga[i], rows_f + vgf[i]
    for out, here in ((mine, low), (theirs, jnp.logical_not(low))):
        out[...] = jnp.zeros(out.shape, F32)
        out[8 : 8 + heads, :] = jnp.where(here, table, 0.0)
        out[0:8, :] = jnp.where(here, rows_a, rows_f)


def table_fold(grid, dl, out, dl_v, sems):
    images, heads, rows, keys = dl.shape
    patches, side = grid * grid, 2 * grid - 1
    wide = -(-(side * grid) // 128) * 128 + 128
    copies = []
    for h in range(heads):
        copy = pltpu.make_async_copy(dl.at[:, h], dl_v.at[h], sems.at[h])
        copy.start()
        copies.append(copy)
    lane = lax.broadcasted_iota(jnp.int32, (1, keys), 1)
    narrow = lax.broadcasted_iota(jnp.int32, (1, 256), 1)
    last = lax.broadcasted_iota(jnp.int32, (1, out.shape[1]), 1)
    for h in range(heads):
        copies[h].wait()
        total = dl_v[h, 0].astype(F32)
        for i in range(1, images):
            total = total + dl_v[h, i].astype(F32)
        block = jnp.where(lane > 0, total, 0.0)
        sums = None
        for r in range(grid):
            part = block[1 + r * grid : 1 + (r + 1) * grid]
            part = jnp.concatenate([part, jnp.zeros((grid, wide - keys), F32)], 1)
            part = pltpu.roll(part, (grid * (grid - 1 - r) - 1) % wide, 1)
            sums = part if sums is None else sums + part
        tiles = [jnp.zeros((grid, 128), F32) for _ in range(out.shape[1] // 128 + 1)]
        for a in range(side):
            at, to = a * side // 128, a * grid // 128 * 128
            start = a * grid - to
            inside = (narrow >= start) & (narrow < start + grid)
            window = jnp.where(inside, sums[:, to : to + 256], 0.0)
            turned = pltpu.roll(window, (a * side + grid - 1 - at * 128 - start) % 256, 1)
            tiles[at] = tiles[at] + turned[:, :128]
            tiles[at + 1] = tiles[at + 1] + turned[:, 128:]
        slid = jnp.concatenate(tiles[:-1], 1)
        flat = slid[0:1]
        for c in range(1, grid):
            flat = flat + pltpu.roll(slid[c : c + 1], out.shape[1] - c, 1)
        upper = jnp.sum(jnp.where(lane > 0, total[0:1], 0.0), 1, keepdims=True)
        left = jnp.sum(total[1 : 1 + patches, 0:1], 0, keepdims=True)
        for k, value in enumerate((upper, left, total[0:1, 0:1])):
            flat = jnp.where(last == side * side + k, value, flat)
        out[h : h + 1, :] = flat


def turn_chunks(refs_in, refs_out):
    flags, held, got = refs_in[0], refs_in[1:5], refs_in[5]
    tall = refs_out[0].shape[1]
    part = tall // 2
    low = flags[0] == 0
    for s in range(4):
        a, b = refs_out[s // 2], refs_out[2 + s // 2]
        k = s % 2
        first = got[s, 0:tall]
        b[k] = first
        a[k, 0:part] = jnp.where(low, held[s][tall:], held[s][0:part])
        a[k, part:] = jnp.where(low, got[s, tall:], held[s][part:tall])


def place_sums(refs_in, refs_out, scratch):
    flags, a_up, a_down, b_up, b_down = refs_in
    gw, gd = refs_out
    gw_v, gd_v, sems = scratch
    blocks, tall, width = gd_v.shape
    low = flags[0] == 0
    cp = Copies(sems)
    for way, (a_ref, b_ref) in enumerate(((a_up, b_up), (a_down, b_down))):
        row = pl.multiple_of(flags[1 + way] * tall, tall)
        for k in range(blocks // 2):
            s = way * (blocks // 2) + k
            a = a_ref[k].astype(F32)
            gw_v[s] = jnp.where(low, a, b_ref[k].astype(F32))
            gd_v[s] = jnp.where(low, 0.0, a)
            cp.store(gw_v.at[s], gw.at[pl.ds(row, tall), pl.ds(s * width, width)])
            cp.store(gd_v.at[s], gd.at[pl.ds(pl.multiple_of(s * width + row, tall), tall)])
    cp.finish()


def bias_fill(grid, tail, flipped, out):
    heads, rows, keys = out.shape
    patches, side = grid * grid, 2 * grid - 1
    wide = -(-(side * grid) // 128) * 128
    high = -(-grid // 8) * 8
    lane = lax.broadcasted_iota(jnp.int32, (1, keys), 1)
    narrow = lax.broadcasted_iota(jnp.int32, (1, 128), 1)
    for h in range(heads):
        corner, upper, left = tail[h, 2], tail[h, 0], tail[h, 1]
        out[h, patches + 1 :, :] = jnp.where(
            lax.broadcasted_iota(jnp.int32, (rows - patches - 1, keys), 1) <= patches, 0.0, -1e30
        )
        out[h, 0:1, :] = jnp.where(lane == 0, corner, jnp.where(lane <= patches, upper, -1e30))
        slid = jnp.broadcast_to(flipped[h : h + 1, :], (high, flipped.shape[1]))
        slid = pltpu.roll(slid, 0, 1, stride=1, stride_axis=0)
        tiles = [jnp.zeros((high, 128), F32) for _ in range(wide // 128)]
        for a in range(side):
            at, to = a * side // 128 * 128, a * grid // 128
            start = a * grid - to * 128
            turned = pltpu.roll(slid[:, at : at + 256], (start - (a * side + grid - 1 - at)) % 256, 1)
            for k in range(2):
                if 128 * k < start + grid and start < 128 * (k + 1):
                    inside = (narrow >= start - 128 * k) & (narrow < start + grid - 128 * k)
                    tiles[to + k] = jnp.where(inside, turned[:, 128 * k : 128 * (k + 1)], tiles[to + k])
        block = jnp.concatenate(tiles, 1)
        for r in range(grid):
            turned = pltpu.roll(block, (1 - grid * (grid - 1 - r)) % wide, 1)[0:grid, 0:keys]
            turned = jnp.where(lane == 0, left, jnp.where(lane <= patches, turned, -1e30))
            out[h, 1 + r * grid : 1 + (r + 1) * grid, :] = turned


def run(body, i, name, ins, specs, state, shapes, extra, scratch, sems, flops, moved):
    fresh = state is None
    ins = [in_hbm(v) if spec is ANY else v for v, spec in zip(ins, specs)]
    n_in, n_state, n_extra = len(ins), len(shapes), len(extra)
    given = 0 if fresh else n_state

    def kernel(*refs):
        refs_in = refs[:n_in]
        outs = refs[n_in + given : n_in + given + n_state]
        more = refs[n_in + given + n_state : n_in + given + n_state + n_extra]
        body(i, refs_in, outs, more, refs[n_in + given + n_state + n_extra :])

    made = pl.pallas_call(
        kernel,
        out_shape=tuple(shapes) + tuple(extra),
        in_specs=list(specs) + [ANY] * given,
        out_specs=tuple(VMEM if in_vmem(v) else ANY for v in [*shapes, *extra]),
        scratch_shapes=[pltpu.VMEM(s.shape, s.dtype) for s in scratch] + [pltpu.SemaphoreType.DMA((sems,))],
        input_output_aliases={} if fresh else {n_in + k: k for k in range(n_state)},
        compiler_params=pltpu.CompilerParams(vmem_limit_bytes=16 * 2**20),
        cost_estimate=pl.CostEstimate(flops=flops, bytes_accessed=moved, transcendentals=0),
        name=name,
    )(*ins, *([] if fresh else state))
    return list(made[:n_state]), list(made[n_state:])


def in_vmem(shape):
    return shape.memory_space == pltpu.VMEM


def pinned(block):
    return pltpu.with_memory_space_constraint(block, pltpu.VMEM)


def in_hbm(block):
    return pltpu.with_memory_space_constraint(block, pltpu.HBM)


def far(shape, dtype=BF):
    return pltpu.HBM(shape, dtype)


def sd(shape, dtype=BF):
    return jax.ShapeDtypeStruct(shape, dtype)


class Kernels:
    def __init__(self, images, rows, keys, width, hidden, heads):
        self.n, self.r, self.k, self.d, self.f, self.h = images, rows, keys, width, hidden, heads

    def forward(self, i, flags, x, vec_a, vec_f, weights, bias, state):
        n, r, k, d, f, h = self.n, self.r, self.k, self.d, self.f, self.h
        narrow, wide = far((n, r, d)), far((n, r, f))
        held = pltpu.VMEM((n, r, d), BF)
        shapes = [far((n, 5, r, d)), held, held, narrow, far((n, h, r, k)), pltpu.VMEM((n, r, f), BF), held, wide, narrow, far((2, n, r, d))]
        row, high = sd((r, d)), sd((r, f))
        scratch = [row, sd((k, 3 * d)), sd((h, r, k)), row, row, high, row, row]
        ins, specs = [flags, pinned(x), vec_a, vec_f, pinned(bias)], [SMEM] + [VMEM] * 4
        extra = [pltpu.VMEM((r, d), BF)]
        if len(weights) > 3:
            ins, specs = ins + list(weights), specs + [ANY] * 4
            extra += [pltpu.VMEM((d, f), BF), pltpu.VMEM((d, f), BF), pltpu.VMEM((f, d), BF)]
        else:
            ins, specs = ins + [pinned(w) for w in weights], specs + [VMEM] * 3
        flops = 2 * r * d * 4 * d + 4 * h * r * k * HD + 4 * r * d * f
        return run(forward_image, i, "forward_image", ins, specs, state, shapes, extra, scratch, 20, flops, 12000000)

    def backward(self, i, flags, g, vec_a, vec_f, weights, hide, kept, state):
        n, r, k, d, f, h = self.n, self.r, self.k, self.d, self.f, self.h
        narrow = far((n, r, d))
        sums = far((n, 8, d), F32)
        held = pltpu.VMEM((n, r, d), BF)
        shapes = [pltpu.VMEM((n, r, f), BF), held, sums, held, pltpu.VMEM((n, r, 3 * d), BF), far((n, h, r, k)), far((2, n, r, d)), sums]
        row, high, pairs, vec = sd((r, d)), sd((r, f)), sd((h, r, k)), sd((8, d), F32)
        scratch = [row, high, row, row, sd((k, 3 * d)), pairs, row, row, row, vec, row, pairs, row, vec]
        sa, a1, ctx, y1, pb, g_all, a2, gp, b2 = kept[:9]
        ins = [flags, pinned(g), vec_a, vec_f, *[pinned(w) for w in weights], hide, sa, pb, y1, gp, b2]
        flops = 2 * r * d * 4 * d + 8 * h * r * k * HD + 4 * r * d * f
        return run(backward_image, i, "backward_image", ins, [SMEM] + [VMEM] * 7 + [ANY] * 5, state, shapes, [pltpu.VMEM((r, d), BF)], scratch, 24, flops, 12000000)

    def parts(self, ups, flags, blocks, chunks):
        n, r, d = self.n, self.r, self.d
        tall = d // chunks
        both = (chunks, tall + tall // 2, d)
        made = pl.pallas_call(
            lambda *refs: weight_parts(ups, refs[:9], refs[9:13], refs[13:17], refs[17:]),
            out_shape=(far(both),) * 8,
            in_specs=[SMEM] + [VMEM] * 8,
            out_specs=(ANY,) * 8,
            scratch_shapes=[pltpu.VMEM((2, *both), BF)] * 2 + [pltpu.SemaphoreType.DMA((8 * chunks,))],
            compiler_params=pltpu.CompilerParams(vmem_limit_bytes=16 * 2**20),
            cost_estimate=pl.CostEstimate(flops=24 * n * r * d * d, bytes_accessed=14000000, transcendentals=0),
            name="weight_parts",
        )(flags, *[pinned(v) for v in blocks])
        return made[:4], made[4:]

    def join(self, flags, pair, got, length, dtype):
        n, r, d = got.shape
        return pl.pallas_call(
            lambda *refs: join_images(refs[:3], refs[3], refs[4:]),
            out_shape=sd((length, 2 * n, d), dtype),
            in_specs=[SMEM] + [ANY] * 2,
            out_specs=VMEM,
            scratch_shapes=[pltpu.VMEM((2 * n, r, d), BF), pltpu.SemaphoreType.DMA((2,))],
            compiler_params=pltpu.CompilerParams(vmem_limit_bytes=16 * 2**20),
            cost_estimate=pl.CostEstimate(flops=0, bytes_accessed=10000000, transcendentals=0),
            name="join_images",
        )(flags, in_hbm(pair), in_hbm(got))

    def smalls(self, flags, dl, vga, vgf, grid):
        n, heads, rows, keys = dl.shape
        d = self.d
        out = sd((8 + -(-heads // 8) * 8, d), F32)
        return pl.pallas_call(
            partial(small_sums, grid),
            out_shape=(out, out),
            in_specs=[SMEM, ANY, VMEM, VMEM],
            out_specs=(VMEM, VMEM),
            scratch_shapes=[
                pltpu.VMEM((heads, d), F32),
                pltpu.VMEM((heads, n, rows, keys), BF),
                pltpu.SemaphoreType.DMA((heads,)),
            ],
            compiler_params=pltpu.CompilerParams(vmem_limit_bytes=16 * 2**20),
            cost_estimate=pl.CostEstimate(flops=0, bytes_accessed=12000000, transcendentals=0),
            name="small_sums",
        )(flags, in_hbm(dl), vga, vgf)

    def turn(self, core, held, got):
        d = self.d
        out = sd((2, d // RING, d))
        made = pl.pallas_call(
            lambda *refs: turn_chunks(refs[:6], refs[6:]),
            out_shape=(out,) * 4,
            in_specs=[SMEM] + [VMEM] * 5,
            out_specs=(VMEM,) * 4,
            compiler_params=pltpu.CompilerParams(vmem_limit_bytes=16 * 2**20),
            cost_estimate=pl.CostEstimate(flops=0, bytes_accessed=3000000, transcendentals=0),
            name="turn_chunks",
        )(core.reshape(1), *held, got)
        return list(made[:2]), list(made[2:])

    def place(self, flags, mine, got, state):
        d, f = self.d, self.f
        blocks, tall = 2 * mine[0].shape[0], d // RING
        given = 0 if state is None else 2
        scratch = [pltpu.VMEM((blocks, tall, d), F32)] * 2 + [pltpu.SemaphoreType.DMA((2 * blocks,))]
        return pl.pallas_call(
            lambda *refs: place_sums(refs[:5], refs[5 + given : 7 + given], refs[7 + given :]),
            out_shape=(sd((d, f), F32), sd((f, d), F32)),
            in_specs=[SMEM] + [VMEM] * 4 + [ANY] * given,
            out_specs=(ANY, ANY),
            scratch_shapes=scratch,
            input_output_aliases={5: 0, 6: 1} if given else {},
            compiler_params=pltpu.CompilerParams(vmem_limit_bytes=16 * 2**20),
            cost_estimate=pl.CostEstimate(flops=0, bytes_accessed=4000000, transcendentals=0),
            name="place_sums",
        )(flags, *mine, *got, *(() if state is None else state))

    def bias(self, table, grid):
        heads = table.shape[0]
        side = 2 * grid - 1
        flipped = table[:, : side * side][:, ::-1]
        flipped = jnp.pad(flipped, ((0, 0), (0, -side * side % 128 + 128)))
        return pl.pallas_call(
            partial(bias_fill, grid),
            out_shape=pltpu.VMEM((heads, self.r, self.k), F32),
            in_specs=[SMEM, VMEM],
            out_specs=VMEM,
            compiler_params=pltpu.CompilerParams(vmem_limit_bytes=16 * 2**20),
            name="bias_fill",
        )(table[:, side * side :], flipped)


def swap(block, pairs):
    return lax.ppermute(block, "section", pairs)


def ring_order(n):
    return list(range(0, n, 2)) + list(range(n - 1, 0, -2))


def ring_place():
    n = lax.axis_size("dp")
    place = [0] * n
    for k, device in enumerate(ring_order(n)):
        place[device] = k
    return jnp.array(place, jnp.int32)[lax.axis_index("dp")] if n == RING else jnp.int32(0)


def weight_shares(kern, flags, blocks, both):
    ringed = lax.axis_size("dp") == RING
    sents, owns = kern.parts([ringed, ringed, False, False], flags, blocks, RING)
    got = {s: swap(sents[s], both) for s in (0, 2, 1, 3)}
    return [(owns[s], got[s]) for s in range(4)]


def weight_sums(kern, locals_, at, carry, early, tasks, low, core, both, to_low, to_high, sections):
    axis = "dp"
    n = lax.axis_size(axis)
    ringed = n == RING
    chunks = RING
    order = ring_order(n)
    tall = kern.d // chunks
    if not ringed:
        sums = [lax.psum((own.astype(F32) + got.astype(F32)).astype(BF), axis) for own, got in locals_]
        first = jnp.stack([v[:, :tall] for v in sums])
        second = jnp.stack([v[:, tall:] for v in sums])
        got_first, got_second = swap(first, to_high), swap(second, to_low)
        kept = jnp.concatenate([second, got_second], 2)
        columns = jnp.where(low, kept, got_first).transpose(1, 2, 0, 3)
        grad_weight = columns.reshape(kern.d, kern.f).astype(F32)
        grad_down = jnp.where(low, 0.0, first.astype(F32)).reshape(kern.f, kern.d)
        for task in [*early.values(), *tasks.values()]:
            carry, waiting = task(carry)
            if waiting is not None:
                carry = {**carry, **waiting}
        return grad_weight, grad_down, carry

    route = {w: [(order[k], order[(k + w) % n]) for k in range(n)] for w in (1, -1)}
    upper = {
        w: [(s * n + p, s * n + q) for s in range(1, sections, 2) for p, q in route[w]] for w in (1, -1)
    }
    held = [None] * 4
    waiting = None
    for k in range(n):
        if k in early:
            if waiting is not None:
                carry = {**carry, **waiting}
            if held[3] is not None:
                held[3], carry = lax.optimization_barrier((held[3], carry))
            carry, waiting = early[k](carry)
        for s in (0, 2, 1, 3):
            own, other = locals_[s]
            total = own[k].astype(F32) + other[k].astype(F32)
            if k > 0:
                total = total + lax.ppermute(held[s], axis, route[1 if s < 2 else -1]).astype(F32)
            held[s] = total.astype(BF)
    a, b = kern.turn(core, held, swap(jnp.stack(held), both))
    a, b, carry = lax.optimization_barrier((a, b, carry))
    state, waiting = None, None
    for k in range(n):
        index = jnp.stack([core, (at + 1 - k) & (n - 1), (at - 1 + k) & (n - 1)])
        if k < n - 1:
            if state is not None:
                a[0], state, carry = lax.optimization_barrier((a[0], state, carry))
            next_a = [lax.ppermute(v, axis, route[w]) for v, w in zip(a, (1, -1))]
            next_b = [lax.ppermute(v, ("section", axis), upper[w]) for v, w in zip(b, (1, -1))]
        if k in tasks:
            carry, waiting = tasks[k](carry)
        state = kern.place(index, a, b, state)
        if k < n - 1:
            a, b = next_a, next_b
    return (*state, carry)


def on_device(embeds, mask, cotangent, section_weight, down_weight, section_vectors, rel_table):
    sections = lax.axis_size("section")
    now = lax.axis_index("section")
    core, stage = now % 2, now // 2
    images, length, width = embeds.shape
    half = images // 2
    hidden = section_weight.shape[2]
    heads = rel_table.shape[1]
    rows, keys = -(-length // 16) * 16, -(-length // 128) * 128
    grid = math.isqrt(length - 1)
    both = [(s, s ^ 1) for s in range(sections)]
    to_low = [(s, s - 1) for s in range(1, sections, 2)]
    to_high = [(s, s + 1) for s in range(0, sections, 2)]
    onward = [(s, s + 2) for s in range(sections - 2)]
    back = [(s + 2, s) for s in range(sections - 2)]
    low = core == 0

    own_w, own_d, own_v, own_t = section_weight[0], down_weight[0], section_vectors[0], rel_table[0]
    other_v = swap(own_v, both)
    table = jnp.where(low, own_t, swap(own_t, to_high))
    other_w = swap(own_w, both)
    other_d = swap(own_d, to_low)
    vec_a, vec_f = jnp.where(low, own_v, other_v), jnp.where(low, other_v, own_v)

    def mine_of(block):
        return lax.dynamic_slice_in_dim(block, core * half, half, 0)

    cover = mine_of(mask)[:, :, None] == 1
    start = jnp.where(cover, vec_a[6].astype(BF), mine_of(embeds))
    pad = ((0, 0), (0, rows - length), (0, 0))
    start = jnp.pad(start, pad)
    hide = jnp.pad((cover & (stage == 0)).astype(F32), pad)
    upstream = jnp.pad(mine_of(cotangent), pad)

    kern = Kernels(half, rows, keys, width, hidden, heads)
    at = ring_place()
    flags_p = jnp.stack([core, at])
    table, flags_p, at = lax.optimization_barrier((table, flags_p, at))
    bias = kern.bias(table, grid)
    flags_a = jnp.stack([(stage == 0).astype(jnp.int32), core])
    flags_b = jnp.stack([(stage == 1).astype(jnp.int32), core])
    weights = [own_w, other_w, own_d, other_d]
    kept, grads = None, None

    def forward(i, flags, x):
        nonlocal kept, weights
        kept, made = kern.forward(i, flags, x, vec_a, vec_f, weights, bias, kept)
        weights = made[1:] or weights
        return made[0]

    arrived = [swap(forward(i, flags_a, start), onward) for i in range(half)]
    for i in range(half):
        forward(i, flags_b, arrived[i])

    def backward(i, flags, g):
        nonlocal grads
        grads, (send,) = kern.backward(i, flags, g, vec_a, vec_f, weights, hide, kept, grads)
        return send

    returned = [swap(backward(i, flags_b, upstream), back) for i in range(half)]
    for i in range(half):
        backward(i, flags_a, returned[i])

    sa, a1, ctx, y1, pb, g_all, a2, gp, b2, out_y = kept
    dh_all, ef, vgf, ea, dq, dl, out_x, vga = grads
    blocks = (g_all, dh_all, a2, ef, a1, ctx, dq, ea)
    shares = weight_shares(kern, flags_p, blocks, both)
    own_parts, vga, vgf, dl, out_x, out_y = lax.optimization_barrier(
        ([v[0] for v in shares], vga, vgf, dl, out_x, out_y)
    )
    shares = [(own, other) for own, (_, other) in zip(own_parts, shares)]
    dp = lax.axis_size("dp")

    def rest(carry, *used):
        return {k: v for k, v in carry.items() if k not in used}

    def swap_y(carry):
        return carry, {"got_y": swap(carry["out_y"][1], both)}

    def fold(carry):
        mine, away = kern.smalls(flags_p, carry["dl"], carry["vga"], carry["vgf"], grid)
        traded = {"got": away, "got_y": carry["out_y"][1], "got_x": carry["out_x"][1]}
        return {"small": mine, **rest(carry, "dl", "vga", "vgf")}, {k: swap(v, both) for k, v in traded.items()}

    def doubling(step):
        def task(carry):
            small = carry["small"] + carry["got"]
            got = lax.ppermute(small, "dp", [(d, d ^ step) for d in range(dp)])
            return {**rest(carry, "got"), "small": small}, {"got": got}

        return task

    def join_y(carry):
        joined = kern.join(flags_a[1:], carry["out_y"], carry["got_y"], length, BF)
        return {"y": joined, **rest(carry, "out_y", "got_y")}, None

    def join_x(carry):
        joined = kern.join(flags_a[1:], carry["out_x"], carry["got_x"], length, F32)
        return {"x": joined, **rest(carry, "out_x", "got_x")}, None

    def both_of(one, two):
        def task(carry):
            carry, waiting = one(carry)
            carry, more = two(carry)
            return carry, {**(waiting or {}), **(more or {})}

        return task

    def add_last(carry):
        return {"small": carry["small"] + carry["got"], **rest(carry, "small", "got")}, None

    def finish(carry):
        small = carry["small"]
        flat = small[8 : 8 + heads, : own_t.shape[1]] * (HD ** 0.5)
        pairs = own_t.shape[1] - 3
        table = jnp.concatenate([flat[:, :pairs][:, ::-1], flat[:, pairs:]], 1)
        return {"rows": small[:8], "table": jnp.where(low, table, 0.0), **rest(carry, "small")}, None

    steps = [doubling(1 << k) for k in range(dp.bit_length() - 1)]
    early = dict(enumerate([fold, *steps, add_last]))
    if len(steps) == 3:
        early = dict(zip((0, 2, 4, 6, 7), early.values()))
    tasks = {3: join_y, 4: finish, 6: join_x}
    grad_weight, grad_down, carry = weight_sums(
        kern,
        shares,
        at,
        {"dl": dl, "vga": vga, "vgf": vgf, "out_y": out_y, "out_x": out_x},
        early,
        tasks,
        low,
        core,
        both,
        to_low,
        to_high,
        sections,
    )
    activations = carry["y"].transpose(1, 0, 2)
    input_grads = carry["x"].transpose(1, 0, 2)
    return (
        activations[None],
        input_grads[None],
        grad_weight[None],
        grad_down[None],
        carry["rows"][None],
        carry["table"][None],
    )


def solution(mesh):
    placed = (
        P("dp", None, None),
        P("dp", None),
        P("dp", None, None),
        P("section", None, None),
        P("section", None, None),
        P("section", None, None),
        P("section", None, None),
    )
    return jax.shard_map(
        on_device,
        mesh=mesh,
        in_specs=placed,
        out_specs=(
            P("section", "dp", None, None),
            P("section", "dp", None, None),
            P("section", None, None),
            P("section", None, None),
            P("section", None, None),
            P("section", None, None),
        ),
        check_vma=False,
    )
```
